32 devices in a mesh: dp: 16 (over z, y, x), mp: 2 (over core).
Axes of the slice: x: 2, y: 2, z: 4, core: 2. Of those that a mesh axis runs over, the one named last changes fastest.
Arguments:
- tokens: bfloat16 [32000, 768], P('dp'), may hold values from -6 to 6
- cotangent: bfloat16 [32000, 768], P('dp'), may hold values from -6 to 6
- buckets: int32 [128, 250, 250], P('dp'), may hold values from 0 to 32, as said below
- inward_master: float32 [768, 3, 768], P('dp', None, 'mp'), may hold values from -0.09375 to 0.09375
- inward_first: float32 [768, 3, 768], P('dp', None, 'mp'), may hold values from -4096 to 4096
- inward_second: float32 [768, 3, 768], P('dp', None, 'mp'), may hold values from 512000 to 2048000
- outward_master: float32 [768, 768], P(('mp', 'dp')), may hold values from -2 to 2
- outward_first: float32 [768, 768], P(('mp', 'dp')), may hold values from -128 to 128
- outward_second: float32 [768, 768], P(('mp', 'dp')), may hold values from 544 to 2176
- expand_master: float32 [768, 3072], P('dp', 'mp'), may hold values from -0.21875 to 0.21875
- expand_first: float32 [768, 3072], P('dp', 'mp'), may hold values from -320 to 320
- expand_second: float32 [768, 3072], P('dp', 'mp'), may hold values from 3520 to 14080
- reduce_master: float32 [3072, 768], P(('mp', 'dp')), may hold values from -0.109375 to 0.109375
- reduce_first: float32 [3072, 768], P(('mp', 'dp')), may hold values from -640 to 640
- reduce_second: float32 [3072, 768], P(('mp', 'dp')), may hold values from 13440 to 54400
- gains_master: float32 [2, 768], replicated, may hold values from 0.5 to 1.5
- gains_first: float32 [2, 768], replicated, may hold values from -1536 to 1536
- gains_second: float32 [2, 768], replicated, may hold values from 72000 to 288000
- table_master: float32 [32, 12], P(None, 'mp'), may hold values from -4 to 4
- table_first: float32 [32, 12], P(None, 'mp'), may hold values from -512 to 512
- table_second: float32 [32, 12], P(None, 'mp'), may hold values from 8000 to 32000
Outputs:
- layer_out: bfloat16 [32000, 768], P('dp')
- input_grad: float32 [32000, 768], P('dp')
- inward_new: float32 [768, 3, 768], P('dp', None, 'mp')
- inward_first_new: float32 [768, 3, 768], P('dp', None, 'mp')
- inward_second_new: float32 [768, 3, 768], P('dp', None, 'mp')
- inward_copy: bfloat16 [768, 3, 768], P('dp', None, 'mp')
- outward_new: float32 [768, 768], P(('mp', 'dp'))
- outward_first_new: float32 [768, 768], P(('mp', 'dp'))
- outward_second_new: float32 [768, 768], P(('mp', 'dp'))
- outward_copy: bfloat16 [768, 768], P(('mp', 'dp'))
- expand_new: float32 [768, 3072], P('dp', 'mp')
- expand_first_new: float32 [768, 3072], P('dp', 'mp')
- expand_second_new: float32 [768, 3072], P('dp', 'mp')
- expand_copy: bfloat16 [768, 3072], P('dp', 'mp')
- reduce_new: float32 [3072, 768], P(('mp', 'dp'))
- reduce_first_new: float32 [3072, 768], P(('mp', 'dp'))
- reduce_second_new: float32 [3072, 768], P(('mp', 'dp'))
- reduce_copy: bfloat16 [3072, 768], P(('mp', 'dp'))
- gains_new: float32 [2, 768], replicated
- gains_first_new: float32 [2, 768], replicated
- gains_second_new: float32 [2, 768], replicated
- table_new: float32 [32, 12], P(None, 'mp')
- table_first_new: float32 [32, 12], P(None, 'mp')
- table_second_new: float32 [32, 12], P(None, 'mp')
The draws below stay inside these ranges and needn't reach their ends.
Inputs may be any that keep to these rules, and one draw needn't show every extreme that they name: Entry [p, i, j] is the bidirectional T5 bucket of the distance from query i to key j of passage p (32 buckets, distances up to 128), or 32 where key j lies in passage p's padding; a passage's valid keys come first and number at least 125.
All inputs are finite; a program needn't handle non-finite values.
Results may differ from the reference program's by a relative error of at most 0.014.
The reference program's roundings to bfloat16 on the way count: a program that leaves them out, or rounds other values in their place, can miss the bound.
Values may be sent and summed in bfloat16 or wider, within the bound.
A program may use at most 192 MiB of HBM per device.

```python
import math
import jax
import jax.numpy as jnp
from jax import lax

D = 768
H = 12
DH = 64
FF = 3072
NB = 32
PLEN = 250
STEP = 5
HD = 768
PASSAGES = 128
TOKENS = 32000


max_distance = 128


def draw_buckets(key, part):
    key = jax.random.fold_in(key, 7)
    lengths = jax.random.randint(key, (PASSAGES, 1, 1), PLEN // 2, PLEN + 1)
    positions = jnp.arange(PLEN, dtype=jnp.int32)
    relative = positions[None, :] - positions[:, None]
    half_count = NB // 2
    exact_count = half_count // 2
    distance = jnp.abs(relative)
    far_bucket = jnp.full_like(distance, exact_count)
    for level in range(1, half_count - exact_count):
        threshold = math.ceil(exact_count * (max_distance / exact_count) ** (level / (half_count - exact_count)))
        far_bucket = far_bucket + (distance >= threshold).astype(jnp.int32)
    bucket = jnp.where(relative > 0, half_count, 0) + jnp.where(distance < exact_count, distance, far_bucket)
    inside = positions[None, None, :] < lengths
    return jnp.where(inside, bucket[None], NB).astype(jnp.int32)


def raised(result, own_key, source, target, blocks, factor):
    owner, partner = [(jnp.arange(result.shape[axis_at]) // (result.shape[axis_at] // blocks)).reshape([-1 if axis == axis_at else 1 for axis in range(result.ndim)]) for axis_at in (source, target)]
    chosen = jax.random.permutation(own_key, blocks)[partner]
    strong = (owner == chosen) | (owner == (partner + blocks // 2) % blocks)
    return jnp.where(strong, factor * result, result)


def levels(rng, dims, cuts, least, top_value):
    def one(dim, blocks):
        draws = jax.random.uniform(jax.random.fold_in(jax.random.fold_in(rng, 6), dim), (blocks,), jnp.float32, least / len(cuts), top_value / len(cuts))
        return jnp.repeat(jnp.exp(draws), dims[dim] // blocks).reshape((-1,) + (1,) * (len(dims) - dim - 1))

    loudness = one(*cuts[0])
    for cut in cuts[1:]:
        loudness = loudness * one(*cut)
    return loudness


def noise(stream_key, shape, deviation, limit, split=(), kind=jnp.bfloat16):
    values = jax.random.normal(stream_key, shape, jnp.float32) * deviation
    if len(split) > 0:
        values = levels(stream_key, shape, split, -0.22, 0.18) * values
    return jnp.clip(values, min=-limit, max=limit).astype(kind)


def bell_draw_with(stream_key, extent, deviation, most, cuts, heavy, held_as=jnp.bfloat16):
    drawn = deviation * jax.random.normal(stream_key, extent, jnp.float32)
    if cuts:
        drawn = drawn * levels(stream_key, extent, cuts, -0.22, 0.18)
    return jnp.clip(raised(drawn, jax.random.fold_in(stream_key, 3), *heavy), -most, most).astype(held_as)


def setup_inputs(seed: int = 0) -> dict:
    keys = jax.random.split(jax.random.key(seed), 22)
    tokens = bell_draw_with(keys[0], (TOKENS, D), 1.0, 6.0, ((0, 16),), (0, 1, 16, 2.0))
    cotangent = noise(keys[1], (TOKENS, D), 1.0, 6.0, ((0, 16),))
    buckets = draw_buckets(jax.random.fold_in(keys[21], 71), 0)
    inward_master = noise(keys[3], (D, 3, HD), (6 * D) ** -0.5, 0.09375, ((0, 16), (2, 2)), jnp.float32)
    inward_first = noise(keys[4], (D, 3, HD), (4 * TOKENS ** 0.5), 4096.0, ((0, 16), (2, 2)), jnp.float32)
    inward_second = jnp.clip(jnp.exp(math.log(2048000) - 1.3862944 * jax.random.uniform(keys[5], (D, 3, HD), jnp.float32) ** levels(keys[5], (D, 3, HD), ((0, 16), (2, 2)), -0.2, 0.2)), 512000.0, 2048000)
    outward_master = noise(keys[6], (HD, D), (max(HD // 96, 1)) ** -0.5, 2.0, ((0, 32),), jnp.float32)
    outward_first = noise(keys[7], (HD, D), (0.13 * TOKENS ** 0.5), 128.0, ((0, 32),), jnp.float32)
    outward_second = jnp.clip(jnp.exp(math.log(2176.0) - 1.3862944 * jax.random.uniform(keys[8], (HD, D), jnp.float32) ** levels(keys[8], (HD, D), ((0, 32),), -0.2, 0.2)), 544.0, 2176.0)
    expand_master = noise(keys[9], (D, FF), D ** -0.5, 0.21875, ((0, 16), (1, 2)), jnp.float32)
    expand_first = noise(keys[10], (D, FF), (0.33 * TOKENS ** 0.5), 320.0, ((0, 16), (1, 2)), jnp.float32)
    expand_second = jnp.clip(jnp.exp(math.log(14080.0) - 1.3862944 * jax.random.uniform(keys[11], (D, FF), jnp.float32) ** levels(keys[11], (D, FF), ((0, 16), (1, 2)), -0.2, 0.2)), 3520.0, 14080.0)
    reduce_master = noise(keys[12], (FF, D), FF ** -0.5, 0.109375, ((0, 32),), jnp.float32)
    reduce_first = noise(keys[13], (FF, D), (0.65 * TOKENS ** 0.5), 640.0, ((0, 32),), jnp.float32)
    reduce_second = jnp.clip(jnp.exp(math.log(54400.0) - 1.39812882 * jax.random.uniform(keys[14], (FF, D), jnp.float32) ** levels(keys[14], (FF, D), ((0, 32),), -0.2, 0.2)), 13440.0, 54400.0)
    gains_master = jnp.clip(1.0 + 0.1 * jax.random.normal(keys[15], (2, D), jnp.float32), 0.5, 1.5)
    gains_first = noise(keys[16], (2, D), (1.5 * TOKENS ** 0.5), 1536.0, (), jnp.float32)
    gains_second = jnp.clip(jnp.exp(jax.random.uniform(keys[17], (2, D), jnp.float32, math.log(72000.0), math.log(288000.0))), 72000.0, 288000.0)
    table_master = noise(keys[18], (NB, H), 0.7, 4.0, ((1, 2),), jnp.float32)
    table_first = noise(keys[19], (NB, H), (0.5 * TOKENS ** 0.5), 512.0, ((1, 2),), jnp.float32)
    table_second = jnp.clip(jnp.exp(math.log(32000.0) - 1.3862944 * jax.random.uniform(keys[20], (NB, H), jnp.float32) ** levels(keys[20], (NB, H), ((1, 2),), -0.2, 0.2)), 8000.0, 32000.0)
    return {"tokens": tokens, "cotangent": cotangent, "buckets": buckets, "inward_master": inward_master, "inward_first": inward_first, "inward_second": inward_second, "outward_master": outward_master, "outward_first": outward_first, "outward_second": outward_second, "expand_master": expand_master, "expand_first": expand_first, "expand_second": expand_second, "reduce_master": reduce_master, "reduce_first": reduce_first, "reduce_second": reduce_second, "gains_master": gains_master, "gains_first": gains_first, "gains_second": gains_second, "table_master": table_master, "table_first": table_first, "table_second": table_second}


norm_eps = 1e-06
masked_score = -1000000000.0
beta_first = 0.5
beta_second = 0.5
adam_eps = 1e-08
decay_rate = 0.01
rate_inward = 0.015
rate_outward = 0.3
rate_expand = 0.04
rate_reduce = 0.02
rate_gains = 0.5
rate_table = 0.5
highest = lax.Precision.HIGHEST

@jax.custom_vjp
def low(v):
    return lax.optimization_barrier(v.astype(jnp.bfloat16)).astype(jnp.float32)

@jax.custom_vjp
def low_back(v):
    return v

def low_keep(v):
    return (low(v), None)

def low_pass(kept, grad):
    return (grad,)

def back_keep(v):
    return (v, None)

def back_low(kept, grad):
    return (low(grad),)
low.defvjp(low_keep, low_pass)
low_back.defvjp(back_keep, back_low)

def rms_apply(values, gain_row):
    inv_rms = lax.rsqrt(lax.optimization_barrier(jnp.mean(values * values, axis=-1, keepdims=True)) + norm_eps)
    return values * inv_rms * gain_row

def adamw(weight, first_moment, second, gradient, step_rate):
    new_first = beta_first * first_moment + (1.0 - beta_first) * gradient
    new_second = beta_second * second + (1.0 - beta_second) * gradient * gradient
    first_hat = new_first / (1.0 - beta_first ** STEP)
    second_hat = new_second / (1.0 - beta_second ** STEP)
    new_weight = weight - step_rate * (first_hat / (jnp.sqrt(second_hat) + adam_eps) + decay_rate * weight)
    return (new_weight, new_first, new_second)

def attend(bias_table, queries, key_rows, value_rows, bucket_rows):
    onehot = (bucket_rows[:, :, None] == jnp.arange(NB, dtype=jnp.int32)).astype(bias_table.dtype)
    bias_scores = jnp.einsum('qkb,bh->hqk', onehot, bias_table, precision=highest)
    scores = jnp.einsum('qhd,khd->hqk', queries, key_rows, precision=highest) + bias_scores
    scores = low_back(scores)
    scores = jnp.where((bucket_rows < NB)[None], scores, masked_score)
    attention = low(jax.nn.softmax(scores, axis=-1))
    return jnp.einsum('hqk,khd->qhd', attention, value_rows, precision=highest)

def layer_forward(inputs, params, bucket_group):
    gains, bias_table, inward, outward, expand, reduce_weight = params
    row_count = inputs.shape[0]
    passages = row_count // PLEN
    normed = low(rms_apply(inputs, gains[0]))
    projected = jnp.einsum('td,dch->tch', normed, low(inward), precision=highest)
    projected = low(low_back(projected)).reshape(passages, PLEN, 3, H, DH)
    checked = jax.checkpoint(attend)
    context = lax.map(lambda passage: checked(bias_table, passage[0], passage[1], passage[2], passage[3]), (projected[:, :, 0], projected[:, :, 1], projected[:, :, 2], bucket_group))
    context = low(low_back(context.reshape(row_count, H * DH)))
    attended = low_back(jnp.dot(context, low(outward), precision=highest))
    hidden = inputs + attended
    normed_two = low(rms_apply(hidden, gains[1]))
    expanded = low_back(jnp.dot(normed_two, low(expand), precision=highest))
    activated = low(jax.nn.gelu(expanded))
    reduced = low_back(jnp.dot(activated, low(reduce_weight), precision=highest))
    return hidden + reduced

def reference(tokens, cotangent, buckets, inward_master, inward_first, inward_second, outward_master, outward_first, outward_second, expand_master, expand_first, expand_second, reduce_master, reduce_first, reduce_second, gains_master, gains_first, gains_second, table_master, table_first, table_second):
    passages = tokens.shape[0] // PLEN
    group_size = math.gcd(passages, 16)
    group_count = passages // group_size
    inputs = tokens.astype(jnp.float32).reshape(group_count, group_size * PLEN, D)
    output_grads = cotangent.astype(jnp.float32).reshape(group_count, group_size * PLEN, D)
    bucket_groups = buckets.reshape(group_count, group_size, PLEN, PLEN)
    params = (gains_master, table_master, inward_master, outward_master, expand_master, reduce_master)

    def group_step(totals, group_items):
        group_inputs, group_grads, group_buckets = group_items

        def forward(input_rows, weights):
            return layer_forward(input_rows, weights, group_buckets)
        outputs, backward = jax.vjp(forward, group_inputs, params)
        input_rows_grad, weight_grads = backward(group_grads)
        totals = jax.tree.map(lambda left, right: left + right, totals, weight_grads)
        return (totals, (outputs.astype(jnp.bfloat16), input_rows_grad))
    zeros = jax.tree.map(jnp.zeros_like, params)
    totals, (outputs, input_grads) = lax.scan(group_step, zeros, (inputs, output_grads, bucket_groups))
    gains_grad, table_grad, inward_grad, outward_grad, expand_grad, reduce_grad = totals
    layer_out = outputs.reshape(tokens.shape[0], D)
    input_grad = input_grads.reshape(tokens.shape[0], D)
    inward_new, inward_first_new, inward_second_new = adamw(inward_master, inward_first, inward_second, inward_grad, rate_inward)
    outward_new, outward_first_new, outward_second_new = adamw(outward_master, outward_first, outward_second, outward_grad, rate_outward)
    expand_new, expand_first_new, expand_second_new = adamw(expand_master, expand_first, expand_second, expand_grad, rate_expand)
    reduce_new, reduce_first_new, reduce_second_new = adamw(reduce_master, reduce_first, reduce_second, reduce_grad, rate_reduce)
    gains_new, gains_first_new, gains_second_new = adamw(gains_master, gains_first, gains_second, gains_grad, rate_gains)
    table_new, table_first_new, table_second_new = adamw(table_master, table_first, table_second, table_grad, rate_table)
    return (layer_out, input_grad, inward_new, inward_first_new, inward_second_new, inward_new.astype(jnp.bfloat16), outward_new, outward_first_new, outward_second_new, outward_new.astype(jnp.bfloat16), expand_new, expand_first_new, expand_second_new, expand_new.astype(jnp.bfloat16), reduce_new, reduce_first_new, reduce_second_new, reduce_new.astype(jnp.bfloat16), gains_new, gains_first_new, gains_second_new, table_new, table_first_new, table_second_new)
```

```python
from functools import partial
import math

import jax
import jax.numpy as jnp
import numpy as np
from jax import lax
from jax.experimental import pallas as pl
from jax.experimental.pallas import tpu as pltpu
from jax.sharding import PartitionSpec as P

DH = 64
PLEN = 250
STEP = 5
ROWS = 256
BUCKETS = 32
SPAN = 128

MESH = pl.DeviceIdType.MESH
BF = jnp.bfloat16
F32 = jnp.float32
MIB = 2**20

norm_eps = 1e-06
masked_score = -1000000000.0
beta_first = 0.5
beta_second = 0.5
adam_eps = 1e-08
decay_rate = 0.01
rate_inward = 0.015
rate_outward = 0.3
rate_expand = 0.04
rate_reduce = 0.02
rate_gains = 0.5
rate_table = 0.5


def adamw(weight, first_moment, second, gradient, step_rate):
    new_first = beta_first * first_moment + (1.0 - beta_first) * gradient
    new_second = beta_second * second + (1.0 - beta_second) * gradient * gradient
    first_hat = new_first / (1.0 - beta_first**STEP)
    second_hat = new_second / (1.0 - beta_second**STEP)
    new_weight = weight - step_rate * (
        first_hat / (jnp.sqrt(second_hat) + adam_eps) + decay_rate * weight
    )
    return (new_weight, new_first, new_second)


def distance_onehot():
    span = 2 * ROWS
    relative = np.arange(span)
    relative = np.where(relative < ROWS, relative, relative - span)
    half = BUCKETS // 2
    exact = half // 2
    distance = np.abs(relative)
    far = np.full_like(distance, exact)
    for level in range(1, half - exact):
        far += distance >= math.ceil(exact * (SPAN / exact) ** (level / (half - exact)))
    bucket = np.where(relative > 0, half, 0) + np.where(distance < exact, distance, far)
    return (bucket[:, None] == np.arange(BUCKETS)[None]).astype(np.float32)


def dot(a, b, ca=1, cb=0):
    return lax.dot_general(a, b, (((ca,), (cb,)), ((), ())), preferred_element_type=F32)


def vmem():
    return pl.BlockSpec(memory_space=pltpu.VMEM)


def links(n):
    me = lax.axis_index("dp")
    nz = n // 4
    x, y, z = lax.rem(me, 2), lax.rem(me // 2, 2), me // 4
    column = lax.rem(me, 4)
    x_peer, y_peer = me + 1 - 2 * x, me + 2 - 4 * y
    far_peer = x_peer + 2 - 4 * y
    return me, nz, z, column, x_peer, y_peer, far_peer


def greet(peers):
    barrier = pltpu.get_barrier_semaphore()
    for peer in peers:
        pl.semaphore_signal(barrier, inc=1, device_id=peer, device_id_type=MESH)
    pl.semaphore_wait(barrier, len(peers))


def dp_peers(n):
    me, nz, z, column, x_peer, y_peer, _ = links(n)
    out = [{"dp": x_peer}, {"dp": y_peer}]
    for k in range(1, nz):
        out.append({"dp": lax.rem(z + k, nz) * 4 + column})
    return out


def gather_kernel(n, *refs):
    own = refs[:4]
    outs = refs[4:8]
    odd, wide, ss, rs = refs[8:12]
    full = (outs[0], odd, outs[2], outs[3])
    me, nz, z, column, x_peer, y_peer, far_peer = links(n)

    def block(k, base):
        return lax.rem(z + k, nz) * 4 + lax.rem(base, 4)

    def copy(a, role, k, blk, peer):
        return pltpu.make_async_remote_copy(
            src_ref=full[a].at[blk],
            dst_ref=full[a].at[blk],
            send_sem=ss.at[a, role, k],
            recv_sem=rs.at[a, role, k],
            device_id={"dp": peer},
            device_id_type=MESH,
        )

    greet(dp_peers(n))
    for a in range(4):
        full[a][me] = own[a][...]
    for a in range(4):
        for k in range(1, nz):
            copy(a, 0, k, me, lax.rem(z - k + nz, nz) * 4 + column).start()
        copy(a, 1, 0, me, x_peer).start()
        copy(a, 2, 0, me, y_peer).start()
    for a in range(4):
        for k in range(nz):
            if k > 0:
                blk = block(k, me)
                copy(a, 0, k, blk, x_peer).wait_recv()
                copy(a, 1, k, blk, x_peer).start()
                copy(a, 2, k, blk, y_peer).start()
        for k in range(nz):
            blk = block(k, x_peer)
            copy(a, 1, k, blk, x_peer).wait_recv()
            if k % 2 == 0:
                copy(a, 3, k, blk, y_peer).start()
            blk = block(k, y_peer)
            copy(a, 2, k, blk, y_peer).wait_recv()
            if k % 2 == 1:
                copy(a, 3, k, blk, x_peer).start()
    for a in range(4):
        for k in range(nz):
            copy(a, 3, k, block(k, far_peer), x_peer).wait_recv()
            if k > 0:
                copy(a, 0, k, me, x_peer).wait_send()
            for role in (1, 2, 3):
                copy(a, role, k, me, x_peer).wait_send()
    rows = wide.shape[0] // n
    for d in range(n):
        wide[d * rows : (d + 1) * rows] = odd[d].astype(F32)[:rows]
    outs[1][...] = wide[...].astype(BF)


def gather_weights(n, inward, outward, expand, reduce_):
    rows_o = outward.shape[0]
    padded = jnp.pad(outward, ((0, -rows_o % 16), (0, 0)))
    shards = [inward, padded, expand, reduce_]
    shapes = [(n,) + s.shape for s in shards]
    d = outward.shape[1]
    nz = n // 4
    out_shapes = [jax.ShapeDtypeStruct(s, BF) for s in shapes]
    out_shapes[1] = jax.ShapeDtypeStruct((n * rows_o, d), BF)
    outs = pl.pallas_call(
        partial(gather_kernel, n),
        out_shape=out_shapes,
        in_specs=[vmem()] * 4,
        out_specs=[vmem()] * 4,
        scratch_shapes=[
            pltpu.VMEM(shapes[1], BF),
            pltpu.VMEM((n * rows_o, d), F32),
            pltpu.SemaphoreType.DMA((4, 4, nz)),
            pltpu.SemaphoreType.DMA((4, 4, nz)),
        ],
        compiler_params=pltpu.CompilerParams(
            collective_id=1, has_side_effects=True, vmem_limit_bytes=32 * MIB
        ),
        name="gather_weights",
    )(*shards)
    return [o.reshape(-1, o.shape[-1]) for o in outs]


def scatter_kernel(n, *refs):
    grads = refs[:4]
    small = refs[4]
    outs = refs[5:9]
    small_out = refs[9]
    bufs = refs[10:14]
    small_z, small_xy, ss, rs, ssm, rsm = refs[14:20]
    me, nz, z, column, x_peer, y_peer, far_peer = links(n)

    def block(k, base):
        return lax.rem(z + k, nz) * 4 + lax.rem(base, 4)

    def copy(a, role, k, src, slot, peer):
        return pltpu.make_async_remote_copy(
            src_ref=src,
            dst_ref=bufs[a].at[slot, k],
            send_sem=ss.at[a, role, k],
            recv_sem=rs.at[a, role, k],
            device_id={"dp": peer},
            device_id_type=MESH,
        )

    def small_copy(role, src, dst, peer):
        return pltpu.make_async_remote_copy(
            src_ref=src,
            dst_ref=dst,
            send_sem=ssm.at[role],
            recv_sem=rsm.at[role],
            device_id={"dp": peer},
            device_id_type=MESH,
        )

    def z_peer(k):
        return lax.rem(z + k, nz) * 4 + column

    greet(dp_peers(n))
    small_z[z] = small[...]
    for k in range(1, nz):
        small_copy(k, small, small_z.at[z], z_peer(k)).start()
    for a in range(4):
        for k in range(nz):
            far = grads[a].at[block(k, far_peer)]
            copy(a, 0, k, far, 0, y_peer if k % 2 == 0 else x_peer).start()
        for k in range(nz):
            if k % 2 == 1:
                copy(a, 1, k, grads[a].at[block(k, x_peer)], 2, x_peer).start()
            else:
                copy(a, 2, k, grads[a].at[block(k, y_peer)], 4, y_peer).start()
    for k in range(1, nz):
        small_copy(k, small, small_z.at[lax.rem(z - k + nz, nz)], x_peer).wait()
    total = small_z[0]
    for k in range(1, nz):
        total += small_z[k]
    small_xy[0] = total
    small_copy(0, small_xy.at[0], small_xy.at[1], x_peer).start()
    for a in range(4):
        for k in range(nz):
            copy(a, 0, k, grads[a].at[0], 0, x_peer).wait_recv()
            role, peer, slot = (1, x_peer, 1) if k % 2 == 0 else (2, y_peer, 3)
            mine = grads[a][block(k, peer)].astype(F32) + bufs[a][0, k].astype(F32)
            bufs[a][slot, k] = mine.astype(BF)
            copy(a, role, k, bufs[a].at[slot, k], slot + 1, peer).start()
        if a == 0:
            small_copy(0, small_xy.at[0], small_xy.at[1], x_peer).wait()
            small_xy[2] = small_xy[0] + small_xy[1]
            small_copy(nz, small_xy.at[2], small_xy.at[3], y_peer).start()
    for a in range(4):
        for k in list(range(1, nz)) + [0]:
            copy(a, 1, k, grads[a].at[0], 2, x_peer).wait_recv()
            copy(a, 2, k, grads[a].at[0], 4, y_peer).wait_recv()
            mine = (
                grads[a][block(k, me)].astype(F32)
                + bufs[a][2, k].astype(F32)
                + bufs[a][4, k].astype(F32)
            )
            if k == 0:
                outs[a][...] = mine
            else:
                bufs[a][5, k] = mine.astype(BF)
                copy(a, 3, k, bufs[a].at[5, k], 6, z_peer(k)).start()
    small_copy(nz, small_xy.at[2], small_xy.at[3], y_peer).wait()
    small_out[...] = small_xy[2] + small_xy[3]
    for a in range(4):
        total = outs[a][...]
        for k in range(1, nz):
            copy(a, 3, k, grads[a].at[0], 6, x_peer).wait_recv()
            total += bufs[a][6, k].astype(F32)
        outs[a][...] = total
        for k in range(nz):
            for role in (0, 1, 2):
                copy(a, role, k, grads[a].at[0], 0, x_peer).wait_send()
            if k > 0:
                copy(a, 3, k, grads[a].at[0], 0, x_peer).wait_send()


def scatter_grads(n, grads, small):
    shapes = [g.shape[1:] for g in grads]
    nz = n // 4
    return pl.pallas_call(
        partial(scatter_kernel, n),
        out_shape=[jax.ShapeDtypeStruct(s, F32) for s in shapes]
        + [jax.ShapeDtypeStruct(small.shape, F32)],
        in_specs=[vmem()] * 5,
        out_specs=[vmem()] * 5,
        scratch_shapes=[pltpu.VMEM((7, nz) + s, BF) for s in shapes]
        + [
            pltpu.VMEM((nz,) + small.shape, F32),
            pltpu.VMEM((4,) + small.shape, F32),
            pltpu.SemaphoreType.DMA((4, 4, nz)),
            pltpu.SemaphoreType.DMA((4, 4, nz)),
            pltpu.SemaphoreType.DMA((nz + 1,)),
            pltpu.SemaphoreType.DMA((nz + 1,)),
        ],
        compiler_params=pltpu.CompilerParams(
            collective_id=2, has_side_effects=True, vmem_limit_bytes=48 * MIB
        ),
        name="scatter_grads",
    )(*grads, small)


def partner():
    return {"mp": 1 - lax.axis_index("mp")}


def swap(mine, theirs, ss, rs, p):
    return pltpu.make_async_remote_copy(
        src_ref=mine.at[p],
        dst_ref=theirs.at[p],
        send_sem=ss.at[p],
        recv_sem=rs.at[p],
        device_id=partner(),
        device_id_type=MESH,
    )


def inverse_rms(v):
    return lax.rsqrt(jnp.mean(v * v, axis=-1, keepdims=True) + norm_eps)


def attend_kernel(
    passages, heads, tok, tok_prev, mask, gains, line, wi, wo,
    proj, probs, ctx, hidden, bias, mine, theirs, ss, rs,
):
    p = pl.program_id(0)

    @pl.when(p == 0)
    def _():
        greet([partner()])
        for h in range(heads):
            rows = jnp.broadcast_to(line[h : h + 1, :], (ROWS, 2 * ROWS))
            bias[h] = pltpu.roll(rows, 0, 1, stride=1, stride_axis=0)[:, :ROWS]

    @pl.when(p < passages)
    def _():
        x = tok[0].astype(F32)
        normed = (x * inverse_rms(x) * gains[0:1, :]).astype(BF)
        proj[0] = dot(normed, wi[...]).astype(BF)
        width = heads * DH
        masked = mask[pl.ds(p, 1), :]
        for h in range(heads):
            q = proj[0, :, h * DH : (h + 1) * DH]
            k = proj[0, :, width + h * DH : width + (h + 1) * DH]
            v = proj[0, :, 2 * width + h * DH : 2 * width + (h + 1) * DH]
            s = dot(q, k, 1, 1) + bias[h] + masked
            e = jnp.exp(s - jnp.max(s, axis=-1, keepdims=True))
            a = (e * (1.0 / jnp.sum(e, axis=-1, keepdims=True))).astype(BF)
            probs[0, h] = a
            ctx[0, :, h * DH : (h + 1) * DH] = dot(a, v).astype(BF)
        mine[p] = dot(ctx[0], wo[...]).astype(BF)
        swap(mine, theirs, ss, rs, p).start()

    @pl.when(p > 0)
    def _():
        last = p - 1
        swap(mine, theirs, ss, rs, last).wait()
        hidden[0] = tok_prev[0].astype(F32) + (
            mine[last].astype(F32) + theirs[last].astype(F32)
        )


def this(passages, rank=3):
    return lambda p: (jnp.minimum(p, passages - 1),) + (0,) * (rank - 1)


def prev(rank=3):
    return lambda p: (jnp.maximum(p - 1, 0),) + (0,) * (rank - 1)


def whole(a):
    return pl.BlockSpec(a.shape, lambda p: (0,) * len(a.shape), pipeline_mode=pl.Buffered(1))


def attend(passages, heads, tok, mask, gains, line, wi, wo):
    d = tok.shape[-1]
    width = heads * DH
    now, lag = this(passages), prev()
    return pl.pallas_call(
        partial(attend_kernel, passages, heads),
        grid=(passages + 1,),
        in_specs=[
            pl.BlockSpec((1, ROWS, d), now),
            pl.BlockSpec((1, ROWS, d), lag),
            whole(mask), whole(gains), whole(line), whole(wi), whole(wo),
        ],
        out_specs=[
            pl.BlockSpec((1, ROWS, 3 * width), now),
            pl.BlockSpec((1, heads, ROWS, ROWS), this(passages, 4)),
            pl.BlockSpec((1, ROWS, width), now),
            pl.BlockSpec((1, ROWS, d), lag),
        ],
        out_shape=[
            jax.ShapeDtypeStruct((passages, ROWS, 3 * width), BF),
            jax.ShapeDtypeStruct((passages, heads, ROWS, ROWS), BF),
            jax.ShapeDtypeStruct((passages, ROWS, width), BF),
            jax.ShapeDtypeStruct((passages, ROWS, d), F32),
        ],
        scratch_shapes=[
            pltpu.VMEM((heads, ROWS, ROWS), F32),
            pltpu.VMEM((passages, ROWS, d), BF),
            pltpu.VMEM((passages, ROWS, d), BF),
            pltpu.SemaphoreType.DMA((passages,)),
            pltpu.SemaphoreType.DMA((passages,)),
        ],
        compiler_params=pltpu.CompilerParams(
            collective_id=3, has_side_effects=True, vmem_limit_bytes=48 * MIB
        ),
        name="attend",
    )(tok, tok, mask, gains, line, wi, wo)


gelu_root = math.sqrt(2.0 / math.pi)
gelu_cube = 0.044715


def feed_kernel(
    passages, parts, hid, hid_prev, cot, cot_prev, gains, we, wr,
    layer, hidden_grad, reduce_grad, expand_grad, gain_grad,
    acc_r, acc_e, out_m, out_t, in_m, in_t, ss, rs, ss2, rs2,
):
    p = pl.program_id(0)

    @pl.when(p == 0)
    def _():
        greet([partner()])
        acc_r[...] = jnp.zeros_like(acc_r)
        acc_e[...] = jnp.zeros_like(acc_e)
        gain_grad[...] = jnp.zeros_like(gain_grad)

    @pl.when(p < passages)
    def _():
        h = hid[0]
        normed = (h * inverse_rms(h) * gains[1:2, :]).astype(BF)
        c = cot[0]
        hidden_units = we.shape[1]
        step = hidden_units // parts
        reduced = None
        for i in range(parts):
            cut = slice(i * step, (i + 1) * step)
            u = dot(normed, we[:, cut])
            square = u * u
            t = jnp.tanh(u * (gelu_root + (gelu_root * gelu_cube) * square))
            half = 0.5 * (1.0 + t)
            act = (u * half).astype(BF)
            slope = half + (0.5 * u) * (1.0 - t * t) * (
                gelu_root + (3.0 * gelu_root * gelu_cube) * square
            )
            back = (dot(c, wr[cut, :], 1, 1) * slope).astype(BF)
            acc_r[cut, :] += dot(act, c, 0, 0)
            acc_e[:, cut] += dot(normed, back, 0, 0)
            r_part = dot(act, wr[cut, :])
            n_part = dot(back, we[:, cut], 1, 1)
            reduced = (r_part, n_part) if reduced is None else (reduced[0] + r_part, reduced[1] + n_part)
        out_m[p] = reduced[0].astype(BF)
        swap(out_m, out_t, ss, rs, p).start()
        in_m[p] = reduced[1].astype(BF)
        swap(in_m, in_t, ss2, rs2, p).start()

    @pl.when(p > 0)
    def _():
        last = p - 1
        h = hid_prev[0]
        swap(out_m, out_t, ss, rs, last).wait()
        layer[0] = (h + (out_m[last].astype(F32) + out_t[last].astype(F32))).astype(BF)
        swap(in_m, in_t, ss2, rs2, last).wait()
        grad = in_m[last].astype(F32) + in_t[last].astype(F32)
        r = inverse_rms(h)
        zed = gains[1:2, :] * grad
        hr = h * r
        gain_grad[0:1, :] += jnp.sum(grad * hr, axis=0, keepdims=True)
        inner = jnp.mean(zed * hr, axis=-1, keepdims=True)
        hidden_grad[0] = cot_prev[0].astype(F32) + r * (zed - hr * inner)

    @pl.when(p == passages)
    def _():
        reduce_grad[...] = acc_r[...].astype(BF)
        expand_grad[...] = acc_e[...].astype(BF)


def feed(passages, hid, cot, gains, we, wr):
    d = hid.shape[-1]
    units = we.shape[1]
    now, lag = this(passages), prev()
    row = (1, ROWS, d)
    fixed = lambda p: (0, 0)
    return pl.pallas_call(
        partial(feed_kernel, passages, 3),
        grid=(passages + 1,),
        in_specs=[
            pl.BlockSpec(row, now), pl.BlockSpec(row, lag), pl.BlockSpec(row, now), pl.BlockSpec(row, lag),
            whole(gains), whole(we), whole(wr),
        ],
        out_specs=[
            pl.BlockSpec(row, lag),
            pl.BlockSpec(row, lag),
            pl.BlockSpec((units, d), fixed),
            pl.BlockSpec((d, units), fixed),
            pl.BlockSpec((8, d), fixed),
        ],
        out_shape=[
            jax.ShapeDtypeStruct((passages, ROWS, d), BF),
            jax.ShapeDtypeStruct((passages, ROWS, d), F32),
            jax.ShapeDtypeStruct((units, d), BF),
            jax.ShapeDtypeStruct((d, units), BF),
            jax.ShapeDtypeStruct((8, d), F32),
        ],
        scratch_shapes=[pltpu.VMEM((units, d), F32), pltpu.VMEM((d, units), F32)]
        + [pltpu.VMEM((passages, ROWS, d), BF)] * 4
        + [pltpu.SemaphoreType.DMA((passages,))] * 4,
        compiler_params=pltpu.CompilerParams(
            collective_id=4, has_side_effects=True, vmem_limit_bytes=60 * MIB
        ),
        name="feed",
    )(hid, hid, cot, cot, gains, we, wr)


def attend_back_kernel(
    passages, heads, blocks, hgrad, hgrad_prev, tok, tok_prev, proj, probs, ctx, gains, wi, wo,
    input_grad, inward_grad, outward_grad, gain_grad, lines,
    acc_i, acc_o, acc_s, dproj, in_m, in_t, ss, rs,
):
    p = pl.program_id(0)

    @pl.when(p == 0)
    def _():
        greet([partner()])
        acc_i[...] = jnp.zeros_like(acc_i)
        acc_o[...] = jnp.zeros_like(acc_o)
        acc_s[...] = jnp.zeros_like(acc_s)
        gain_grad[...] = jnp.zeros_like(gain_grad)

    @pl.when(p < passages)
    def _():
        width = heads * DH
        above = hgrad[0].astype(BF)
        acc_o[...] += dot(ctx[0], above, 0, 0)
        dctx = dot(above, wo[...], 1, 1).astype(BF)
        for h in range(heads):
            at = [slice(c * width + h * DH, c * width + (h + 1) * DH) for c in range(3)]
            q, k, v = (proj[0, :, s] for s in at)
            dc = dctx[:, h * DH : (h + 1) * DH]
            a = probs[0, h]
            dproj[:, at[2]] = dot(a, dc, 0, 0).astype(BF)
            dp = dot(dc, v, 1, 1)
            a = a.astype(F32)
            centre = jnp.sum(a * dp, axis=-1, keepdims=True)
            ds = (a * (dp - centre)).astype(BF)
            acc_s[h] += ds.astype(F32)
            dproj[:, at[0]] = dot(ds, k).astype(BF)
            dproj[:, at[1]] = dot(ds, q, 0, 0).astype(BF)
        x = tok[0].astype(F32)
        normed = (x * inverse_rms(x) * gains[0:1, :]).astype(BF)
        acc_i[...] += dot(normed, dproj[...], 0, 0)
        in_m[p] = dot(dproj[...], wi[...], 1, 1).astype(BF)
        swap(in_m, in_t, ss, rs, p).start()

    @pl.when(p > 0)
    def _():
        last = p - 1
        x = tok_prev[0].astype(F32)
        swap(in_m, in_t, ss, rs, last).wait()
        grad = in_m[last].astype(F32) + in_t[last].astype(F32)
        r = inverse_rms(x)
        zed = gains[0:1, :] * grad
        xr = x * r
        gain_grad[0:1, :] += jnp.sum(grad * xr, axis=0, keepdims=True)
        inner = jnp.mean(zed * xr, axis=-1, keepdims=True)
        input_grad[0] = hgrad_prev[0] + r * (zed - xr * inner)

    @pl.when(p == passages)
    def _():
        inward_grad[...] = acc_i[...].astype(BF)
        rows = acc_o.shape[0] // blocks
        pad = outward_grad.shape[1] - rows
        for b in range(blocks):
            part = acc_o[b * rows : (b + 1) * rows, :]
            if pad:
                part = jnp.concatenate([part, jnp.zeros((pad, part.shape[1]), F32)], axis=0)
            outward_grad[b] = part.astype(BF)
        lines[...] = jnp.zeros_like(lines)
        for h in range(heads):
            rows = jnp.concatenate([acc_s[h], jnp.zeros((ROWS, ROWS), F32)], axis=1)
            while rows.shape[0] > 1:
                half = rows.shape[0] // 2
                rows = rows[:half] + pltpu.roll(rows[half:], 2 * ROWS - half, 1)
            lines[h : h + 1, :] = rows


def attend_back(passages, heads, blocks, hgrad, tok, proj, probs, ctx, gains, wi, wo):
    d = hgrad.shape[-1]
    width = heads * DH
    now, lag = this(passages), prev()
    row = (1, ROWS, d)
    fixed = lambda p: (0, 0)
    rows = width // blocks
    rows += -rows % 16
    return pl.pallas_call(
        partial(attend_back_kernel, passages, heads, blocks),
        grid=(passages + 1,),
        in_specs=[
            pl.BlockSpec(row, now), pl.BlockSpec(row, lag), pl.BlockSpec(row, now), pl.BlockSpec(row, lag),
            pl.BlockSpec((1, ROWS, 3 * width), now),
            pl.BlockSpec((1, heads, ROWS, ROWS), this(passages, 4)),
            pl.BlockSpec((1, ROWS, width), now),
            whole(gains), whole(wi), whole(wo),
        ],
        out_specs=[
            pl.BlockSpec(row, lag),
            pl.BlockSpec((d, 3 * width), fixed),
            pl.BlockSpec((blocks, rows, d), lambda p: (0, 0, 0)),
            pl.BlockSpec((8, d), fixed),
            pl.BlockSpec((8, 2 * ROWS), fixed),
        ],
        out_shape=[
            jax.ShapeDtypeStruct((passages, ROWS, d), F32),
            jax.ShapeDtypeStruct((d, 3 * width), BF),
            jax.ShapeDtypeStruct((blocks, rows, d), BF),
            jax.ShapeDtypeStruct((8, d), F32),
            jax.ShapeDtypeStruct((8, 2 * ROWS), F32),
        ],
        scratch_shapes=[
            pltpu.VMEM((d, 3 * width), F32),
            pltpu.VMEM((width, d), F32),
            pltpu.VMEM((heads, ROWS, ROWS), F32),
            pltpu.VMEM((ROWS, 3 * width), BF),
            pltpu.VMEM((passages, ROWS, d), BF),
            pltpu.VMEM((passages, ROWS, d), BF),
            pltpu.SemaphoreType.DMA((passages,)),
            pltpu.SemaphoreType.DMA((passages,)),
        ],
        compiler_params=pltpu.CompilerParams(
            collective_id=5, has_side_effects=True, vmem_limit_bytes=60 * MIB
        ),
        name="attend_back",
    )(hgrad, hgrad, tok, tok, proj, probs, ctx, gains, wi, wo)


def shards(
    n,
    tokens,
    cotangent,
    buckets,
    inward_master,
    inward_first,
    inward_second,
    outward_master,
    outward_first,
    outward_second,
    expand_master,
    expand_first,
    expand_second,
    reduce_master,
    reduce_first,
    reduce_second,
    gains_master,
    gains_first,
    gains_second,
    table_master,
    table_first,
    table_second,
):
    d = tokens.shape[1]
    passages = tokens.shape[0] // PLEN
    heads = inward_master.shape[2] // DH
    width = heads * DH
    inward_rows = inward_master.shape[0]
    inward_flat = inward_master.reshape(inward_rows, 3 * width)
    masters = (inward_flat, outward_master, expand_master, reduce_master)
    direct = (
        n % 4 == 0
        and inward_rows % 16 == 0
        and reduce_master.shape[0] % 16 == 0
        and outward_master.shape[0] % 8 == 0
    )
    if direct:
        wi, wo, we, wr = gather_weights(n, *(w.astype(BF) for w in masters))
    else:
        wi, wo, we, wr = (
            lax.all_gather(w.astype(BF), "dp", axis=0, tiled=True) for w in masters
        )

    def passage_rows(a):
        return jnp.pad(a.reshape(passages, PLEN, d), ((0, 0), (0, ROWS - PLEN), (0, 0)))

    tok, cot = passage_rows(tokens), passage_rows(cotangent)
    mask = jnp.where(buckets[:, 0, :] < BUCKETS, 0.0, masked_score)
    mask = jnp.pad(mask, ((0, -passages % 8), (0, ROWS - PLEN)), constant_values=masked_score)
    onehot = jnp.asarray(distance_onehot())
    line = lax.dot_general(
        table_master, onehot, (((0,), (1,)), ((), ())), precision=lax.Precision.HIGHEST
    )
    line = jnp.pad(line, ((0, -heads % 8), (0, 0)))
    proj, probs, ctx, hidden = attend(passages, heads, tok, mask, gains_master, line, wi, wo)
    layer, hidden_grad, reduce_grad, expand_grad, gain_two = feed(
        passages, hidden, cot, gains_master, we, wr
    )
    blocks = n if direct else 1
    input_grad, inward_grad, outward_grad, gain_one, lines = attend_back(
        passages, heads, blocks, hidden_grad, tok, proj, probs, ctx, gains_master, wi, wo
    )
    table_grad = lax.dot_general(
        lines[:heads], onehot, (((1,), (0,)), ((), ())), precision=lax.Precision.HIGHEST
    )
    if direct:
        flat = jnp.pad(table_grad.reshape(1, -1), ((0, 0), (0, d - table_grad.size)))
        small = jnp.concatenate([gain_one[:1], gain_two[:1], flat, jnp.zeros((5, d), F32)], axis=0)
        cut = [
            g.reshape((n, g.shape[0] // n, g.shape[1]))
            for g in (inward_grad, expand_grad, reduce_grad)
        ]
        sums = scatter_grads(n, [cut[0], outward_grad, cut[1], cut[2]], small)
        inward_sum, outward_sum, expand_sum, reduce_sum, small = sums
        outward_sum = outward_sum[: outward_master.shape[0]]
        gains_sum = small[:2]
        table_sum = small[2, : table_grad.size].reshape(table_grad.shape).T
    else:
        inward_sum, outward_sum, expand_sum, reduce_sum = (
            lax.psum_scatter(g.astype(F32), "dp", scatter_dimension=0, tiled=True)
            for g in (inward_grad, outward_grad[0], expand_grad, reduce_grad)
        )
        gains_sum, table_sum = lax.psum(
            (jnp.concatenate([gain_one[:1], gain_two[:1]]), table_grad.T), "dp"
        )
    inward_sum = inward_sum.reshape(inward_master.shape)

    layer_out = layer[:, :PLEN].reshape(tokens.shape)
    input_grad = input_grad[:, :PLEN].reshape(tokens.shape)
    inward_new, inward_first_new, inward_second_new = adamw(
        inward_master, inward_first, inward_second, inward_sum, rate_inward
    )
    outward_new, outward_first_new, outward_second_new = adamw(
        outward_master, outward_first, outward_second, outward_sum, rate_outward
    )
    expand_new, expand_first_new, expand_second_new = adamw(
        expand_master, expand_first, expand_second, expand_sum, rate_expand
    )
    reduce_new, reduce_first_new, reduce_second_new = adamw(
        reduce_master, reduce_first, reduce_second, reduce_sum, rate_reduce
    )
    gains_new, gains_first_new, gains_second_new = adamw(
        gains_master, gains_first, gains_second, gains_sum, rate_gains
    )
    table_new, table_first_new, table_second_new = adamw(
        table_master, table_first, table_second, table_sum, rate_table
    )
    return (
        layer_out,
        input_grad,
        inward_new,
        inward_first_new,
        inward_second_new,
        inward_new.astype(jnp.bfloat16),
        outward_new,
        outward_first_new,
        outward_second_new,
        outward_new.astype(jnp.bfloat16),
        expand_new,
        expand_first_new,
        expand_second_new,
        expand_new.astype(jnp.bfloat16),
        reduce_new,
        reduce_first_new,
        reduce_second_new,
        reduce_new.astype(jnp.bfloat16),
        gains_new,
        gains_first_new,
        gains_second_new,
        table_new,
        table_first_new,
        table_second_new,
    )


def solution(mesh):
    rows = P("dp", None)
    inward = P("dp", None, "mp")
    tall = P(("mp", "dp"), None)
    wide = P("dp", "mp")
    table = P(None, "mp")
    return jax.shard_map(
        partial(shards, mesh.shape["dp"]),
        mesh=mesh,
        in_specs=(rows, rows, P("dp", None, None))
        + (inward,) * 3
        + (tall,) * 3
        + (wide,) * 3
        + (tall,) * 3
        + (P(),) * 3
        + (table,) * 3,
        out_specs=(rows, rows)
        + (inward,) * 4
        + (tall,) * 4
        + (wide,) * 4
        + (tall,) * 4
        + (P(),) * 3
        + (table,) * 3,
        check_vma=False,
    )
```

```python
from functools import partial
import math

import jax
import jax.numpy as jnp
import numpy as np
from jax import lax
from jax.experimental import pallas as pl
from jax.experimental.pallas import tpu as pltpu
from jax.sharding import PartitionSpec as P

DH = 64
PLEN = 250
STEP = 5
ROWS = 256
BUCKETS = 32
SPAN = 128

MESH = pl.DeviceIdType.MESH
BF = jnp.bfloat16
F32 = jnp.float32
MIB = 2**20

norm_eps = 1e-06
masked_score = -1000000000.0
beta_first = 0.5
beta_second = 0.5
adam_eps = 1e-08
decay_rate = 0.01
rate_inward = 0.015
rate_outward = 0.3
rate_expand = 0.04
rate_reduce = 0.02
rate_gains = 0.5
rate_table = 0.5


def adamw(weight, first_moment, second, gradient, step_rate):
    new_first = beta_first * first_moment + (1.0 - beta_first) * gradient
    new_second = beta_second * second + (1.0 - beta_second) * gradient * gradient
    first_hat = new_first / (1.0 - beta_first**STEP)
    second_hat = new_second / (1.0 - beta_second**STEP)
    new_weight = weight - step_rate * (
        first_hat / (jnp.sqrt(second_hat) + adam_eps) + decay_rate * weight
    )
    return (new_weight, new_first, new_second)


def distance_onehot():
    span = 2 * ROWS
    relative = np.arange(span)
    relative = np.where(relative < ROWS, relative, relative - span)
    half = BUCKETS // 2
    exact = half // 2
    distance = np.abs(relative)
    far = np.full_like(distance, exact)
    for level in range(1, half - exact):
        far += distance >= math.ceil(exact * (SPAN / exact) ** (level / (half - exact)))
    bucket = np.where(relative > 0, half, 0) + np.where(distance < exact, distance, far)
    return (bucket[:, None] == np.arange(BUCKETS)[None]).astype(np.float32)


def dot(a, b, ca=1, cb=0):
    return lax.dot_general(a, b, (((ca,), (cb,)), ((), ())), preferred_element_type=F32)


class Refs:
    pass


def run(kernel, grid, ins, outs, scratch, collective, limit, name):
    names = [i[0] for i in ins] + [o[0] for o in outs] + [s[0] for s in scratch]

    def body(*refs):
        space = Refs()
        for key, ref in zip(names, refs, strict=True):
            setattr(space, key, ref)
        kernel(space)

    results = pl.pallas_call(
        body,
        grid=grid,
        in_specs=[i[2] for i in ins],
        out_specs=[o[3] for o in outs],
        out_shape=[jax.ShapeDtypeStruct(o[1], o[2]) for o in outs],
        scratch_shapes=[s[1] for s in scratch],
        compiler_params=pltpu.CompilerParams(
            collective_id=collective, has_side_effects=True, vmem_limit_bytes=limit * MIB
        ),
        name=name,
    )(*[i[1] for i in ins])
    return dict(zip([o[0] for o in outs], results))


def whole(shape):
    return pl.BlockSpec(shape, lambda p: (0,) * len(shape), pipeline_mode=pl.Buffered(1))


def steps(first, count, shape):
    rest = (0,) * (len(shape) - 1)
    return pl.BlockSpec(shape, lambda p: (jnp.clip(p - first, 0, count - 1),) + rest)


ANY = pl.BlockSpec(memory_space=pl.ANY)


class Links:
    def __init__(self, n):
        me = lax.axis_index("dp")
        self.n, self.nz, self.me = n, n // 4, me
        x, y = lax.rem(me, 2), lax.rem(me // 2, 2)
        self.z, self.column = me // 4, lax.rem(me, 4)
        self.x_peer, self.y_peer = me + 1 - 2 * x, me + 2 - 4 * y
        self.far_peer = self.x_peer + 2 - 4 * y
        self.z_pair = self.z + 1 - 2 * lax.rem(self.z, 2)
        self.pair_peer = self.z_pair * 4 + self.column

    def z_peer(self, k):
        return lax.rem(self.z + k + self.nz, self.nz) * 4 + self.column

    def block(self, k, column_of, z=None):
        return lax.rem((self.z if z is None else z) + k, self.nz) * 4 + lax.rem(column_of, 4)

    def peers(self):
        ids = [self.x_peer, self.y_peer] + [self.z_peer(k) for k in range(1, self.nz)]
        return [{"dp": i} for i in ids]


def greet(peers):
    barrier = pltpu.get_barrier_semaphore()
    for peer in peers:
        pl.semaphore_signal(barrier, inc=1, device_id=peer, device_id_type=MESH)
    pl.semaphore_wait(barrier, len(peers))


def partner():
    return {"mp": 1 - lax.axis_index("mp")}


def cut(ref, blk, rows):
    return ref.at[pl.ds(pl.multiple_of(blk * rows, 16), rows)]


def remote(src, dst, send, recv, peer):
    return pltpu.make_async_remote_copy(
        src_ref=src,
        dst_ref=dst,
        send_sem=send,
        recv_sem=recv,
        device_id=peer,
        device_id_type=MESH,
    )


class Gather:
    def __init__(self, links, full, ss, rs):
        self.l, self.full, self.ss, self.rs = links, full, ss, rs

    def copy(self, a, role, k, blk, peer):
        ref, rows = self.full[a]
        at = cut(ref, blk, rows)
        return remote(at, at, self.ss.at[a, role, k], self.rs.at[a, role, k], {"dp": peer})

    def put(self, a, value, lanes=None):
        ref, rows = self.full[a]
        at = pl.ds(pl.multiple_of(self.l.me * rows, 16), rows)
        if lanes is None:
            ref[at] = value
        else:
            ref[at, lanes] = value

    def own(self, a):
        l = self.l
        for k in range(1, l.nz):
            self.copy(a, 0, k, l.me, l.z_peer(-k)).start()
        self.copy(a, 1, 0, l.me, l.x_peer).start()
        self.copy(a, 2, 0, l.me, l.y_peer).start()

    def along(self, a):
        l = self.l
        for k in range(1, l.nz):
            blk = l.block(k, l.me)
            self.copy(a, 0, k, blk, l.x_peer).wait_recv()
            self.copy(a, 1, k, blk, l.x_peer).start()
            self.copy(a, 2, k, blk, l.y_peer).start()

    def across(self, a):
        l = self.l
        for k in range(0, l.nz, 2):
            role, source, target = (1, l.x_peer, l.y_peer) if k % 4 == 0 else (2, l.y_peer, l.x_peer)
            blk = l.block(k, source)
            self.copy(a, role, k, blk, source).wait_recv()
            self.copy(a, 3, k, blk, target).start()

    def share(self, a):
        l = self.l
        for k in range(0, l.nz, 2):
            blk = l.block(k, l.far_peer)
            self.copy(a, 3, k, blk, l.x_peer).wait_recv()
            self.copy(a, 4, k, blk, l.pair_peer).start()

    def arrived(self, a):
        l = self.l
        for k in range(l.nz):
            if k % 4 != 0:
                self.copy(a, 1, k, l.block(k, l.x_peer), l.x_peer).wait_recv()
            if k % 4 != 2:
                self.copy(a, 2, k, l.block(k, l.y_peer), l.y_peer).wait_recv()
            if k % 2 == 0:
                self.copy(a, 4, k, l.block(k, l.far_peer, l.z_pair), l.pair_peer).wait_recv()

    def sent(self, a):
        l = self.l
        for k in range(l.nz):
            roles = (0,) * (k > 0) + (1, 2) + (3, 4) * (k % 2 == 0)
            for role in roles:
                self.copy(a, role, k, l.me, l.x_peer).wait_send()


class Scatter:
    def __init__(self, links, grads, bufs, ss, rs):
        self.l, self.grads, self.bufs, self.ss, self.rs = links, grads, bufs, ss, rs

    def part(self, a, blk):
        ref, rows = self.grads[a]
        return cut(ref, blk, rows)

    def read(self, a, blk):
        ref, rows = self.grads[a]
        return ref[pl.ds(pl.multiple_of(blk * rows, 16), rows), :].astype(F32)

    def copy(self, a, role, k, src, slot, peer):
        dst = self.bufs[a].at[slot, k]
        return remote(src, dst, self.ss.at[a, role, k], self.rs.at[a, role, k], {"dp": peer})

    def arrive(self, a, role, k, slot):
        self.copy(a, role, k, self.part(a, 0), slot, self.l.x_peer).wait_recv()

    def far(self, a):
        l = self.l
        for k in range(l.nz):
            peer = l.y_peer if k % 2 == 0 else l.x_peer
            self.copy(a, 0, k, self.part(a, l.block(k, l.far_peer)), 0, peer).start()

    def plain(self, a):
        l = self.l
        for k in range(l.nz):
            if k % 2 == 1:
                self.copy(a, 1, k, self.part(a, l.block(k, l.x_peer)), 2, l.x_peer).start()
            else:
                self.copy(a, 2, k, self.part(a, l.block(k, l.y_peer)), 4, l.y_peer).start()

    def near(self, a):
        l = self.l
        for k in range(l.nz):
            self.arrive(a, 0, k, 0)
            role, peer, slot = (1, l.x_peer, 1) if k % 2 == 0 else (2, l.y_peer, 3)
            mine = self.read(a, l.block(k, peer)) + self.bufs[a][0, k].astype(F32)
            self.bufs[a][slot, k] = mine.astype(BF)
            self.copy(a, role, k, self.bufs[a].at[slot, k], slot + 1, peer).start()

    def along(self, a, kept):
        l = self.l
        for k in list(range(1, l.nz)) + [0]:
            self.arrive(a, 1, k, 2)
            self.arrive(a, 2, k, 4)
            mine = (
                self.read(a, l.block(k, l.me))
                + self.bufs[a][2, k].astype(F32)
                + self.bufs[a][4, k].astype(F32)
            )
            if k == 0:
                kept[...] = mine
            else:
                self.bufs[a][5, k] = mine.astype(BF)
                self.copy(a, 3, k, self.bufs[a].at[5, k], 6, l.z_peer(k)).start()

    def total(self, a, kept):
        total = kept[...]
        for k in range(1, self.l.nz):
            self.arrive(a, 3, k, 6)
            total += self.bufs[a][6, k].astype(F32)
        return total

    def sent(self, a):
        for k in range(self.l.nz):
            for role in (0, 1, 2) + (3,) * (k > 0):
                self.copy(a, role, k, self.part(a, 0), 0, self.l.x_peer).wait_send()


class Swap:
    def __init__(self, mine, theirs, ss, rs):
        self.mine, self.theirs, self.ss, self.rs = mine, theirs, ss, rs

    def copy(self, slot):
        return remote(
            self.mine.at[slot], self.theirs.at[slot], self.ss.at[slot], self.rs.at[slot], partner()
        )

    def put(self, p, value):
        self.mine[lax.rem(p, 2)] = value.astype(BF)

    def send(self, p):
        self.copy(lax.rem(p, 2)).start()

    def take(self, p):
        slot = lax.rem(p, 2)
        self.copy(slot).wait()
        return self.mine[slot].astype(F32) + self.theirs[slot].astype(F32)


def swap_scratch(name, d):
    return [
        (name + "_mine", pltpu.VMEM((2, ROWS, d), BF)),
        (name + "_theirs", pltpu.VMEM((2, ROWS, d), BF)),
        (name + "_ss", pltpu.SemaphoreType.DMA((2,))),
        (name + "_rs", pltpu.SemaphoreType.DMA((2,))),
    ]


def swap_of(r, name):
    return Swap(*(getattr(r, name + part) for part in ("_mine", "_theirs", "_ss", "_rs")))


gelu_root = math.sqrt(2.0 / math.pi)
gelu_cube = 0.044715
WINDOW = 272


def inverse_rms(v):
    return lax.rsqrt(jnp.mean(v * v, axis=-1, keepdims=True) + norm_eps)


def window_start(p, total):
    return min(p * PLEN // 16 * 16, total - WINDOW)


def align(source, target, windows, sems, passages):
    total = source.shape[0]

    def fetch(p):
        return pltpu.make_async_copy(
            source.at[pl.ds(window_start(p, total), WINDOW)], windows.at[p % 2], sems.at[p % 2]
        )

    def start():
        fetch(0).start()
        fetch(1).start()

    def move(first, last):
        for p in range(first, last):
            fetch(p).wait()
            off = p * PLEN - window_start(p, total)
            rows = windows[p % 2].astype(F32)[off : off + PLEN]
            pad = jnp.zeros((ROWS - PLEN, rows.shape[1]), F32)
            target[p] = jnp.concatenate([rows, pad], axis=0).astype(BF)
            if p + 2 < passages:
                fetch(p + 2).start()

    return start, move


def forward_kernel(n, passages, heads, direct, parts, r):
    s = pl.program_id(0)
    width = heads * DH
    count = passages
    att, out, back_in = (swap_of(r, name) for name in ("att", "out", "in"))
    if direct:
        links = Links(n)
        full = [
            (r.wi, r.wi.shape[0] // n), (r.wo_wide, r.wo_wide.shape[0] // n),
            (r.we, r.we.shape[0] // n), (r.wr, r.wr.shape[0] // n),
        ]
        gather = Gather(links, full, r.g_ss, r.g_rs)
    tok_start, tok_move = align(r.tokens, r.tok, r.tok_window, r.tok_sem, passages)
    cot_start, cot_move = align(r.cotangent, r.cot, r.cot_window, r.cot_sem, passages)

    def local(src, dst, i):
        return pltpu.make_async_copy(src, dst, r.out_sem.at[i])

    @pl.when(s == 0)
    def _():
        tok_start()
        cot_start()
        if direct:
            for c in range(3):
                gather.put(0, r.own_i[c].astype(BF), slice(c * width, (c + 1) * width))
            rows_o = r.own_o.shape[0]
            pad = jnp.zeros((full[1][1] - rows_o, r.own_o.shape[1]), F32)
            gather.put(1, jnp.concatenate([r.own_o[...], pad], axis=0).astype(BF))
            gather.put(2, r.own_e[...].astype(BF))
            gather.put(3, r.own_r[...].astype(BF))
            greet(links.peers() + [partner()])
            gather.own(0)
            gather.own(1)
        else:
            greet([partner()])
        r.acc_r[...] = jnp.zeros_like(r.acc_r)
        r.acc_e[...] = jnp.zeros_like(r.acc_e)
        r.acc_o[...] = jnp.zeros_like(r.acc_o)
        r.gain_grad[...] = jnp.zeros_like(r.gain_grad)
        tok_move(0, passages // 2)
        if direct:
            gather.along(0)
            gather.own(2)
        tok_move(passages // 2, passages)
        local(r.tok, r.tok_out, 0).start()
        if direct:
            gather.across(0)
        cot_move(0, passages // 2)
        if direct:
            gather.along(1)
            gather.own(3)
            gather.share(0)
        cot_move(passages // 2, passages)
        for h in range(heads):
            rows = jnp.broadcast_to(r.line[h : h + 1, :], (ROWS, 2 * ROWS))
            r.bias[h] = pltpu.roll(rows, 0, 1, stride=1, stride_axis=0)[:, :ROWS]
        if direct:
            gather.across(1)
            gather.arrived(0)

    @pl.when(s < count)
    def _():
        x = r.tok[s].astype(F32)
        normed = (x * inverse_rms(x) * r.gains[0:1, :]).astype(BF)
        r.normed[0] = normed
        r.proj[0] = dot(normed, r.wi[...]).astype(BF)
        masked = r.mask[pl.ds(s, 1), :]
        for h in range(heads):
            q = r.proj[0, :, h * DH : (h + 1) * DH]
            k = r.proj[0, :, width + h * DH : width + (h + 1) * DH]
            v = r.proj[0, :, 2 * width + h * DH : 2 * width + (h + 1) * DH]
            sc = dot(q, k, 1, 1) + r.bias[h] + masked
            e = jnp.exp(sc - jnp.max(sc, axis=-1, keepdims=True))
            a = (e * (1.0 / jnp.sum(e, axis=-1, keepdims=True))).astype(BF)
            r.probs[0, h] = a
            r.ctx[s, :, h * DH : (h + 1) * DH] = dot(a, v).astype(BF)

    if direct:

        @pl.when(s == 0)
        def _():
            gather.share(1)
            gather.arrived(1)
            rows = r.own_o.shape[0]
            padded = full[1][1]
            for d in range(n):
                block = r.wo_wide[d * padded : (d + 1) * padded, :].astype(F32)
                r.wo_f32[d * rows : (d + 1) * rows, :] = block[:rows]
            r.wo[...] = r.wo_f32[...].astype(BF)

        for at, what, a in (
            (1, gather.along, 2), (2, gather.across, 2), (3, gather.share, 2),
            (4, gather.along, 3), (5, gather.across, 3), (6, gather.share, 3),
        ):
            pl.when(s == at)(partial(what, a))

        @pl.when(s == count - 1)
        def _():
            local(r.wi, r.wi_out, 1).start()
            local(r.wo, r.wo_out, 2).start()

    def settle(p):
        r.hidden[p] = r.tok[p].astype(F32) + att.take(p)

    @pl.when(s < count)
    def _():
        att.put(s, dot(r.ctx[s], r.wo[...]))

    @pl.when((s > 0) & (s < count))
    def _():
        settle(s - 1)

    @pl.when(s < count)
    def _():
        att.send(s)

    p = s - count

    @pl.when(s == count)
    def _():
        if direct:
            gather.arrived(2)
            gather.arrived(3)

    @pl.when((s >= count) & (s < 2 * count))
    def _():
        h = r.hidden[p]
        normed = (h * inverse_rms(h) * r.gains[1:2, :]).astype(BF)
        c = r.cot[p]
        step = r.we.shape[1] // parts
        reduced = None
        for i in range(parts):
            at = slice(i * step, (i + 1) * step)
            u = dot(normed, r.we[:, at])
            square = u * u
            t = jnp.tanh(u * (gelu_root + (gelu_root * gelu_cube) * square))
            half = 0.5 * (1.0 + t)
            act = (u * half).astype(BF)
            slope = half + (0.5 * u) * (1.0 - t * t) * (
                gelu_root + (3.0 * gelu_root * gelu_cube) * square
            )
            back = (dot(c, r.wr[at, :], 1, 1) * slope).astype(BF)
            r.acc_r[at, :] += dot(act, c, 0, 0)
            r.acc_e[:, at] += dot(normed, back, 0, 0)
            r_part = dot(act, r.wr[at, :])
            n_part = dot(back, r.we[:, at], 1, 1)
            if reduced is not None:
                r_part, n_part = reduced[0] + r_part, reduced[1] + n_part
            reduced = (r_part, n_part)
        out.put(p, reduced[0])
        back_in.put(p, reduced[1])

    @pl.when(s == count)
    def _():
        settle(count - 1)

    @pl.when(s == 2 * count - 1)
    def _():
        r.reduce_grad[...] = r.acc_r[...].astype(BF)
        r.expand_grad[...] = r.acc_e[...].astype(BF)

    @pl.when(s > count)
    def _():
        last = p - 1
        h = r.hidden[last]
        r.layer[0] = (h + out.take(last)).astype(BF)
        grad = back_in.take(last)
        inv = inverse_rms(h)
        zed = r.gains[1:2, :] * grad
        hr = h * inv
        r.gain_grad[0:1, :] += jnp.sum(grad * hr, axis=0, keepdims=True)
        inner = jnp.mean(zed * hr, axis=-1, keepdims=True)
        hidden_grad = r.cot[last].astype(F32) + inv * (zed - hr * inner)
        r.hidden_grad[0] = hidden_grad
        r.acc_o[...] += dot(r.ctx[last], hidden_grad.astype(BF), 0, 0)

    @pl.when((s >= count) & (s < 2 * count))
    def _():
        out.send(p)
        back_in.send(p)

    @pl.when(s == 2 * count)
    def _():
        rows = r.acc_o.shape[0] // (n if direct else 1)
        padded = rows + -rows % 16
        for b in range(n if direct else 1):
            part = r.acc_o[b * rows : (b + 1) * rows, :]
            if padded > rows:
                part = jnp.concatenate([part, jnp.zeros((padded - rows, part.shape[1]), F32)], axis=0)
            r.outward_grad[b * padded : (b + 1) * padded, :] = part.astype(BF)
        local(r.tok, r.tok_out, 0).wait()
        if direct:
            local(r.wi, r.wi_out, 1).wait()
            local(r.wo, r.wo_out, 2).wait()
            for a in range(4):
                gather.sent(a)


def forward(n, passages, heads, direct, tokens, cotangent, mask, gains, line, weights):
    d = tokens.shape[1]
    width = heads * DH
    one = (1, ROWS, d)
    fixed = lambda p: (0, 0)
    wide = lambda shape: pl.BlockSpec(shape, fixed, pipeline_mode=pl.Buffered(1))
    late, first = passages + 1, 0
    ins = [("tokens", tokens, ANY), ("cotangent", cotangent, ANY)]
    ins += [(k, v, whole(v.shape)) for k, v in (("mask", mask), ("gains", gains), ("line", line))]
    ins += [(k, v, whole(v.shape)) for k, v in weights.items()]
    if direct:
        units = weights["own_r"].shape[0] * n
        padded = weights["own_o"].shape[0]
        padded += -padded % 16
    else:
        units = weights["wr"].shape[0]
    outs = [
        ("proj", (passages, ROWS, 3 * width), BF, steps(first, passages, (1, ROWS, 3 * width))),
        ("probs", (passages, heads, ROWS, ROWS), BF, steps(first, passages, (1, heads, ROWS, ROWS))),
        ("normed", (passages, ROWS, d), BF, steps(first, passages, one)),
        ("tok_out", (passages, ROWS, d), BF, ANY),
        ("layer", (passages, ROWS, d), BF, steps(late, passages, one)),
        ("hidden_grad", (passages, ROWS, d), F32, steps(late, passages, one)),
        ("reduce_grad", (units, d), BF, wide((units, d))),
        ("expand_grad", (d, units), BF, wide((d, units))),
        ("gain_grad", (8, d), F32, wide((8, d))),
    ]
    rows_o = padded * n if direct else width
    outs.append(("outward_grad", (rows_o, d), BF, wide((rows_o, d))))
    scratch = [
        ("tok", pltpu.VMEM((passages, ROWS, d), BF)),
        ("cot", pltpu.VMEM((passages, ROWS, d), BF)),
        ("tok_window", pltpu.VMEM((2, WINDOW, d), BF)),
        ("cot_window", pltpu.VMEM((2, WINDOW, d), BF)),
        ("tok_sem", pltpu.SemaphoreType.DMA((2,))),
        ("cot_sem", pltpu.SemaphoreType.DMA((2,))),
        ("out_sem", pltpu.SemaphoreType.DMA((3,))),
        ("bias", pltpu.VMEM((heads, ROWS, ROWS), F32)),
        ("ctx", pltpu.VMEM((passages, ROWS, width), BF)),
        ("hidden", pltpu.VMEM((passages, ROWS, d), F32)),
        ("acc_r", pltpu.VMEM((units, d), F32)),
        ("acc_e", pltpu.VMEM((d, units), F32)),
        ("acc_o", pltpu.VMEM((width, d), F32)),
    ]
    for name in ("att", "out", "in"):
        scratch += swap_scratch(name, d)
    if direct:
        outs += [("wi_out", (d, 3 * width), BF, ANY), ("wo_out", (width, d), BF, ANY)]
        scratch += [
            ("wi", pltpu.VMEM((d, 3 * width), BF)),
            ("wo", pltpu.VMEM((width, d), BF)),
            ("wo_f32", pltpu.VMEM((width, d), F32)),
            ("wo_wide", pltpu.VMEM((n * padded, d), BF)),
            ("we", pltpu.VMEM((d, units), BF)),
            ("wr", pltpu.VMEM((units, d), BF)),
            ("g_ss", pltpu.SemaphoreType.DMA((4, 5, n // 4))),
            ("g_rs", pltpu.SemaphoreType.DMA((4, 5, n // 4))),
        ]
    kernel = partial(forward_kernel, n, passages, heads, direct, 3)
    return run(kernel, (2 * passages + 1,), ins, outs, scratch, 1, 62, "forward")


def backward_kernel(n, passages, heads, direct, r):
    s = pl.program_id(0)
    width = heads * DH
    swap = swap_of(r, "in")
    if direct:
        links = Links(n)
        names = ("r", "e", "o", "i")
        grads = [(g, g.shape[0] // n) for g in (r.reduce_grad, r.expand_grad, r.outward_grad, r.inward_grad)]
        bufs = [getattr(r, "buf_" + k) for k in names]
        kept = [getattr(r, "kept_" + k) for k in names]
        sums = Scatter(links, grads, bufs, r.s_ss, r.s_rs)

    @pl.when(s == 0)
    def _():
        if direct:
            greet(links.peers() + [partner()])
            for a in range(3):
                sums.far(a)
            for a in range(3):
                sums.plain(a)
        else:
            greet([partner()])
        r.acc_i[...] = jnp.zeros_like(r.acc_i)
        r.acc_s[...] = jnp.zeros_like(r.acc_s)
        r.gain_one[...] = jnp.zeros_like(r.gain_one)

    if direct:
        for at, what, arrays in ((2, "near", (0,)), (3, "near", (1, 2)), (5, "along", (0,)), (6, "along", (1, 2))):

            @pl.when(s == at)
            def _():
                for a in arrays:
                    if what == "near":
                        sums.near(a)
                    else:
                        sums.along(a, kept[a])

    @pl.when(s < passages)
    def _():
        above = r.hgrad[0].astype(BF)
        dctx = dot(above, r.wo[...], 1, 1).astype(BF)
        for h in range(heads):
            at = [slice(c * width + h * DH, c * width + (h + 1) * DH) for c in range(3)]
            q, k, v = (r.proj[0, :, c] for c in at)
            dc = dctx[:, h * DH : (h + 1) * DH]
            a = r.probs[0, h]
            r.dproj[:, at[2]] = dot(a, dc, 0, 0).astype(BF)
            dp = dot(dc, v, 1, 1)
            a = a.astype(F32)
            centre = jnp.sum(a * dp, axis=-1, keepdims=True)
            ds = (a * (dp - centre)).astype(BF)
            r.acc_s[h] += ds.astype(F32)
            r.dproj[:, at[0]] = dot(ds, k).astype(BF)
            r.dproj[:, at[1]] = dot(ds, q, 0, 0).astype(BF)
        r.acc_i[...] += dot(r.normed[0], r.dproj[...], 0, 0)
        swap.put(s, dot(r.dproj[...], r.wi[...], 1, 1))

    @pl.when(s == passages - 1)
    def _():
        r.inward_grad[...] = r.acc_i[...].astype(BF)
        if direct:
            sums.far(3)
            sums.plain(3)

    @pl.when(s > 0)
    def _():
        last = s - 1
        x = r.tok_prev[0].astype(F32)
        grad = swap.take(last)
        inv = inverse_rms(x)
        zed = r.gains[0:1, :] * grad
        xr = x * inv
        r.gain_one[0:1, :] += jnp.sum(grad * xr, axis=0, keepdims=True)
        inner = jnp.mean(zed * xr, axis=-1, keepdims=True)
        r.input_grad[0] = r.hgrad_prev[0] + inv * (zed - xr * inner)

    @pl.when(s < passages)
    def _():
        swap.send(s)

    @pl.when(s == passages)
    def _():
        small = r.small
        small[...] = jnp.zeros_like(small)
        small[0:1, :] = r.gain_one[0:1, :]
        small[1:2, :] = r.gain_two[0:1, :]
        for h in range(heads):
            rows = jnp.concatenate([r.acc_s[h], jnp.zeros((ROWS, ROWS), F32)], axis=1)
            while rows.shape[0] > 1:
                half = rows.shape[0] // 2
                rows = rows[:half] + pltpu.roll(rows[half:], 2 * ROWS - half, 1)
            small[8 + h : 9 + h, : 2 * ROWS] = rows
        if not direct:
            r.small_out[...] = small[...]
            return
        finish(n, heads, links, sums, kept, r)


def finish(n, heads, links, sums, kept, r):
    nz = links.nz
    width = heads * DH
    small, small_z, small_xy = r.small, r.small_z, r.small_xy

    def small_copy(role, src, dst, peer):
        return remote(src, dst, r.m_ss.at[role], r.m_rs.at[role], {"dp": peer})

    def update(key, gradient, rate, index=None):
        pick = (lambda ref: ref[...]) if index is None else (lambda ref: ref[index])
        refs = [getattr(r, key + part) for part in ("_w", "_m", "_v")]
        new = adamw(*(pick(ref) for ref in refs), gradient, rate)
        targets = [getattr(r, key + part) for part in ("_nw", "_nm", "_nv")]
        if hasattr(r, key + "_nc"):
            targets.append(getattr(r, key + "_nc"))
            new = new + (new[0].astype(BF),)
        for target, value in zip(targets, new, strict=True):
            if index is None:
                target[...] = value
            else:
                target[index] = value

    small_z[links.z] = small[...]
    for k in range(1, nz):
        small_copy(k, small, small_z.at[links.z], links.z_peer(k)).start()
    update("r", sums.total(0, kept[0]), rate_reduce)
    sums.near(3)
    for k in range(1, nz):
        small_copy(k, small, small_z.at[lax.rem(links.z - k + nz, nz)], links.x_peer).wait()
    total = small_z[0]
    for k in range(1, nz):
        total += small_z[k]
    small_xy[0] = total
    small_copy(0, small_xy.at[0], small_xy.at[1], links.x_peer).start()
    update("e", sums.total(1, kept[1]), rate_expand)
    update("o", sums.total(2, kept[2])[: r.o_w.shape[0]], rate_outward)
    small_copy(0, small_xy.at[0], small_xy.at[1], links.x_peer).wait()
    small_xy[2] = small_xy[0] + small_xy[1]
    small_copy(nz, small_xy.at[2], small_xy.at[3], links.y_peer).start()
    sums.along(3, kept[3])
    small_copy(nz, small_xy.at[2], small_xy.at[3], links.y_peer).wait()
    total = small_xy[2] + small_xy[3]
    update("g", total[:2], rate_gains)
    table_grad = lax.dot_general(
        r.onehot[...], total[8:, : 2 * ROWS], (((0,), (1,)), ((), ())),
        precision=lax.Precision.HIGHEST, preferred_element_type=F32,
    )
    update("t", table_grad[:, :heads], rate_table)
    inward = sums.total(3, kept[3])
    for c in range(3):
        update("i", inward[:, c * width : (c + 1) * width], rate_inward, c)
    for a in range(4):
        sums.sent(a)


def backward(n, passages, heads, direct, f, gains, wi, wo, onehot, states):
    d = f["normed"].shape[-1]
    width = heads * DH
    one = (1, ROWS, d)
    now = lambda shape: steps(0, passages, shape)
    lag = lambda shape: steps(1, passages, shape)
    hgrad, tok = f["hidden_grad"], f["tok_out"]
    ins = [
        ("hgrad", hgrad, now(one)),
        ("hgrad_prev", hgrad, lag(one)),
        ("tok_prev", tok, lag(one)),
        ("normed", f["normed"], now(one)),
        ("proj", f["proj"], now((1, ROWS, 3 * width))),
        ("probs", f["probs"], now((1, heads, ROWS, ROWS))),
    ]
    fixed = [("gains", gains), ("wi", wi), ("wo", wo), ("gain_two", f["gain_grad"])]
    outs = [("input_grad", (passages, ROWS, d), F32, lag(one))]
    scratch = [
        ("acc_i", pltpu.VMEM((d, 3 * width), F32)),
        ("acc_s", pltpu.VMEM((heads, ROWS, ROWS), F32)),
        ("dproj", pltpu.VMEM((ROWS, 3 * width), BF)),
        ("gain_one", pltpu.VMEM((8, d), F32)),
        ("small", pltpu.VMEM((16, d), F32)),
    ] + swap_scratch("in", d)
    if direct:
        nz = n // 4
        fixed += [("onehot", onehot)]
        fixed += [(k, f[k]) for k in ("reduce_grad", "expand_grad", "outward_grad")]
        for key, (w, m, v) in states.items():
            fixed += [(key + "_w", w), (key + "_m", m), (key + "_v", v)]
            for part in ("_nw", "_nm", "_nv"):
                outs.append((key + part, w.shape, F32, whole(w.shape)))
            if key not in "gt":
                outs.append((key + "_nc", w.shape, BF, whole(w.shape)))
        blocks = {
            "r": (f["reduce_grad"].shape[0] // n, d),
            "e": (d // n, f["expand_grad"].shape[1]),
            "o": (f["outward_grad"].shape[0] // n, d),
            "i": (d // n, 3 * width),
        }
        scratch.append(("inward_grad", pltpu.VMEM((d, 3 * width), BF)))
        for key, shape in blocks.items():
            scratch.append(("buf_" + key, pltpu.VMEM((7, nz) + shape, BF)))
            scratch.append(("kept_" + key, pltpu.VMEM(shape, F32)))
        scratch += [
            ("small_z", pltpu.VMEM((nz, 16, d), F32)),
            ("small_xy", pltpu.VMEM((4, 16, d), F32)),
            ("s_ss", pltpu.SemaphoreType.DMA((4, 4, nz))),
            ("s_rs", pltpu.SemaphoreType.DMA((4, 4, nz))),
            ("m_ss", pltpu.SemaphoreType.DMA((nz + 1,))),
            ("m_rs", pltpu.SemaphoreType.DMA((nz + 1,))),
        ]
    else:
        outs.append(("inward_grad", (d, 3 * width), BF, whole((d, 3 * width))))
        outs.append(("small_out", (16, d), F32, whole((16, d))))
    ins += [(k, v, whole(v.shape)) for k, v in fixed]
    kernel = partial(backward_kernel, n, passages, heads, direct)
    return run(kernel, (passages + 1,), ins, outs, scratch, 2, 62, "backward")


def shards(
    n,
    tokens,
    cotangent,
    buckets,
    inward_master,
    inward_first,
    inward_second,
    outward_master,
    outward_first,
    outward_second,
    expand_master,
    expand_first,
    expand_second,
    reduce_master,
    reduce_first,
    reduce_second,
    gains_master,
    gains_first,
    gains_second,
    table_master,
    table_first,
    table_second,
):
    passages = tokens.shape[0] // PLEN
    heads = inward_master.shape[2] // DH
    width = heads * DH
    states = {
        "i": tuple(a.transpose(1, 0, 2) for a in (inward_master, inward_first, inward_second)),
        "o": (outward_master, outward_first, outward_second),
        "e": (expand_master, expand_first, expand_second),
        "r": (reduce_master, reduce_first, reduce_second),
        "g": (gains_master, gains_first, gains_second),
        "t": (table_master, table_first, table_second),
    }
    direct = (
        n % 8 == 0
        and inward_master.shape[0] % 16 == 0
        and reduce_master.shape[0] % 16 == 0
        and outward_master.shape[0] % 8 == 0
    )
    if direct:
        weights = {"own_" + key: states[key][0] for key in "ioer"}
    else:
        masters = {
            "wi": inward_master.reshape(-1, 3 * width),
            "wo": outward_master,
            "we": expand_master,
            "wr": reduce_master,
        }
        weights = {
            key: lax.all_gather(w.astype(BF), "dp", axis=0, tiled=True)
            for key, w in masters.items()
        }
    mask = jnp.where(buckets[:, 0, :] < BUCKETS, 0.0, masked_score)
    mask = jnp.pad(mask, ((0, -passages % 8), (0, ROWS - PLEN)), constant_values=masked_score)
    onehot = jnp.asarray(distance_onehot())
    line = lax.dot_general(
        table_master, onehot, (((0,), (1,)), ((), ())), precision=lax.Precision.HIGHEST
    )
    line = jnp.pad(line, ((0, -heads % 8), (0, 0)))
    f = forward(n, passages, heads, direct, tokens, cotangent, mask, gains_master, line, weights)
    wi, wo = (f["wi_out"], f["wo_out"]) if direct else (weights["wi"], weights["wo"])
    b = backward(n, passages, heads, direct, f, gains_master, wi, wo, onehot, states)
    layer_out = f["layer"][:, :PLEN].reshape(tokens.shape)
    input_grad = b["input_grad"][:, :PLEN].reshape(tokens.shape)
    new = {}
    if direct:
        for key in "ioergt":
            parts = ("_nw", "_nm", "_nv") + ("_nc",) * (key not in "gt")
            new[key] = [b[key + part] for part in parts]
        new["i"] = [a.transpose(1, 0, 2) for a in new["i"]]
    else:
        grads = {
            "i": b["inward_grad"], "o": f["outward_grad"], "e": f["expand_grad"], "r": f["reduce_grad"],
        }
        sums = {
            key: lax.psum_scatter(g.astype(F32), "dp", scatter_dimension=0, tiled=True)
            for key, g in grads.items()
        }
        small = lax.psum(b["small_out"], "dp")
        sums["i"] = sums["i"].reshape(inward_master.shape)
        sums["g"] = small[:2]
        sums["t"] = lax.dot_general(
            onehot, small[8 : 8 + heads, : 2 * ROWS], (((0,), (1,)), ((), ())),
            precision=lax.Precision.HIGHEST,
        )
        states["i"] = (inward_master, inward_first, inward_second)
        rates = {
            "i": rate_inward, "o": rate_outward, "e": rate_expand,
            "r": rate_reduce, "g": rate_gains, "t": rate_table,
        }
        for key in "ioergt":
            new[key] = list(adamw(*states[key], sums[key], rates[key]))
            if key not in "gt":
                new[key].append(new[key][0].astype(BF))
    outputs = [layer_out, input_grad]
    for key in "ioergt":
        outputs += new[key]
    return tuple(outputs)


def solution(mesh):
    rows = P("dp", None)
    inward = P("dp", None, "mp")
    tall = P(("mp", "dp"), None)
    wide = P("dp", "mp")
    table = P(None, "mp")
    return jax.shard_map(
        partial(shards, mesh.shape["dp"]),
        mesh=mesh,
        in_specs=(rows, rows, P("dp", None, None))
        + (inward,) * 3
        + (tall,) * 3
        + (wide,) * 3
        + (tall,) * 3
        + (P(),) * 3
        + (table,) * 3,
        out_specs=(rows, rows)
        + (inward,) * 4
        + (tall,) * 4
        + (wide,) * 4
        + (tall,) * 4
        + (P(),) * 3
        + (table,) * 3,
        check_vma=False,
    )
```

```python
from functools import partial
import math

import jax
import jax.numpy as jnp
import numpy as np
from jax import lax
from jax.experimental import pallas as pl
from jax.experimental.pallas import tpu as pltpu
from jax.sharding import PartitionSpec as P

DH = 64
PLEN = 250
STEP = 5
ROWS = 256
BUCKETS = 32
SPAN = 128

MESH = pl.DeviceIdType.MESH
BF = jnp.bfloat16
F32 = jnp.float32
MIB = 2**20

norm_eps = 1e-06
masked_score = -1000000000.0
beta_first = 0.5
beta_second = 0.5
adam_eps = 1e-08
decay_rate = 0.01
rate_inward = 0.015
rate_outward = 0.3
rate_expand = 0.04
rate_reduce = 0.02
rate_gains = 0.5
rate_table = 0.5


def adamw(weight, first_moment, second, gradient, step_rate):
    new_first = beta_first * first_moment + (1.0 - beta_first) * gradient
    new_second = beta_second * second + (1.0 - beta_second) * gradient * gradient
    first_hat = new_first / (1.0 - beta_first**STEP)
    second_hat = new_second / (1.0 - beta_second**STEP)
    new_weight = weight - step_rate * (
        first_hat / (jnp.sqrt(second_hat) + adam_eps) + decay_rate * weight
    )
    return (new_weight, new_first, new_second)


def distance_onehot():
    span = 2 * ROWS
    relative = np.arange(span)
    relative = np.where(relative < ROWS, relative, relative - span)
    half = BUCKETS // 2
    exact = half // 2
    distance = np.abs(relative)
    far = np.full_like(distance, exact)
    for level in range(1, half - exact):
        far += distance >= math.ceil(exact * (SPAN / exact) ** (level / (half - exact)))
    bucket = np.where(relative > 0, half, 0) + np.where(distance < exact, distance, far)
    return (bucket[:, None] == np.arange(BUCKETS)[None]).astype(np.float32)


def dot(a, b, ca=1, cb=0):
    return lax.dot_general(a, b, (((ca,), (cb,)), ((), ())), preferred_element_type=F32)


class Refs:
    pass


def run(kernel, grid, ins, outs, scratch, collective, limit, name):
    names = [i[0] for i in ins] + [o[0] for o in outs] + [s[0] for s in scratch]

    def body(*refs):
        space = Refs()
        for key, ref in zip(names, refs, strict=True):
            setattr(space, key, ref)
        kernel(space)

    results = pl.pallas_call(
        body,
        grid=grid,
        in_specs=[i[2] for i in ins],
        out_specs=[o[3] for o in outs],
        out_shape=[jax.ShapeDtypeStruct(o[1], o[2]) for o in outs],
        scratch_shapes=[s[1] for s in scratch],
        compiler_params=pltpu.CompilerParams(
            collective_id=collective, has_side_effects=True, vmem_limit_bytes=limit * MIB
        ),
        name=name,
    )(*[i[1] for i in ins])
    return dict(zip([o[0] for o in outs], results))


def whole(shape):
    return pl.BlockSpec(shape, lambda p: (0,) * len(shape), pipeline_mode=pl.Buffered(1))


def steps(first, count, shape):
    rest = (0,) * (len(shape) - 1)
    return pl.BlockSpec(shape, lambda p: (jnp.clip(p - first, 0, count - 1),) + rest)


ANY = pl.BlockSpec(memory_space=pl.ANY)


class Links:
    def __init__(self, n):
        me = lax.axis_index("dp")
        self.n, self.nz, self.me = n, n // 4, me
        x, y = lax.rem(me, 2), lax.rem(me // 2, 2)
        self.z, self.column = me // 4, lax.rem(me, 4)
        self.x_peer, self.y_peer = me + 1 - 2 * x, me + 2 - 4 * y
        self.far_peer = self.x_peer + 2 - 4 * y
        self.z_pair = self.z + 1 - 2 * lax.rem(self.z, 2)
        self.pair_peer = self.z_pair * 4 + self.column

    def z_peer(self, k):
        return lax.rem(self.z + k + self.nz, self.nz) * 4 + self.column

    def block(self, k, column_of, z=None):
        return lax.rem((self.z if z is None else z) + k, self.nz) * 4 + lax.rem(column_of, 4)

    def peers(self):
        ids = [self.x_peer, self.y_peer] + [self.z_peer(k) for k in range(1, self.nz)]
        return [{"dp": i} for i in ids]

    def column_peer(self, k):
        return self.z * 4 + lax.rem(self.column + k + 4, 4)


def greet(peers):
    barrier = pltpu.get_barrier_semaphore()
    for peer in peers:
        pl.semaphore_signal(barrier, inc=1, device_id=peer, device_id_type=MESH)
    pl.semaphore_wait(barrier, len(peers))


def partner():
    return {"mp": 1 - lax.axis_index("mp")}


def cut(ref, blk, rows):
    return ref.at[pl.ds(pl.multiple_of(blk * rows, 16), rows)]


def remote(src, dst, send, recv, peer):
    return pltpu.make_async_remote_copy(
        src_ref=src,
        dst_ref=dst,
        send_sem=send,
        recv_sem=recv,
        device_id=peer,
        device_id_type=MESH,
    )


class Gather:
    def __init__(self, links, full, ss, rs):
        self.l, self.full, self.ss, self.rs = links, full, ss, rs

    def at(self, a, blk):
        ref, rows, lanes = self.full[a]
        rows = pl.ds(pl.multiple_of(blk * rows, 16), rows)
        return ref.at[rows] if lanes is None else ref.at[rows, pl.ds(*lanes)]

    def copy(self, a, role, k, blk, peer):
        at = self.at(a, blk)
        return remote(at, at, self.ss.at[a, role, k], self.rs.at[a, role, k], {"dp": peer})

    def put(self, a, value):
        self.at(a, self.l.me)[...] = value

    def own(self, a):
        l = self.l
        for k in range(1, l.nz):
            self.copy(a, 0, k, l.me, l.z_peer(-k)).start()
        self.copy(a, 1, 0, l.me, l.x_peer).start()
        self.copy(a, 2, 0, l.me, l.y_peer).start()

    def along(self, a):
        l = self.l
        for k in range(1, l.nz):
            blk = l.block(k, l.me)
            self.copy(a, 0, k, blk, l.x_peer).wait_recv()
            self.copy(a, 1, k, blk, l.x_peer).start()
            self.copy(a, 2, k, blk, l.y_peer).start()

    def across(self, a):
        l = self.l
        for k in range(0, l.nz, 2):
            role, source, target = (1, l.x_peer, l.y_peer) if k % 4 == 0 else (2, l.y_peer, l.x_peer)
            blk = l.block(k, source)
            self.copy(a, role, k, blk, source).wait_recv()
            self.copy(a, 3, k, blk, target).start()

    def share(self, a):
        l = self.l
        for k in range(0, l.nz, 2):
            blk = l.block(k, l.far_peer)
            self.copy(a, 3, k, blk, l.x_peer).wait_recv()
            self.copy(a, 4, k, blk, l.pair_peer).start()

    def arrived(self, a):
        l = self.l
        for k in range(l.nz):
            if k % 4 != 0:
                self.copy(a, 1, k, l.block(k, l.x_peer), l.x_peer).wait_recv()
            if k % 4 != 2:
                self.copy(a, 2, k, l.block(k, l.y_peer), l.y_peer).wait_recv()
            if k % 2 == 0:
                self.copy(a, 4, k, l.block(k, l.far_peer, l.z_pair), l.pair_peer).wait_recv()

    def sent(self, a):
        l = self.l
        for k in range(l.nz):
            roles = (0,) * (k > 0) + (1, 2) + (3, 4) * (k % 2 == 0)
            for role in roles:
                self.copy(a, role, k, l.me, l.x_peer).wait_send()


class Scatter:
    def __init__(self, links, grads, bufs, ss, rs):
        self.l, self.grads, self.bufs, self.ss, self.rs = links, grads, bufs, ss, rs

    def part(self, a, blk):
        ref, rows = self.grads[a]
        return cut(ref, blk, rows)

    def read(self, a, blk):
        ref, rows = self.grads[a]
        return ref[pl.ds(pl.multiple_of(blk * rows, 16), rows), :].astype(F32)

    def copy(self, a, role, k, src, slot, peer):
        dst = self.bufs[a].at[slot, k]
        return remote(src, dst, self.ss.at[a, role, k], self.rs.at[a, role, k], {"dp": peer})

    def arrive(self, a, role, k, slot):
        self.copy(a, role, k, self.part(a, 0), slot, self.l.x_peer).wait_recv()

    def far(self, a):
        l = self.l
        for k in range(l.nz):
            peer = l.y_peer if k % 2 == 0 else l.x_peer
            self.copy(a, 0, k, self.part(a, l.block(k, l.far_peer)), 0, peer).start()

    def plain(self, a):
        l = self.l
        for k in range(l.nz):
            if k % 2 == 1:
                self.copy(a, 1, k, self.part(a, l.block(k, l.x_peer)), 2, l.x_peer).start()
            else:
                self.copy(a, 2, k, self.part(a, l.block(k, l.y_peer)), 4, l.y_peer).start()

    def near(self, a):
        l = self.l
        for k in range(l.nz):
            self.arrive(a, 0, k, 0)
            role, peer, slot = (1, l.x_peer, 1) if k % 2 == 0 else (2, l.y_peer, 3)
            mine = self.read(a, l.block(k, peer)) + self.bufs[a][0, k].astype(F32)
            self.bufs[a][slot, k] = mine.astype(BF)
            self.copy(a, role, k, self.bufs[a].at[slot, k], slot + 1, peer).start()

    def along(self, a, kept):
        l = self.l
        for k in list(range(1, l.nz)) + [0]:
            self.arrive(a, 1, k, 2)
            self.arrive(a, 2, k, 4)
            mine = (
                self.read(a, l.block(k, l.me))
                + self.bufs[a][2, k].astype(F32)
                + self.bufs[a][4, k].astype(F32)
            )
            if k == 0:
                kept[...] = mine
            else:
                self.bufs[a][5, k] = mine.astype(BF)
                self.copy(a, 3, k, self.bufs[a].at[5, k], 6, l.z_peer(k)).start()

    def total(self, a, kept):
        total = kept[...]
        for k in range(1, self.l.nz):
            self.arrive(a, 3, k, 6)
            total += self.bufs[a][6, k].astype(F32)
        return total

    def sent(self, a):
        for k in range(self.l.nz):
            for role in (0, 1, 2) + (3,) * (k > 0):
                self.copy(a, role, k, self.part(a, 0), 0, self.l.x_peer).wait_send()


class Swap:
    def __init__(self, mine, theirs, ss, rs):
        self.mine, self.theirs, self.ss, self.rs = mine, theirs, ss, rs

    def copy(self, slot):
        return remote(
            self.mine.at[slot], self.theirs.at[slot], self.ss.at[slot], self.rs.at[slot], partner()
        )

    def put(self, p, value):
        self.mine[lax.rem(p, 2)] = value.astype(BF)

    def send(self, p):
        self.copy(lax.rem(p, 2)).start()

    def take(self, p):
        slot = lax.rem(p, 2)
        self.copy(slot).wait()
        return self.mine[slot].astype(F32) + self.theirs[slot].astype(F32)


def swap_scratch(name, d):
    return [
        (name + "_mine", pltpu.VMEM((2, ROWS, d), BF)),
        (name + "_theirs", pltpu.VMEM((2, ROWS, d), BF)),
        (name + "_ss", pltpu.SemaphoreType.DMA((2,))),
        (name + "_rs", pltpu.SemaphoreType.DMA((2,))),
    ]


def swap_of(r, name):
    return Swap(*(getattr(r, name + part) for part in ("_mine", "_theirs", "_ss", "_rs")))


class Spread:
    def __init__(self, links, own, z_slots, xy_slots, ss, rs):
        self.l, self.own, self.z_slots, self.xy_slots = links, own, z_slots, xy_slots
        self.ss, self.rs = ss, rs

    def copy(self, stage, k, src, dst, peer):
        return remote(src, dst, self.ss.at[stage, k], self.rs.at[stage, k], {"dp": peer})

    def along(self):
        l = self.l
        self.z_slots[l.z] = self.own[...]
        for k in range(1, l.nz):
            self.copy(0, k, self.own, self.z_slots.at[l.z], l.z_peer(k)).start()

    def across(self):
        l = self.l
        for k in range(1, l.nz):
            self.copy(0, k, self.own, self.z_slots.at[lax.rem(l.z - k + l.nz, l.nz)], l.z_peer(k)).wait()
        total = self.z_slots[0]
        for k in range(1, l.nz):
            total += self.z_slots[k]
        self.own[...] = total
        self.xy_slots[l.column] = total
        for k in range(1, 4):
            self.copy(1, k, self.own, self.xy_slots.at[l.column], l.column_peer(k)).start()

    def total(self):
        l = self.l
        for k in range(1, 4):
            self.copy(1, k, self.own, self.xy_slots.at[lax.rem(l.column - k + 4, 4)], l.column_peer(k)).wait()
        total = self.xy_slots[0]
        for k in range(1, 4):
            total += self.xy_slots[k]
        return total


def every(step, actions):
    for at, what, argument in actions:
        pl.when(step == at)(partial(what, argument))


gelu_root = math.sqrt(2.0 / math.pi)
gelu_cube = 0.044715
WINDOW = 272


def inverse_rms(v):
    return lax.rsqrt(jnp.mean(v * v, axis=-1, keepdims=True) + norm_eps)


def window_start(p, total):
    return min(p * PLEN // 16 * 16, total - WINDOW)


def align(source, target, windows, sems, passages):
    total = source.shape[0]

    def fetch(p):
        return pltpu.make_async_copy(
            source.at[pl.ds(window_start(p, total), WINDOW)], windows.at[p % 2], sems.at[p % 2]
        )

    def start():
        fetch(0).start()
        fetch(1).start()

    def move(first, last):
        for p in range(first, last):
            fetch(p).wait()
            off = p * PLEN - window_start(p, total)
            rows = windows[p % 2].astype(F32)[off : off + PLEN]
            pad = jnp.zeros((ROWS - PLEN, rows.shape[1]), F32)
            target[p] = jnp.concatenate([rows, pad], axis=0).astype(BF)
            if p + 2 < passages:
                fetch(p + 2).start()

    return start, move


PAIR = 2 * DH


def attend_kernel(n, passages, heads, direct, r):
    s = pl.program_id(0)
    pairs = heads // 2
    att = swap_of(r, "att")
    if direct:
        links = Links(n)
        rows_i, rows_o = r.wi.shape[0] // n, r.wo_wide.shape[0] // n
        full = [(r.wi, rows_i, (3 * PAIR * j, 3 * PAIR)) for j in range(pairs)]
        full += [(r.wo_wide, rows_o, None)]
        full += [(r.we, r.we.shape[0] // n, None), (r.wr, r.wr.shape[0] // n, None)]
        o, e, red = pairs, pairs + 1, pairs + 2
        gather = Gather(links, full, r.g_ss, r.g_rs)
    tok_start, tok_move = align(r.tokens, r.tok, r.tok_window, r.tok_sem, passages)
    cot_start, cot_move = align(r.cotangent, r.cot, r.cot_window, r.cot_sem, passages)

    def local(src, dst, i):
        return pltpu.make_async_copy(src, dst, r.out_sem.at[i])

    @pl.when(s == 0)
    def _():
        tok_start()
        cot_start()
        if direct:
            for j in range(pairs):
                lanes = slice(j * PAIR, (j + 1) * PAIR)
                gather.put(j, jnp.concatenate([r.own_i[c][:, lanes] for c in range(3)], axis=1).astype(BF))
            pad = jnp.zeros((rows_o - r.own_o.shape[0], r.own_o.shape[1]), F32)
            gather.put(o, jnp.concatenate([r.own_o[...], pad], axis=0).astype(BF))
            gather.put(e, r.own_e[0])
            gather.put(red, r.own_r[: full[red][1]].astype(BF))
            greet(links.peers() + [partner()])
            for a in range(pairs + 1):
                gather.own(a)
        else:
            greet([partner()])
        tok_move(0, passages // 2)
        if direct:
            gather.along(0)
            gather.along(1)
        tok_move(passages // 2, passages)
        local(r.tok, r.tok_out, 0).start()
        if direct:
            gather.across(0)
            gather.along(2)
            gather.across(1)
            gather.share(0)
        cot_move(0, passages // 2)
        if direct:
            gather.along(o)
            gather.across(2)
            gather.share(1)
            gather.own(e)
        cot_move(passages // 2, passages)
        local(r.cot, r.cot_out, 1).start()
        for h in range(heads):
            line = dot_exact(r.table[h : h + 1, :], r.onehot[...])
            rows = jnp.broadcast_to(line, (ROWS, 2 * ROWS))
            r.bias[h] = pltpu.roll(rows, 0, 1, stride=1, stride_axis=0)[:, :ROWS]
        if direct:
            gather.across(o)
            gather.share(2)
            gather.own(red)
            gather.share(o)
            for j in range(pairs):
                gather.arrived(j)

    @pl.when(s < passages)
    def _():
        x = r.tok[s].astype(F32)
        normed = (x * inverse_rms(x) * r.gains[0:1, :]).astype(BF)
        r.normed[0] = normed
        r.proj[0] = dot(normed, r.wi[...]).astype(BF)
        valid = r.buckets[0, pl.ds(s, 1), :] < BUCKETS
        masked = jnp.concatenate(
            [jnp.where(valid, 0.0, masked_score), jnp.full((1, ROWS - PLEN), masked_score, F32)], axis=1
        )
        for h in range(heads):
            first = h // 2 * 3 * PAIR + h % 2 * DH
            q, k, v = (r.proj[0, :, first + c * PAIR : first + c * PAIR + DH] for c in range(3))
            sc = dot(q, k, 1, 1) + r.bias[h] + masked
            e_ = jnp.exp(sc - jnp.max(sc, axis=-1, keepdims=True))
            a = (e_ * (1.0 / jnp.sum(e_, axis=-1, keepdims=True))).astype(BF)
            r.probs[0, h] = a
            r.ctx[0, :, h * DH : (h + 1) * DH] = dot(a, v).astype(BF)

    if direct:

        @pl.when(s == 0)
        def _():
            gather.arrived(o)
            rows = r.own_o.shape[0]
            for d in range(n):
                block = r.wo_wide[d * rows_o : (d + 1) * rows_o, :].astype(F32)
                r.wo_f32[d * rows : (d + 1) * rows, :] = block[:rows]
            r.wo[...] = r.wo_f32[...].astype(BF)

        every(s, (
            (1, gather.along, e), (2, gather.along, red), (2, gather.across, e), (4, gather.across, red),
            (4, gather.share, e), (5, gather.share, red),
        ))

        @pl.when(s == passages - 1)
        def _():
            local(r.wi, r.wi_out, 2).start()
            local(r.wo, r.wo_out, 3).start()

    @pl.when(s < passages)
    def _():
        att.put(s, dot(r.ctx[0], r.wo[...]))

    if direct:

        @pl.when(s == passages)
        def _():
            gather.arrived(e)
            gather.arrived(red)
            local(r.we, r.we_out, 4).start()
            local(r.wr, r.wr_out, 5).start()

    @pl.when(s > 0)
    def _():
        last = s - 1
        r.hidden[0] = r.tok[last].astype(F32) + att.take(last)

    @pl.when(s < passages)
    def _():
        att.send(s)

    @pl.when(s == passages)
    def _():
        local(r.tok, r.tok_out, 0).wait()
        local(r.cot, r.cot_out, 1).wait()
        if direct:
            for a in range(pairs + 3):
                gather.sent(a)
            local(r.wi, r.wi_out, 2).wait()
            local(r.wo, r.wo_out, 3).wait()
            local(r.we, r.we_out, 4).wait()
            local(r.wr, r.wr_out, 5).wait()


def dot_exact(a, b):
    return lax.dot_general(
        a, b, (((1,), (1,)), ((), ())), precision=lax.Precision.HIGHEST, preferred_element_type=F32
    )


def attend(n, passages, heads, direct, tokens, cotangent, buckets, gains, table, onehot, weights):
    d = tokens.shape[1]
    width = heads * DH
    one = (1, ROWS, d)
    ins = [("tokens", tokens, ANY), ("cotangent", cotangent, ANY)]
    first_rows = pl.BlockSpec((1,) + buckets.shape[1:], lambda p: (0, 0, 0), pipeline_mode=pl.Buffered(1))
    ins += [("buckets", buckets, first_rows)]
    ins += [(k, v, whole(v.shape)) for k, v in (("gains", gains), ("table", table), ("onehot", onehot))]
    ins += [(k, v, whole(v.shape)) for k, v in weights.items()]
    outs = [
        ("proj", (passages, ROWS, 3 * width), BF, steps(0, passages, (1, ROWS, 3 * width))),
        ("probs", (passages, heads, ROWS, ROWS), BF, steps(0, passages, (1, heads, ROWS, ROWS))),
        ("normed", (passages, ROWS, d), BF, steps(0, passages, one)),
        ("ctx", (passages, ROWS, width), BF, steps(0, passages, (1, ROWS, width))),
        ("hidden", (passages, ROWS, d), F32, steps(1, passages, one)),
        ("tok_out", (passages, ROWS, d), BF, ANY),
        ("cot_out", (passages, ROWS, d), BF, ANY),
    ]
    scratch = [
        ("tok", pltpu.VMEM((passages, ROWS, d), BF)),
        ("cot", pltpu.VMEM((passages, ROWS, d), BF)),
        ("tok_window", pltpu.VMEM((2, WINDOW, d), BF)),
        ("cot_window", pltpu.VMEM((2, WINDOW, d), BF)),
        ("tok_sem", pltpu.SemaphoreType.DMA((2,))),
        ("cot_sem", pltpu.SemaphoreType.DMA((2,))),
        ("out_sem", pltpu.SemaphoreType.DMA((6,))),
        ("bias", pltpu.VMEM((heads, ROWS, ROWS), F32)),
    ] + swap_scratch("att", d)
    if direct:
        part = weights["own_r"].shape[0] // 2 * n
        padded = weights["own_o"].shape[0]
        padded += -padded % 16
        shapes = {"wi": (d, 3 * width), "wo": (width, d), "we": (d, part), "wr": (part, d)}
        for key, shape in shapes.items():
            outs.append((key + "_out", shape, BF, ANY))
            scratch.append((key, pltpu.VMEM(shape, BF)))
        arrays = heads // 2 + 3
        scratch += [
            ("wo_f32", pltpu.VMEM((width, d), F32)),
            ("wo_wide", pltpu.VMEM((n * padded, d), BF)),
            ("g_ss", pltpu.SemaphoreType.DMA((arrays, 5, n // 4))),
            ("g_rs", pltpu.SemaphoreType.DMA((arrays, 5, n // 4))),
        ]
    kernel = partial(attend_kernel, n, passages, heads, direct)
    return run(kernel, (passages + 1,), ins, outs, scratch, 1, 60, "attend")


def feed_kernel(n, passages, direct, r):
    s = pl.program_id(0)
    count = passages
    out, back_in = (swap_of(r, name) for name in ("out", "in"))
    if direct:
        links = Links(n)
        full = [(r.we_b, r.we_b.shape[0] // n, None), (r.wr_b, r.wr_b.shape[0] // n, None)]
        gather = Gather(links, full, r.g_ss, r.g_rs)
        grads = [(g, g.shape[0] // n) for g in (r.stage_r, r.stage_e)]
        kept = [r.sum_r, r.sum_e]
        sums = Scatter(links, grads, [r.buf_r, r.buf_e], r.s_ss, r.s_rs)

    @pl.when(s == 0)
    def _():
        if direct:
            gather.put(0, r.own_e[1])
            gather.put(1, r.own_r[full[1][1] :].astype(BF))
            greet(links.peers() + [partner()])
            gather.own(0)
            gather.own(1)
        else:
            greet([partner()])
        r.gain_grad[...] = jnp.zeros_like(r.gain_grad)

    @pl.when((s == 0) | (s == count))
    def _():
        r.acc_r[...] = jnp.zeros_like(r.acc_r)
        r.acc_e[...] = jnp.zeros_like(r.acc_e)

    if direct:
        every(s, (
            (1, gather.along, 0), (2, gather.along, 1), (2, gather.across, 0), (4, gather.across, 1),
            (4, gather.share, 0), (6, gather.share, 1), (count, gather.arrived, 0), (count, gather.arrived, 1),
            (count, sums.far, 0), (count, sums.far, 1), (count, sums.plain, 0), (count, sums.plain, 1),
            (count + 2, sums.near, 0), (count + 3, sums.near, 1),
        ))
        for a in range(2):
            pl.when(s == count + 6 + a)(partial(sums.along, a, kept[a]))

    def part(normed, c, we, wr):
        u = dot(normed, we[...])
        square = u * u
        t = jnp.tanh(u * (gelu_root + (gelu_root * gelu_cube) * square))
        half = 0.5 * (1.0 + t)
        act = (u * half).astype(BF)
        slope = half + (0.5 * u) * (1.0 - t * t) * (
            gelu_root + (3.0 * gelu_root * gelu_cube) * square
        )
        back = (dot(c, wr[...], 1, 1) * slope).astype(BF)
        r.acc_r[...] += dot(act, c, 0, 0)
        r.acc_e[...] += dot(normed, back, 0, 0)
        return dot(act, wr[...]), dot(back, we[...], 1, 1)

    @pl.when(s < count)
    def _():
        h = r.hidden_now[0]
        normed = (h * inverse_rms(h) * r.gains[1:2, :]).astype(BF)
        r.normed_two[s] = normed
        r.out_sum[s], r.in_sum[s] = part(normed, r.cot_now[0], r.we_a, r.wr_a)

    @pl.when(s == count - 1)
    def _():
        r.stage_r[...] = r.acc_r[...].astype(BF)
        r.stage_e[...] = r.acc_e[...].astype(BF)

    p = s - count

    @pl.when((s >= count) & (s < 2 * count))
    def _():
        r_part, n_part = part(r.normed_two[p], r.cot_now[0], r.we_b, r.wr_b)
        out.put(p, r.out_sum[p] + r_part)
        back_in.put(p, r.in_sum[p] + n_part)

    @pl.when(s == 2 * count - 1)
    def _():
        r.grad_r[...] = r.acc_r[...].astype(BF)
        r.grad_e[...] = r.acc_e[...].astype(BF)

    @pl.when(s > count)
    def _():
        last = p - 1
        h = r.hidden[0]
        r.layer[0] = (h + out.take(last)).astype(BF)
        grad = back_in.take(last)
        inv = inverse_rms(h)
        zed = r.gains[1:2, :] * grad
        hr = h * inv
        r.gain_grad[0:1, :] += jnp.sum(grad * hr, axis=0, keepdims=True)
        inner = jnp.mean(zed * hr, axis=-1, keepdims=True)
        hidden_grad = r.cot[0].astype(F32) + inv * (zed - hr * inner)
        r.hidden_grad[0] = hidden_grad
        r.above[0] = hidden_grad.astype(BF)

    @pl.when((s >= count) & (s < 2 * count))
    def _():
        out.send(p)
        back_in.send(p)

    if direct:

        @pl.when(s == 2 * count)
        def _():
            for a in range(2):
                kept[a][...] = sums.total(a, kept[a])
            for a in range(2):
                gather.sent(a)
                sums.sent(a)


def feed(n, passages, direct, f, gains, weights):
    d = gains.shape[1]
    one = (1, ROWS, d)
    late = steps(passages + 1, passages, one)
    again = pl.BlockSpec(one, lambda p: (lax.rem(jnp.minimum(p, 2 * passages - 1), passages), 0, 0))
    ins = [
        ("hidden_now", f["hidden"], steps(0, passages, one)),
        ("hidden", f["hidden"], late),
        ("cot_now", f["cot_out"], again),
        ("cot", f["cot_out"], late),
    ]
    fixed = dict(weights, gains=gains)
    part = weights["wr_a"].shape[0]
    outs = [
        ("layer", (passages, ROWS, d), BF, late),
        ("hidden_grad", (passages, ROWS, d), F32, late),
        ("above", (passages, ROWS, d), BF, late),
        ("grad_r", (part, d), BF, whole((part, d))),
        ("grad_e", (d, part), BF, whole((d, part))),
        ("gain_grad", (8, d), F32, whole((8, d))),
    ]
    scratch = [
        ("normed_two", pltpu.VMEM((passages, ROWS, d), BF)),
        ("out_sum", pltpu.VMEM((passages, ROWS, d), F32)),
        ("in_sum", pltpu.VMEM((passages, ROWS, d), F32)),
        ("acc_r", pltpu.VMEM((part, d), F32)),
        ("acc_e", pltpu.VMEM((d, part), F32)),
    ]
    stage = [("stage_r", (part, d)), ("stage_e", (d, part))]
    if direct:
        scratch += [(k, pltpu.VMEM(shape, BF)) for k, shape in stage]
        nz = n // 4
        scratch += [
            ("we_b", pltpu.VMEM((d, part), BF)),
            ("wr_b", pltpu.VMEM((part, d), BF)),
            ("buf_r", pltpu.VMEM((7, nz, part // n, d), BF)),
            ("buf_e", pltpu.VMEM((7, nz, d // n, part), BF)),
            ("g_ss", pltpu.SemaphoreType.DMA((2, 5, nz))),
            ("g_rs", pltpu.SemaphoreType.DMA((2, 5, nz))),
            ("s_ss", pltpu.SemaphoreType.DMA((2, 4, nz))),
            ("s_rs", pltpu.SemaphoreType.DMA((2, 4, nz))),
        ]
        for key, shape in (("sum_r", (part // n, d)), ("sum_e", (d // n, part))):
            outs.append((key, shape, F32, whole(shape)))
    else:
        outs += [(k, shape, BF, whole(shape)) for k, shape in stage]
    for name in ("out", "in"):
        scratch += swap_scratch(name, d)
    ins += [(k, v, whole(v.shape)) for k, v in fixed.items()]
    kernel = partial(feed_kernel, n, passages, direct)
    return run(kernel, (2 * passages + 1,), ins, outs, scratch, 2, 60, "feed")


def back_kernel(n, passages, heads, direct, r):
    s = pl.program_id(0)
    pairs = heads // 2
    count = passages
    rounds = pairs * count
    swap = swap_of(r, "in")
    stage = [getattr(r, f"stage_i{j}") for j in range(pairs)]
    if direct:
        links = Links(n)
        refs = [r.grad_r, r.grad_e, r.stage_o] + stage
        grads = [(g, g.shape[0] // n) for g in refs]
        names = ["r", "e", "o"] + [f"i{j}" for j in range(pairs)]
        bufs = [getattr(r, "buf_" + k) for k in names]
        kept = [getattr(r, "sum_" + k) for k in names]
        sums = Scatter(links, grads, bufs, r.s_ss, r.s_rs)
        wide = Spread(links, r.wide, r.wide_z, r.wide_xy, r.w_ss, r.w_rs)
        last_small = Spread(links, r.slim, r.slim_z, r.slim_xy, r.l_ss, r.l_rs)

    @pl.when(s == 0)
    def _():
        if direct:
            greet(links.peers() + [{"dp": links.far_peer}, partner()])
            for a in range(2):
                sums.far(a)
            for a in range(2):
                sums.plain(a)
        else:
            greet([partner()])
        r.acc_o[...] = jnp.zeros_like(r.acc_o)
        r.acc_s[...] = jnp.zeros_like(r.acc_s)
        r.gain_one[...] = jnp.zeros_like(r.gain_one)

    if direct:
        near = [(0, 3), (1, 4), (2, count + 3)] + [(3 + j, (j + 1) * count + 5 - j) for j in range(pairs)]
        far = [(2, count)] + [(3 + j, (j + 1) * count) for j in range(pairs)]
        along = [(0, 8), (1, 10), (2, count + 6)] + [(3 + j, (j + 1) * count + 8 - j) for j in range(pairs)]
        for a, at in far:
            every(s, ((at, sums.far, a), (at, sums.plain, a)))
        for a, at in near:
            every(s, ((at, sums.near, a),))
        for a, at in along:
            pl.when(s == at)(partial(sums.along, a, kept[a]))

    j, p = s // count, lax.rem(s, count)

    @pl.when(s < count)
    def _():
        above = r.above[0]
        r.acc_o[...] += dot(r.ctx[0], above, 0, 0)
        dctx = dot(above, r.wo[...], 1, 1).astype(BF)
        for i in range(pairs):
            r.dctx[i, p] = dctx[:, i * PAIR : (i + 1) * PAIR]

    @pl.when((s < rounds) & (p == 0))
    def _():
        r.acc_i[...] = jnp.zeros_like(r.acc_i)

    @pl.when(s < rounds)
    def _():
        grads_of = [[], [], []]
        dc_pair = r.dctx[j, p]
        for h in range(2):
            q, k, v = (r.proj[0, :, c * PAIR + h * DH : c * PAIR + (h + 1) * DH] for c in range(3))
            dc = dc_pair[:, h * DH : (h + 1) * DH]
            a = r.probs[0, h]
            grads_of[2].append(dot(a, dc, 0, 0))
            dp = dot(dc, v, 1, 1)
            a = a.astype(F32)
            centre = jnp.sum(a * dp, axis=-1, keepdims=True)
            ds = (a * (dp - centre)).astype(BF)
            r.acc_s[2 * j + h] += ds.astype(F32)
            grads_of[0].append(dot(ds, k))
            grads_of[1].append(dot(ds, q, 0, 0))
        dproj = jnp.concatenate([g for c in range(3) for g in grads_of[c]], axis=1).astype(BF)
        r.dproj[p, :, pl.ds(pl.multiple_of(j * 3 * PAIR, 3 * PAIR), 3 * PAIR)] = dproj
        r.acc_i[...] += dot(r.normed[0], dproj, 0, 0)

    @pl.when(s == count - 1)
    def _():
        blocks = n if direct else 1
        rows = r.acc_o.shape[0] // blocks
        padded = r.stage_o.shape[0] // blocks
        for b in range(blocks):
            part = r.acc_o[b * rows : (b + 1) * rows, :]
            if padded > rows:
                part = jnp.concatenate([part, jnp.zeros((padded - rows, part.shape[1]), F32)], axis=0)
            r.stage_o[b * padded : (b + 1) * padded, :] = part.astype(BF)

    for i in range(pairs):

        @pl.when(s == (i + 1) * count - 1)
        def _():
            stage[i][...] = r.acc_i[...].astype(BF)

    @pl.when(s == rounds)
    def _():
        r.wide[...] = jnp.zeros_like(r.wide)
        r.wide[heads : heads + 1, :] = r.gain_two[0:1, :]
        for h in range(heads):
            rows = jnp.concatenate([r.acc_s[h], jnp.zeros((ROWS, ROWS), F32)], axis=1)
            while rows.shape[0] > 1:
                half = rows.shape[0] // 2
                rows = rows[:half] + pltpu.roll(rows[half:], 2 * ROWS - half, 1)
            r.wide[h : h + 1, : 2 * ROWS] = rows
        if direct:
            wide.along()

    if direct:
        pl.when(s == rounds + 2)(wide.across)

    t = s - rounds

    @pl.when((s >= rounds) & (s < rounds + count))
    def _():
        swap.put(t, dot(r.dproj[t], r.wi[...], 1, 1))

    @pl.when(s > rounds)
    def _():
        x = r.tok[0].astype(F32)
        grad = swap.take(t - 1)
        inv = inverse_rms(x)
        zed = r.gains[0:1, :] * grad
        xr = x * inv
        r.gain_one[0:1, :] += jnp.sum(grad * xr, axis=0, keepdims=True)
        inner = jnp.mean(zed * xr, axis=-1, keepdims=True)
        r.input_grad[0] = r.hidden_grad[0] + inv * (zed - xr * inner)

    @pl.when((s >= rounds) & (s < rounds + count))
    def _():
        swap.send(t)

    @pl.when(s == rounds + count)
    def _():
        if not direct:
            r.wide_sum[...] = r.wide[...]
            r.slim_sum[...] = r.gain_one[...]
            return
        d = r.gain_one.shape[1]
        for c in range(d // 128):
            r.slim[c : c + 1, :] = r.gain_one[0:1, c * 128 : (c + 1) * 128]
        for c in range(d // 128, 8):
            r.slim[c : c + 1, :] = jnp.zeros((1, 128), F32)
        last_small.along()
        r.wide_sum[...] = wide.total()
        for a in range(3):
            kept[a][...] = sums.total(a, kept[a])
        last_small.across()
        for a in range(3, 3 + pairs):
            kept[a][...] = sums.total(a, kept[a])
        r.slim_sum[...] = last_small.total()
        for a in range(3 + pairs):
            sums.sent(a)


def back(n, passages, heads, direct, f, m, gains, wi, wo):
    d = gains.shape[1]
    width = heads * DH
    pairs = heads // 2
    rounds = pairs * passages
    one = (1, ROWS, d)
    first = lambda shape: steps(0, passages, shape)
    late = steps(rounds + 1, passages, one)

    def turn(s):
        s = jnp.minimum(s, rounds - 1)
        return s // passages, lax.rem(s, passages)

    ins = [
        ("above", m["above"], first(one)),
        ("ctx", f["ctx"], first((1, ROWS, width))),
        ("normed", f["normed"], pl.BlockSpec(one, lambda s: (turn(s)[1], 0, 0))),
        ("proj", f["proj"], pl.BlockSpec((1, ROWS, 3 * PAIR), lambda s: (turn(s)[1], 0, turn(s)[0]))),
        ("probs", f["probs"], pl.BlockSpec((1, 2, ROWS, ROWS), lambda s: (turn(s)[1], turn(s)[0], 0, 0))),
        ("tok", f["tok_out"], late),
        ("hidden_grad", m["hidden_grad"], late),
    ]
    fixed = [("gains", gains), ("wi", wi), ("wo", wo), ("gain_two", m["gain_grad"])]
    outs = [
        ("input_grad", (passages, ROWS, d), F32, late),
        ("wide_sum", (8, d), F32, whole((8, d))),
    ]
    scratch = [
        ("acc_i", pltpu.VMEM((d, 3 * PAIR), F32)),
        ("acc_o", pltpu.VMEM((width, d), F32)),
        ("acc_s", pltpu.VMEM((heads, ROWS, ROWS), F32)),
        ("dctx", pltpu.VMEM((pairs, passages, ROWS, PAIR), BF)),
        ("dproj", pltpu.VMEM((passages, ROWS, 3 * width), BF)),
        ("gain_one", pltpu.VMEM((8, d), F32)),
        ("wide", pltpu.VMEM((8, d), F32)),
    ] + swap_scratch("in", d)
    rows_o = width
    if direct:
        rows_o = width // n
        rows_o = (rows_o + -rows_o % 16) * n
    stage = [("stage_o", (rows_o, d))] + [(f"stage_i{j}", (d, 3 * PAIR)) for j in range(pairs)]
    if direct:
        nz = n // 4
        fixed += [(k, m[k]) for k in ("grad_r", "grad_e")]
        scratch += [(k, pltpu.VMEM(shape, BF)) for k, shape in stage]
        blocks = {"r": m["grad_r"].shape, "e": m["grad_e"].shape, "o": (rows_o, d)}
        blocks.update({f"i{j}": (d, 3 * PAIR) for j in range(pairs)})
        for key, shape in blocks.items():
            shape = (shape[0] // n, shape[1])
            scratch.append(("buf_" + key, pltpu.VMEM((7, nz) + shape, BF)))
            outs.append(("sum_" + key, shape, F32, whole(shape)))
        outs.append(("slim_sum", (8, 128), F32, whole((8, 128))))
        scratch += [
            ("wide_z", pltpu.VMEM((nz, 8, d), F32)),
            ("wide_xy", pltpu.VMEM((4, 8, d), F32)),
            ("slim", pltpu.VMEM((8, 128), F32)),
            ("slim_z", pltpu.VMEM((nz, 8, 128), F32)),
            ("slim_xy", pltpu.VMEM((4, 8, 128), F32)),
            ("s_ss", pltpu.SemaphoreType.DMA((len(blocks), 4, nz))),
            ("s_rs", pltpu.SemaphoreType.DMA((len(blocks), 4, nz))),
        ]
        for key in ("w_ss", "w_rs", "l_ss", "l_rs"):
            scratch.append((key, pltpu.SemaphoreType.DMA((2, max(nz, 4)))))
    else:
        outs += [(k, shape, BF, whole(shape)) for k, shape in stage]
        outs.append(("slim_sum", (8, d), F32, whole((8, d))))
    ins += [(k, v, whole(v.shape)) for k, v in fixed]
    kernel = partial(back_kernel, n, passages, heads, direct)
    return run(kernel, (rounds + passages + 1,), ins, outs, scratch, 3, 60, "back")


def shards(
    n,
    tokens,
    cotangent,
    buckets,
    inward_master,
    inward_first,
    inward_second,
    outward_master,
    outward_first,
    outward_second,
    expand_master,
    expand_first,
    expand_second,
    reduce_master,
    reduce_first,
    reduce_second,
    gains_master,
    gains_first,
    gains_second,
    table_master,
    table_first,
    table_second,
):
    d = tokens.shape[1]
    passages = tokens.shape[0] // PLEN
    heads = inward_master.shape[2] // DH
    pairs = heads // 2
    rows_i, rows_e, rows_r = inward_master.shape[0], expand_master.shape[0], reduce_master.shape[0]
    units = expand_master.shape[1]
    direct = n % 8 == 0 and rows_i % 16 == 0 and rows_r % 32 == 0 and outward_master.shape[0] % 8 == 0

    def by_pairs(a):
        return a.reshape(-1, 3, pairs, PAIR).transpose(0, 2, 1, 3).reshape(-1, 3 * pairs * PAIR)

    def unit_halves(a):
        return a.reshape(rows_e, n, 2, units // (2 * n)).transpose(2, 0, 1, 3).reshape(2, rows_e, -1)

    def unit_order(a):
        return a.reshape(2, rows_e, n, units // (2 * n)).transpose(1, 2, 0, 3).reshape(rows_e, units)

    onehot = jnp.asarray(distance_onehot())
    bucket_rows = buckets.transpose(1, 0, 2)
    table_rows = jnp.pad(table_master.T, ((0, -heads % 8), (0, 0)))
    if direct:
        own_e = unit_halves(expand_master.astype(BF))
        first = {
            "own_i": inward_master.transpose(1, 0, 2),
            "own_o": outward_master,
            "own_e": own_e,
            "own_r": reduce_master,
        }
    else:
        masters = (by_pairs(inward_master), outward_master, expand_master, reduce_master)
        wi, wo, we, wr = (
            lax.all_gather(w.astype(BF), "dp", axis=0, tiled=True) for w in masters
        )
        first = {"wi": wi, "wo": wo}
    f = attend(
        n, passages, heads, direct, tokens, cotangent, bucket_rows, gains_master, table_rows, onehot, first
    )
    if direct:
        wi, wo = f["wi_out"], f["wo_out"]
        second = {"we_a": f["we_out"], "wr_a": f["wr_out"], "own_e": own_e, "own_r": reduce_master}
    else:
        half = units // 2
        second = {"we_a": we[:, :half], "wr_a": wr[:half], "we_b": we[:, half:], "wr_b": wr[half:]}
    m = feed(n, passages, direct, f, gains_master, second)
    b = back(n, passages, heads, direct, f, m, gains_master, wi, wo)

    def scatter(g):
        return lax.psum_scatter(g.astype(F32), "dp", scatter_dimension=0, tiled=True)

    if direct:
        inward_parts = [b[f"sum_i{j}"] for j in range(pairs)]
        outward_sum = b["sum_o"][: outward_master.shape[0]]
        expand_sum = unit_order(jnp.stack([m["sum_e"], b["sum_e"]]))
        reduce_sum = jnp.concatenate([m["sum_r"], b["sum_r"]], axis=0)
        wide_sum = b["wide_sum"]
        gain_one = b["slim_sum"][: d // 128].reshape(1, d)
    else:
        inward_parts = [scatter(b[f"stage_i{j}"]) for j in range(pairs)]
        outward_sum = scatter(b["stage_o"])
        expand_sum = scatter(jnp.concatenate([m["stage_e"], m["grad_e"]], axis=1))
        reduce_sum = scatter(jnp.concatenate([m["stage_r"], m["grad_r"]], axis=0))
        wide_sum, gain_one = lax.psum((b["wide_sum"], b["slim_sum"][:1]), "dp")
    inward_sum = jnp.stack([g.reshape(-1, 3, PAIR) for g in inward_parts], axis=2)
    inward_sum = inward_sum.reshape(inward_master.shape)
    gains_sum = jnp.concatenate([gain_one, wide_sum[heads : heads + 1]], axis=0)
    table_sum = lax.dot_general(
        onehot.T, wide_sum[:heads, : 2 * ROWS], (((1,), (1,)), ((), ())), precision=lax.Precision.HIGHEST
    )

    layer_out = m["layer"][:, :PLEN].reshape(tokens.shape)
    input_grad = b["input_grad"][:, :PLEN].reshape(tokens.shape)
    outputs = [layer_out, input_grad]
    for w, first_moment, second_moment, gradient, rate, copied in (
        (inward_master, inward_first, inward_second, inward_sum, rate_inward, True),
        (outward_master, outward_first, outward_second, outward_sum, rate_outward, True),
        (expand_master, expand_first, expand_second, expand_sum, rate_expand, True),
        (reduce_master, reduce_first, reduce_second, reduce_sum, rate_reduce, True),
        (gains_master, gains_first, gains_second, gains_sum, rate_gains, False),
        (table_master, table_first, table_second, table_sum, rate_table, False),
    ):
        new = adamw(w, first_moment, second_moment, gradient, rate)
        outputs += list(new)
        if copied:
            outputs.append(new[0].astype(BF))
    return tuple(outputs)


def solution(mesh):
    rows = P("dp", None)
    inward = P("dp", None, "mp")
    tall = P(("mp", "dp"), None)
    wide = P("dp", "mp")
    table = P(None, "mp")
    return jax.shard_map(
        partial(shards, mesh.shape["dp"]),
        mesh=mesh,
        in_specs=(rows, rows, P("dp", None, None))
        + (inward,) * 3
        + (tall,) * 3
        + (wide,) * 3
        + (tall,) * 3
        + (P(),) * 3
        + (table,) * 3,
        out_specs=(rows, rows)
        + (inward,) * 4
        + (tall,) * 4
        + (wide,) * 4
        + (tall,) * 4
        + (P(),) * 3
        + (table,) * 3,
        check_vma=False,
    )
```

```python
from functools import partial
import math

import jax
import jax.numpy as jnp
import numpy as np
from jax import lax
from jax.experimental import pallas as pl
from jax.experimental.pallas import tpu as pltpu
from jax.sharding import PartitionSpec as P

DH = 64
PLEN = 250
STEP = 5
ROWS = 256
BUCKETS = 32
SPAN = 128

MESH = pl.DeviceIdType.MESH
BF = jnp.bfloat16
F32 = jnp.float32
MIB = 2**20

norm_eps = 1e-06
masked_score = -1000000000.0
beta_first = 0.5
beta_second = 0.5
adam_eps = 1e-08
decay_rate = 0.01
rate_inward = 0.015
rate_outward = 0.3
rate_expand = 0.04
rate_reduce = 0.02
rate_gains = 0.5
rate_table = 0.5


def adamw(weight, first_moment, second, gradient, step_rate):
    new_first = beta_first * first_moment + (1.0 - beta_first) * gradient
    new_second = beta_second * second + (1.0 - beta_second) * gradient * gradient
    first_hat = new_first / (1.0 - beta_first**STEP)
    second_hat = new_second / (1.0 - beta_second**STEP)
    new_weight = weight - step_rate * (
        first_hat / (jnp.sqrt(second_hat) + adam_eps) + decay_rate * weight
    )
    return (new_weight, new_first, new_second)


def distance_onehot():
    span = 2 * ROWS
    relative = np.arange(span)
    relative = np.where(relative < ROWS, relative, relative - span)
    half = BUCKETS // 2
    exact = half // 2
    distance = np.abs(relative)
    far = np.full_like(distance, exact)
    for level in range(1, half - exact):
        far += distance >= math.ceil(exact * (SPAN / exact) ** (level / (half - exact)))
    bucket = np.where(relative > 0, half, 0) + np.where(distance < exact, distance, far)
    return (bucket[:, None] == np.arange(BUCKETS)[None]).astype(np.float32)


def dot(a, b, ca=1, cb=0):
    return lax.dot_general(a, b, (((ca,), (cb,)), ((), ())), preferred_element_type=F32)


class Refs:
    pass


def run(kernel, ins, outs, scratch, collective, limit, name):
    names = [i[0] for i in ins] + [o[0] for o in outs] + [s[0] for s in scratch]

    def body(*refs):
        space = Refs()
        for key, ref in zip(names, refs, strict=True):
            setattr(space, key, ref)
        kernel(space)

    results = pl.pallas_call(
        body,
        in_specs=[i[2] for i in ins],
        out_specs=[o[3] for o in outs],
        out_shape=[jax.ShapeDtypeStruct(o[1], o[2]) for o in outs],
        scratch_shapes=[s[1] for s in scratch],
        compiler_params=pltpu.CompilerParams(
            collective_id=collective, has_side_effects=True, vmem_limit_bytes=limit * MIB
        ),
        name=name,
    )(*[i[1] for i in ins])
    return dict(zip([o[0] for o in outs], results))


ANY = pl.BlockSpec(memory_space=pl.ANY)
VMEM = pl.BlockSpec(memory_space=pltpu.VMEM)


class Load:
    def __init__(self, r, name):
        self.hbm, self.buf, self.sem = (getattr(r, name + part) for part in ("", "_buf", "_sem"))

    def copy(self, p):
        return pltpu.make_async_copy(self.hbm.at[p], self.buf.at[p], self.sem.at[p])

    def start(self):
        for p in range(self.hbm.shape[0]):
            self.copy(p).start()

    def wait(self, p):
        self.copy(p).wait()


class Drain:
    def __init__(self, r, name):
        self.hbm, self.buf, self.sem = (getattr(r, name + part) for part in ("", "_buf", "_sem"))

    def copy(self, p):
        slot = lax.rem(p, 2)
        return pltpu.make_async_copy(self.buf.at[slot], self.hbm.at[p], self.sem.at[slot])

    def slot(self, p):
        pl.when(p >= 2)(lambda: self.copy(p - 2).wait())
        return self.buf.at[lax.rem(p, 2)]

    def start(self, p):
        self.copy(p).start()

    def last(self):
        for p in range(max(self.hbm.shape[0] - 2, 0), self.hbm.shape[0]):
            self.copy(p).wait()


def stream_scratch(name, shape, dtype):
    return [
        (name + "_buf", pltpu.VMEM((2,) + tuple(shape), dtype)),
        (name + "_sem", pltpu.SemaphoreType.DMA((2,))),
    ]


class Links:
    def __init__(self, n):
        me = lax.axis_index("dp")
        self.n, self.nz, self.me = n, n // 4, me
        x, y = lax.rem(me, 2), lax.rem(me // 2, 2)
        self.z, self.column = me // 4, lax.rem(me, 4)
        self.x_peer, self.y_peer = me + 1 - 2 * x, me + 2 - 4 * y
        self.far_peer = self.x_peer + 2 - 4 * y
        self.z_pair = self.z + 1 - 2 * lax.rem(self.z, 2)
        self.pair_peer = self.z_pair * 4 + self.column

    def z_peer(self, k):
        return lax.rem(self.z + k + self.nz, self.nz) * 4 + self.column

    def block(self, k, column_of, z=None):
        return lax.rem((self.z if z is None else z) + k, self.nz) * 4 + lax.rem(column_of, 4)

    def peers(self):
        ids = [self.x_peer, self.y_peer] + [self.z_peer(k) for k in range(1, self.nz)]
        return [{"dp": i} for i in ids]

    def column_peer(self, k):
        return self.z * 4 + lax.rem(self.column + k + 4, 4)


def greet(peers):
    barrier = pltpu.get_barrier_semaphore()
    for peer in peers:
        pl.semaphore_signal(barrier, inc=1, device_id=peer, device_id_type=MESH)
    pl.semaphore_wait(barrier, len(peers))


def partner():
    return {"mp": 1 - lax.axis_index("mp")}


def cut(ref, blk, rows):
    return ref.at[pl.ds(pl.multiple_of(blk * rows, 16), rows)]


def remote(src, dst, send, recv, peer):
    return pltpu.make_async_remote_copy(
        src_ref=src,
        dst_ref=dst,
        send_sem=send,
        recv_sem=recv,
        device_id=peer,
        device_id_type=MESH,
    )


class Gather:
    def __init__(self, links, full, ss, rs):
        self.l, self.full, self.ss, self.rs = links, full, ss, rs

    def at(self, a, blk):
        ref, rows, lanes = self.full[a]
        rows = pl.ds(pl.multiple_of(blk * rows, 16), rows)
        return ref.at[rows] if lanes is None else ref.at[rows, pl.ds(*lanes)]

    def copy(self, a, role, k, blk, peer):
        at = self.at(a, blk)
        return remote(at, at, self.ss.at[a, role, k], self.rs.at[a, role, k], {"dp": peer})

    def put(self, a, value):
        self.at(a, self.l.me)[...] = value

    def own(self, a):
        l = self.l
        for k in range(1, l.nz):
            self.copy(a, 0, k, l.me, l.z_peer(-k)).start()
        self.copy(a, 1, 0, l.me, l.x_peer).start()
        self.copy(a, 2, 0, l.me, l.y_peer).start()

    def along(self, a):
        l = self.l
        for k in range(1, l.nz):
            blk = l.block(k, l.me)
            self.copy(a, 0, k, blk, l.x_peer).wait_recv()
            self.copy(a, 1, k, blk, l.x_peer).start()
            self.copy(a, 2, k, blk, l.y_peer).start()

    def across(self, a):
        l = self.l
        for k in range(0, l.nz, 2):
            role, source, target = (1, l.x_peer, l.y_peer) if k % 4 == 0 else (2, l.y_peer, l.x_peer)
            blk = l.block(k, source)
            self.copy(a, role, k, blk, source).wait_recv()
            self.copy(a, 3, k, blk, target).start()

    def share(self, a):
        l = self.l
        for k in range(0, l.nz, 2):
            blk = l.block(k, l.far_peer)
            self.copy(a, 3, k, blk, l.x_peer).wait_recv()
            self.copy(a, 4, k, blk, l.pair_peer).start()

    def arrived(self, a):
        l = self.l
        for k in range(l.nz):
            if k % 4 != 0:
                self.copy(a, 1, k, l.block(k, l.x_peer), l.x_peer).wait_recv()
            if k % 4 != 2:
                self.copy(a, 2, k, l.block(k, l.y_peer), l.y_peer).wait_recv()
            if k % 2 == 0:
                self.copy(a, 4, k, l.block(k, l.far_peer, l.z_pair), l.pair_peer).wait_recv()

    def sent(self, a):
        l = self.l
        for k in range(l.nz):
            roles = (0,) * (k > 0) + (1, 2) + (3, 4) * (k % 2 == 0)
            for role in roles:
                self.copy(a, role, k, l.me, l.x_peer).wait_send()


class Scatter:
    def __init__(self, links, grads, bufs, ss, rs):
        self.l, self.grads, self.bufs, self.ss, self.rs = links, grads, bufs, ss, rs

    def part(self, a, blk):
        ref, rows = self.grads[a]
        return cut(ref, blk, rows)

    def read(self, a, blk):
        ref, rows = self.grads[a]
        return ref[pl.ds(pl.multiple_of(blk * rows, 16), rows), :].astype(F32)

    def copy(self, a, role, k, src, slot, peer):
        dst = self.bufs[a].at[slot, k]
        return remote(src, dst, self.ss.at[a, role, k], self.rs.at[a, role, k], {"dp": peer})

    def arrive(self, a, role, k, slot):
        self.copy(a, role, k, self.part(a, 0), slot, self.l.x_peer).wait_recv()

    def far(self, a):
        l = self.l
        for k in range(l.nz):
            peer = l.y_peer if k % 2 == 0 else l.x_peer
            self.copy(a, 0, k, self.part(a, l.block(k, l.far_peer)), 0, peer).start()

    def plain(self, a):
        l = self.l
        for k in range(l.nz):
            if k % 2 == 1:
                self.copy(a, 1, k, self.part(a, l.block(k, l.x_peer)), 1, l.x_peer).start()
            else:
                self.copy(a, 2, k, self.part(a, l.block(k, l.y_peer)), 2, l.y_peer).start()

    def near(self, a):
        l = self.l
        for k in range(l.nz):
            self.arrive(a, 0, k, 0)
            role, peer = (1, l.x_peer) if k % 2 == 0 else (2, l.y_peer)
            mine = self.read(a, l.block(k, peer)) + self.bufs[a][0, k].astype(F32)
            self.bufs[a][0, k] = mine.astype(BF)
            self.copy(a, role, k, self.bufs[a].at[0, k], role, peer).start()

    def along(self, a, kept):
        l = self.l
        for k in list(range(1, l.nz)) + [0]:
            self.arrive(a, 1, k, 1)
            self.arrive(a, 2, k, 2)
            mine = (
                self.read(a, l.block(k, l.me))
                + self.bufs[a][1, k].astype(F32)
                + self.bufs[a][2, k].astype(F32)
            )
            if k == 0:
                kept[...] = mine
            else:
                self.bufs[a][1, k] = mine.astype(BF)
                self.copy(a, 3, k, self.bufs[a].at[1, k], 3, l.z_peer(k)).start()

    def total(self, a, kept):
        total = kept[...]
        for k in range(1, self.l.nz):
            self.arrive(a, 3, k, 3)
            total += self.bufs[a][3, k].astype(F32)
        kept[...] = total

    def sent(self, a):
        for k in range(self.l.nz):
            for role in (0, 1, 2) + (3,) * (k > 0):
                self.copy(a, role, k, self.part(a, 0), 0, self.l.x_peer).wait_send()


LAG = 2
SLOTS = 4


class Swap:
    def __init__(self, mine, theirs, ss, rs):
        self.mine, self.theirs, self.ss, self.rs = mine, theirs, ss, rs

    def copy(self, slot):
        return remote(
            self.mine.at[slot], self.theirs.at[slot], self.ss.at[slot], self.rs.at[slot], partner()
        )

    def put(self, p, value):
        self.mine[lax.rem(p, SLOTS)] = value.astype(BF)

    def send(self, p):
        self.copy(lax.rem(p, SLOTS)).start()

    def wait(self, p):
        self.copy(lax.rem(p, SLOTS)).wait()

    def rows(self, p, at):
        slot = lax.rem(p, SLOTS)
        return self.mine[slot, at].astype(F32) + self.theirs[slot, at].astype(F32)


def swap_scratch(name, d):
    return [
        (name + "_mine", pltpu.VMEM((SLOTS, ROWS, d), BF)),
        (name + "_theirs", pltpu.VMEM((SLOTS, ROWS, d), BF)),
        (name + "_ss", pltpu.SemaphoreType.DMA((SLOTS,))),
        (name + "_rs", pltpu.SemaphoreType.DMA((SLOTS,))),
    ]


def swap_of(r, name):
    return Swap(*(getattr(r, name + part) for part in ("_mine", "_theirs", "_ss", "_rs")))


class Spread:
    def __init__(self, links, own, z_slots, xy_slots, mp_slot, ss, rs):
        self.l, self.own, self.z_slots, self.xy_slots = links, own, z_slots, xy_slots
        self.mp_slot = mp_slot
        self.ss, self.rs = ss, rs

    def copy(self, stage, k, src, dst, peer):
        return remote(src, dst, self.ss.at[stage, k], self.rs.at[stage, k], {"dp": peer})

    def along(self):
        l = self.l
        self.z_slots[l.z] = self.own[...]
        for k in range(1, l.nz):
            self.copy(0, k, self.own, self.z_slots.at[l.z], l.z_peer(k)).start()

    def across(self):
        l = self.l
        for k in range(1, l.nz):
            self.copy(0, k, self.own, self.z_slots.at[lax.rem(l.z - k + l.nz, l.nz)], l.z_peer(k)).wait()
        total = self.z_slots[0]
        for k in range(1, l.nz):
            total += self.z_slots[k]
        self.own[...] = total
        self.xy_slots[l.column] = total
        for k in range(1, 4):
            self.copy(1, k, self.own, self.xy_slots.at[l.column], l.column_peer(k)).start()

    def over(self):
        l = self.l
        for k in range(1, 4):
            self.copy(1, k, self.own, self.xy_slots.at[lax.rem(l.column - k + 4, 4)], l.column_peer(k)).wait()
        total = self.xy_slots[0]
        for k in range(1, 4):
            total += self.xy_slots[k]
        self.own[...] = total
        self.pair().start()

    def pair(self):
        return remote(self.own, self.mp_slot, self.ss.at[1, 0], self.rs.at[1, 0], partner())

    def total(self, split):
        self.pair().wait()
        own, other = self.own[...], self.mp_slot[...]
        row = lax.broadcasted_iota(jnp.int32, own.shape, 0)
        return jnp.where(row >= split, own + other, own)


def every(step, actions):
    for at, what, argument in actions:
        pl.when(step == at)(partial(what, argument))


gelu_root = math.sqrt(2.0 / math.pi)
gelu_cube = 0.044715
WINDOW = 272


STRIP = 32


def strips(step=STRIP):
    return [slice(i, i + step) for i in range(0, ROWS, step)]


def inverse_rms(v):
    return lax.rsqrt(jnp.mean(v * v, axis=-1, keepdims=True) + norm_eps)


def window_start(p, total):
    return min(p * PLEN // 16 * 16, total - WINDOW)


def align(source, target, windows, sems, passages):
    total = source.shape[0]

    def fetch(p):
        return pltpu.make_async_copy(
            source.at[pl.ds(window_start(p, total), WINDOW)], windows.at[p % 2], sems.at[p % 2]
        )

    def start():
        fetch(0).start()
        fetch(1).start()

    def move(first, last):
        for p in range(first, last):
            fetch(p).wait()
            off = p * PLEN - window_start(p, total)
            rows = windows[p % 2].astype(F32)[off : off + PLEN]
            pad = jnp.zeros((ROWS - PLEN, rows.shape[1]), F32)
            target[p] = jnp.concatenate([rows, pad], axis=0).astype(BF)
            if p + 2 < passages:
                fetch(p + 2).start()

    return start, move


def loop(first, last, body):
    lax.fori_loop(first, last, lambda p, carry: (body(p), carry)[1], 0)


PAIR = 2 * DH


def low_lanes(shape):
    return lax.broadcasted_iota(jnp.int32, shape, 1) < DH


def of_head(h, pair):
    low = low_lanes(pair.shape)
    zero = jnp.zeros_like(pair)
    return jnp.where(low, pair, zero) if h % 2 == 0 else jnp.where(low, zero, pair)


def either(first, second):
    return jnp.where(low_lanes(first.shape), first, second)


def forward_kernel(n, passages, heads, direct, r):
    width = heads * DH
    count = passages
    pair, back_in = (swap_of(r, name) for name in ("pair", "in"))
    if direct:
        links = Links(n)
        rows_o = r.wo_wide.shape[0] // n
        full = [(r.wi, r.wi.shape[0] // n, None), (r.wo_wide, rows_o, None)]
        full += [(w, w.shape[0] // n, None) for w in (r.we_a, r.wr_a, r.we_b, r.wr_b)]
        gather = Gather(links, full, r.g_ss, r.g_rs)
        grads = [(g, g.shape[0] // n) for g in (r.stage_r, r.stage_e)]
        kept = [r.sum_r, r.sum_e]
        sums = Scatter(links, grads, [r.buf_r, r.buf_e], r.s_ss, r.s_rs)
    tok_start, tok_move = align(r.tokens, r.tok, r.window, r.window_sem, passages)
    cot_start, cot_move = align(r.cotangent, r.cot, r.window, r.window_sem, passages)
    half = passages // 2
    proj, probs, normed_out, ctx = (Drain(r, name) for name in ("proj", "probs", "normed", "ctx"))
    layer, hidden_grad = (Drain(r, name) for name in ("layer", "hidden_grad"))

    def local(src, dst, i):
        return pltpu.make_async_copy(src, dst, r.out_sem.at[i])

    local(r.buckets.at[0], r.bucket_rows, 5).start()
    tok_start()
    if direct:
        gather.put(0, jnp.concatenate([r.own_i[c] for c in range(3)], axis=1).astype(BF))
        pad = jnp.zeros((rows_o - r.own_o.shape[0], r.own_o.shape[1]), F32)
        gather.put(1, jnp.concatenate([r.own_o[...], pad], axis=0).astype(BF))
        greet(links.peers() + [partner()])
        gather.own(0)
        gather.own(1)
        gather.put(2, r.own_e[0])
        gather.put(3, r.own_r[: full[3][1]].astype(BF))
        gather.put(4, r.own_e[1])
        gather.put(5, r.own_r[full[3][1] :].astype(BF))
    else:
        greet([partner()])
    tok_move(0, half)
    if direct:
        gather.along(0)
        gather.own(2)
    tok_move(half, passages)
    local(r.tok, r.tok_out, 0).start()
    cot_start()
    if direct:
        gather.across(0)
        gather.along(1)
    cot_move(0, half)
    if direct:
        gather.share(0)
        gather.own(3)
        gather.across(1)
    cot_move(half, passages)
    for h in range(heads):
        line = dot_exact(r.table[h : h + 1, :], r.onehot[...])
        rows = jnp.broadcast_to(line, (ROWS, 2 * ROWS))
        r.bias[h] = pltpu.roll(rows, 0, 1, stride=1, stride_axis=0)[:, :ROWS]
    r.gain_grad[...] = jnp.zeros_like(r.gain_grad)

    def normalise(p):
        for at in strips():
            x = r.tok[p, at].astype(F32)
            r.out_sum[p, at] = x * inverse_rms(x) * r.gains[0:1, :]

    loop(0, count, normalise)
    local(r.buckets.at[0], r.bucket_rows, 5).wait()
    if direct:
        gather.share(1)
        gather.own(4)
        gather.arrived(0)

    def lanes(c, j):
        return slice(c * width + j * PAIR, c * width + (j + 1) * PAIR)

    def settle(p):
        pair.wait(p)
        for at in strips():
            r.hidden[p, at] = r.tok[p, at].astype(F32) + pair.rows(p, at)

    def attend(p):
        normed = r.out_sum[p].astype(BF)
        normed_slot, proj_slot, probs_slot, ctx_slot = (
            stream.slot(p) for stream in (normed_out, proj, probs, ctx)
        )
        normed_slot[...] = normed
        proj_slot[...] = dot(normed, r.wi[...]).astype(BF)
        valid = r.bucket_rows[pl.ds(p, 1), :] < BUCKETS
        masked = jnp.concatenate(
            [jnp.where(valid, 0.0, masked_score), jnp.full((1, ROWS - PLEN), masked_score, F32)], axis=1
        )
        pairs = [[proj_slot[:, lanes(c, j)] for c in range(3)] for j in range(heads // 2)]
        products = [dot(of_head(h, pairs[h // 2][0]), pairs[h // 2][1], 1, 1) for h in range(heads)]
        weighted = []
        for h in range(heads):
            parts = []
            for at in strips(64):
                sc = products[h][at] + r.bias[h, at] + masked
                e_ = jnp.exp(sc - jnp.max(sc, axis=-1, keepdims=True))
                parts.append((e_ * (1.0 / jnp.sum(e_, axis=-1, keepdims=True))).astype(BF))
                probs_slot[h, at] = parts[-1]
            weighted.append(jnp.concatenate(parts, axis=0))
        results = [dot(weighted[h], pairs[h // 2][2]) for h in range(heads)]
        for j in range(heads // 2):
            ctx_slot[:, lanes(0, j)] = either(results[2 * j], results[2 * j + 1]).astype(BF)
        if direct:

            @pl.when(p == 0)
            def _():
                gather.arrived(1)
                rows = r.own_o.shape[0]
                wide = r.acc_r
                for d in range(n):
                    block = r.wo_wide[d * rows_o : (d + 1) * rows_o, :].astype(F32)
                    wide[d * rows : (d + 1) * rows, :] = block[:rows]
                r.wo[...] = wide[: n * rows, :].astype(BF)

            every(p, (
                (1, gather.along, 2), (1, gather.own, 5), (2, gather.across, 2), (2, gather.along, 3),
                (3, gather.share, 2), (4, gather.across, 3), (4, gather.along, 4), (5, gather.share, 3),
                (6, gather.across, 4), (6, gather.along, 5), (7, gather.share, 4),
            ))
        pair.put(p, dot(ctx_slot[...], r.wo[...]))
        pl.when(p >= LAG)(lambda: settle(p - LAG))
        pair.send(p)
        for stream in (normed_out, proj, probs, ctx):
            stream.start(p)

    loop(0, count, attend)

    if direct:
        gather.across(5)
        gather.arrived(2)
        gather.arrived(3)
        local(r.wi, r.wi_out, 1).start()
        local(r.wo, r.wo_out, 2).start()

    def clear():
        r.acc_r[...] = jnp.zeros_like(r.acc_r)
        r.acc_e[...] = jnp.zeros_like(r.acc_e)

    def normed_two(p):
        parts = []
        for at in strips():
            h = r.hidden[p, at]
            parts.append((h * inverse_rms(h) * r.gains[1:2, :]).astype(BF))
        return jnp.concatenate(parts, axis=0)

    def inner_part(normed, c, we, wr):
        u_all, in_all = dot(normed, we[...]), dot(c, wr[...], 1, 1)
        acts, backs = [], []
        for at in strips():
            u = u_all[at]
            square = u * u
            t = jnp.tanh(u * (gelu_root + (gelu_root * gelu_cube) * square))
            half = 0.5 * (1.0 + t)
            acts.append((u * half).astype(BF))
            slope = half + (0.5 * u) * (1.0 - t * t) * (
                gelu_root + (3.0 * gelu_root * gelu_cube) * square
            )
            backs.append((in_all[at] * slope).astype(BF))
        return jnp.concatenate(acts, axis=0), jnp.concatenate(backs, axis=0)

    def outer_part(normed, c, act, back, we, wr):
        r.acc_r[...] += dot(act, c, 0, 0)
        r.acc_e[...] += dot(normed, back, 0, 0)
        return dot(act, wr[...]), dot(back, we[...], 1, 1)

    def first(p):
        normed, c = normed_two(p), r.cot[p]
        act, back = inner_part(normed, c, r.we_a, r.wr_a)
        r.out_sum[p], r.in_sum[p] = outer_part(normed, c, act, back, r.we_a, r.wr_a)

        @pl.when(p == 0)
        def _():
            for last in range(count - LAG, count):
                settle(last)

        if direct:
            every(p, ((1, gather.share, 5),))

    clear()
    loop(0, count, first)
    r.stage_r[...] = r.acc_r[...].astype(BF)
    r.stage_e[...] = r.acc_e[...].astype(BF)
    if direct:
        sums.far(0)
        sums.far(1)
        gather.arrived(4)
        gather.arrived(5)
    clear()

    def finish(last):
        layer_slot, grad_slot = layer.slot(last), hidden_grad.slot(last)
        pair.wait(count + last)
        back_in.wait(last)
        gain_rows = jnp.zeros((1, r.gains.shape[1]), F32)
        for at in strips():
            h = r.hidden[last, at]
            layer_slot[at] = (h + pair.rows(count + last, at)).astype(BF)
            grad = back_in.rows(last, at)
            inv = inverse_rms(h)
            hr = h * inv
            gain_rows += jnp.sum(grad * hr, axis=0, keepdims=True)
            zed = r.gains[1:2, :] * grad
            inner = jnp.mean(zed * hr, axis=-1, keepdims=True)
            grad_slot[at] = r.cot[last, at].astype(F32) + inv * (zed - hr * inner)
        r.gain_grad[0:1, :] += gain_rows

    def second(p, with_finish=True):
        normed, c = normed_two(p), r.cot[p]
        act, back = inner_part(normed, c, r.we_b, r.wr_b)
        if with_finish:
            finish(p - LAG)
        r_part, n_part = outer_part(normed, c, act, back, r.we_b, r.wr_b)
        pair.put(count + p, r.out_sum[p] + r_part)
        back_in.put(p, r.in_sum[p] + n_part)
        pair.send(count + p)
        back_in.send(p)
        if with_finish:
            for stream in (layer, hidden_grad):
                stream.start(p - LAG)
            if direct:
                every(p, ((2, sums.near, 0), (3, sums.near, 1)))
                for a in range(2):
                    pl.when(p == 6 + a)(partial(sums.along, a, kept[a]))

    loop(0, LAG, lambda p: second(p, False))
    if direct:
        sums.plain(0)
        sums.plain(1)
    loop(LAG, count, second)
    stage_rb, stage_eb = (r.wr_a, r.we_a) if direct else (r.stage_rb, r.stage_eb)
    if direct:
        gather.sent(2)
        gather.sent(3)
    stage_rb[...] = r.acc_r[...].astype(BF)
    stage_eb[...] = r.acc_e[...].astype(BF)
    local(stage_rb, r.grad_r, 3).start()
    local(stage_eb, r.grad_e, 4).start()
    for p in range(count - LAG, count):
        finish(p)
        for stream in (layer, hidden_grad):
            stream.start(p)
    if direct:
        for a in range(2):
            sums.total(a, kept[a])
        for a in (0, 1, 4, 5):
            gather.sent(a)
        for a in range(2):
            sums.sent(a)
        local(r.wi, r.wi_out, 1).wait()
        local(r.wo, r.wo_out, 2).wait()
    local(r.tok, r.tok_out, 0).wait()
    local(stage_rb, r.grad_r, 3).wait()
    local(stage_eb, r.grad_e, 4).wait()
    for stream in (normed_out, proj, probs, ctx, layer, hidden_grad):
        stream.last()


def dot_exact(a, b):
    return lax.dot_general(
        a, b, (((1,), (1,)), ((), ())), precision=lax.Precision.HIGHEST, preferred_element_type=F32
    )


def forward(n, passages, heads, direct, tokens, cotangent, buckets, gains, table, onehot, weights):
    d = tokens.shape[1]
    width = heads * DH
    ins = [("tokens", tokens, ANY), ("cotangent", cotangent, ANY)]
    ins += [("buckets", buckets, ANY)]
    ins += [(k, v, VMEM) for k, v in (("gains", gains), ("table", table), ("onehot", onehot))]
    ins += [(k, v, VMEM) for k, v in weights.items()]
    if direct:
        part = weights["own_r"].shape[0] // 2 * n
    else:
        part = weights["wr_a"].shape[0]
    streams = {
        "proj": ((ROWS, 3 * width), BF),
        "probs": ((heads, ROWS, ROWS), BF),
        "normed": ((ROWS, d), BF),
        "ctx": ((ROWS, width), BF),
        "layer": ((ROWS, d), BF),
        "hidden_grad": ((ROWS, d), F32),
    }
    outs = [(k, (passages,) + shape, dtype, ANY) for k, (shape, dtype) in streams.items()]
    outs += [
        ("tok_out", (passages, ROWS, d), BF, ANY),
        ("grad_r", (part, d), BF, ANY),
        ("grad_e", (d, part), BF, ANY),
        ("gain_grad", (8, d), F32, VMEM),
    ]
    scratch = [
        ("tok", pltpu.VMEM((passages, ROWS, d), BF)),
        ("cot", pltpu.VMEM((passages, ROWS, d), BF)),
        ("window", pltpu.VMEM((2, WINDOW, d), BF)),
        ("window_sem", pltpu.SemaphoreType.DMA((2,))),
        ("bucket_rows", pltpu.VMEM(buckets.shape[1:], buckets.dtype)),
        ("out_sem", pltpu.SemaphoreType.DMA((6,))),
        ("bias", pltpu.VMEM((heads, ROWS, ROWS), F32)),
        ("hidden", pltpu.VMEM((passages, ROWS, d), F32)),
        ("out_sum", pltpu.VMEM((passages, ROWS, d), F32)),
        ("in_sum", pltpu.VMEM((passages, ROWS, d), F32)),
        ("acc_r", pltpu.VMEM((part, d), F32)),
        ("acc_e", pltpu.VMEM((d, part), F32)),
    ]
    for k, (shape, dtype) in streams.items():
        scratch += stream_scratch(k, shape, dtype)
    for name in ("pair", "in"):
        scratch += swap_scratch(name, d)
    stage = [("stage_r", (part, d)), ("stage_e", (d, part))]
    if direct:
        nz = n // 4
        padded = weights["own_o"].shape[0]
        padded += -padded % 16
        outs += [("wi_out", (d, 3 * width), BF, ANY), ("wo_out", (width, d), BF, ANY)]
        for key, shape in (("sum_r", (part // n, d)), ("sum_e", (d // n, part))):
            outs.append((key, shape, F32, VMEM))
        scratch += [(k, pltpu.VMEM(shape, BF)) for k, shape in stage]
        shapes = {"wi": (d, 3 * width), "wo": (width, d), "wo_wide": (n * padded, d)}
        for half in "ab":
            shapes["we_" + half], shapes["wr_" + half] = (d, part), (part, d)
        scratch += [(key, pltpu.VMEM(shape, BF)) for key, shape in shapes.items()]
        scratch += [
            ("buf_r", pltpu.VMEM((4, nz, part // n, d), BF)),
            ("buf_e", pltpu.VMEM((4, nz, d // n, part), BF)),
            ("g_ss", pltpu.SemaphoreType.DMA((6, 5, nz))),
            ("g_rs", pltpu.SemaphoreType.DMA((6, 5, nz))),
            ("s_ss", pltpu.SemaphoreType.DMA((2, 4, nz))),
            ("s_rs", pltpu.SemaphoreType.DMA((2, 4, nz))),
        ]
    else:
        outs += [(k, shape, BF, VMEM) for k, shape in stage]
        scratch += [("stage_rb", pltpu.VMEM((part, d), BF)), ("stage_eb", pltpu.VMEM((d, part), BF))]
    kernel = partial(forward_kernel, n, passages, heads, direct)
    return run(kernel, ins, outs, scratch, 1, 63, "forward")


def back_kernel(n, passages, heads, direct, r):
    width = heads * DH
    count = passages
    swap = swap_of(r, "in")
    if direct:
        links = Links(n)
        refs = [r.grad_r, r.grad_e, r.stage_o, r.stage_v, r.stage_qk]
        grads = [(g, g.shape[0] // n) for g in refs]
        names = ["r", "e", "o", "v", "qk"]
        bufs = [getattr(r, "buf_" + k) for k in names]
        kept = [getattr(r, "sum_" + k) for k in names]
        sums = Scatter(links, grads, bufs, r.s_ss, r.s_rs)
        wide = Spread(links, r.wide, r.wide_z, r.wide_xy, r.wide_mp, r.w_ss, r.w_rs)
    ctx, normed, probs, proj, tok, hidden_grad = (
        Load(r, name) for name in ("ctx", "normed", "probs", "proj", "tok", "hidden_grad")
    )
    input_grad = Drain(r, "input_grad")

    for p in range(count):
        for stream in (hidden_grad, ctx, probs, normed):
            stream.copy(p).start()
    for stream in (proj, tok):
        stream.start()
    if direct:
        greet(links.peers() + [{"dp": links.far_peer}, partner()])
        sums.far(0)
        sums.far(1)
    else:
        greet([partner()])
    r.acc_o[...] = jnp.zeros_like(r.acc_o)
    r.acc_s[...] = jnp.zeros_like(r.acc_s)
    r.acc_v[...] = jnp.zeros_like(r.acc_v)
    r.acc_qk[...] = jnp.zeros_like(r.acc_qk)

    def lanes(c, j):
        return slice(c * width + j * PAIR, c * width + (j + 1) * PAIR)

    def values(p):
        for stream in (hidden_grad, ctx, probs, normed):
            stream.wait(p)
        top = hidden_grad.buf[p].astype(BF)
        r.acc_o[...] += dot(ctx.buf[p], top, 0, 0)
        dctx = dot(top, r.wo[...], 1, 1).astype(BF)
        r.dctx[p] = dctx
        results = [dot(probs.buf[p, h], dctx[:, lanes(0, h // 2)], 0, 0) for h in range(heads)]
        dv = [either(results[2 * j], results[2 * j + 1]) for j in range(heads // 2)]
        dv = jnp.concatenate(dv, axis=1).astype(BF)
        r.dproj[p, :, 2 * width :] = dv
        r.acc_v[...] += dot(normed.buf[p], dv, 0, 0)
        if direct:
            every(p, (
                (2, sums.plain, 0), (3, sums.plain, 1), (5, sums.near, 0), (7, sums.near, 1),
            ))

    loop(0, count, values)
    blocks = n if direct else 1
    rows = r.acc_o.shape[0] // blocks
    padded = r.stage_o.shape[0] // blocks
    for b in range(blocks):
        part = r.acc_o[b * rows : (b + 1) * rows, :]
        if padded > rows:
            part = jnp.concatenate([part, jnp.zeros((padded - rows, part.shape[1]), F32)], axis=0)
        r.stage_o[b * padded : (b + 1) * padded, :] = part.astype(BF)
    r.stage_v[...] = r.acc_v[...].astype(BF)
    if direct:
        sums.far(2)
        sums.far(3)

    def scores(p):
        proj.wait(p)
        pairs = [[proj.buf[p, :, lanes(c, j)] for c in range(3)] for j in range(heads // 2)]
        products = [
            dot(of_head(h, r.dctx[p, :, lanes(0, h // 2)]), pairs[h // 2][2], 1, 1) for h in range(heads)
        ]
        ds = []
        for h in range(heads):
            parts = []
            for rows in strips(64):
                a = probs.buf[p, h, rows].astype(F32)
                dp = products[h][rows]
                centre = jnp.sum(a * dp, axis=-1, keepdims=True)
                parts.append((a * (dp - centre)).astype(BF))
                r.acc_s[h, rows] += parts[-1].astype(F32)
            ds.append(jnp.concatenate(parts, axis=0))
        dq = [dot(ds[h], pairs[h // 2][1]) for h in range(heads)]
        dk = [dot(ds[h], pairs[h // 2][0], 0, 0) for h in range(heads)]
        for j in range(heads // 2):
            r.dproj[p, :, lanes(0, j)] = either(dq[2 * j], dq[2 * j + 1]).astype(BF)
            r.dproj[p, :, lanes(1, j)] = either(dk[2 * j], dk[2 * j + 1]).astype(BF)
        r.acc_qk[...] += dot(normed.buf[p], r.dproj[p, :, : 2 * width], 0, 0)
        if direct:
            every(p, ((0, sums.plain, 2), (0, sums.plain, 3)))
            for a, at in ((0, 1), (1, 2), (2, 5), (3, 6)):
                pl.when(p == at)(partial(sums.along, a, kept[a]))
            every(p, ((3, sums.near, 2), (4, sums.near, 3)))

    loop(0, count, scores)
    r.stage_qk[...] = r.acc_qk[...].astype(BF)
    if direct:
        sums.far(4)
    terms = jnp.sum(r.acc_v[...] * r.wi[:, 2 * width :].astype(F32), axis=1, keepdims=True)
    terms += jnp.sum(r.acc_qk[...] * r.wi[:, : 2 * width].astype(F32), axis=1, keepdims=True)
    r.wide[...] = jnp.zeros_like(r.wide)
    r.wide[heads : heads + 1, :] = 0.5 * r.gain_two[0:1, :]
    r.wide[heads + 1 : heads + 2, :] = terms.T / r.gains[0:1, :]
    for h in range(heads):
        lines = jnp.concatenate([r.acc_s[h], jnp.zeros((ROWS, ROWS), F32)], axis=1)
        while lines.shape[0] > 1:
            half = lines.shape[0] // 2
            lines = lines[:half] + pltpu.roll(lines[half:], 2 * ROWS - half, 1)
        r.wide[h : h + 1, : 2 * ROWS] = lines
    if direct:
        wide.along()
        sums.plain(4)

    def finish(last):
        tok.wait(last)
        slot = input_grad.slot(last)
        swap.wait(last)
        for at in strips():
            x = tok.buf[last, at].astype(F32)
            inv = inverse_rms(x)
            xr = x * inv
            zed = r.gains[0:1, :] * swap.rows(last, at)
            inner = jnp.mean(zed * xr, axis=-1, keepdims=True)
            slot[at] = hidden_grad.buf[last, at] + inv * (zed - xr * inner)

    def inputs(t, with_finish=True):
        terms = dot(r.dproj[t, :, : 2 * width], r.wi[:, : 2 * width], 1, 1)
        if with_finish:
            finish(t - LAG)
        terms += dot(r.dproj[t, :, 2 * width :], r.wi[:, 2 * width :], 1, 1)
        swap.put(t, terms)
        swap.send(t)
        if with_finish:
            input_grad.start(t - LAG)
            if direct:
                every(t, ((4, sums.near, 4),))
                pl.when(t == 2)(wide.across)
                pl.when(t == 5)(wide.over)

    loop(0, LAG, lambda t: inputs(t, False))
    loop(LAG, count, inputs)
    if direct:
        for a in range(4):
            sums.total(a, kept[a])
        sums.along(4, kept[4])
    for p in range(count - LAG, count):
        finish(p)
        input_grad.start(p)
    if direct:
        r.wide_sum[...] = wide.total(heads)
        sums.total(4, kept[4])
        for a in range(5):
            sums.sent(a)
    else:
        r.wide_sum[...] = r.wide[...]
    input_grad.last()


def back(n, passages, heads, direct, f, gains, wi, wo):
    d = gains.shape[1]
    width = heads * DH
    streams = {
        "ctx": ((ROWS, width), BF),
        "normed": ((ROWS, d), BF),
        "probs": ((heads, ROWS, ROWS), BF),
        "proj": ((ROWS, 3 * width), BF),
        "tok": ((ROWS, d), BF),
        "hidden_grad": ((ROWS, d), F32),
    }
    ins = [(k, f["tok_out" if k == "tok" else k], ANY) for k in streams]
    fixed = [("gains", gains), ("wi", wi), ("wo", wo), ("gain_two", f["gain_grad"])]
    outs = [
        ("input_grad", (passages, ROWS, d), F32, ANY),
        ("wide_sum", (8, d), F32, VMEM),
    ]
    scratch = [
        ("acc_qk", pltpu.VMEM((d, 2 * width), F32)),
        ("acc_v", pltpu.VMEM((d, width), F32)),
        ("acc_o", pltpu.VMEM((width, d), F32)),
        ("acc_s", pltpu.VMEM((heads, ROWS, ROWS), F32)),
        ("dctx", pltpu.VMEM((passages, ROWS, width), BF)),
        ("dproj", pltpu.VMEM((passages, ROWS, 3 * width), BF)),
        ("wide", pltpu.VMEM((8, d), F32)),
    ] + swap_scratch("in", d)
    for k, (shape, dtype) in streams.items():
        scratch.append((k + "_buf", pltpu.VMEM((passages,) + shape, dtype)))
        scratch.append((k + "_sem", pltpu.SemaphoreType.DMA((passages,))))
    scratch += stream_scratch("input_grad", (ROWS, d), F32)
    rows_o = width
    if direct:
        rows_o = width // n
        rows_o = (rows_o + -rows_o % 16) * n
    stage = [("stage_o", (rows_o, d)), ("stage_v", (d, width)), ("stage_qk", (d, 2 * width))]
    if direct:
        nz = n // 4
        fixed += [(k, f[k]) for k in ("grad_r", "grad_e")]
        scratch += [(k, pltpu.VMEM(shape, BF)) for k, shape in stage]
        blocks = {"r": f["grad_r"].shape, "e": f["grad_e"].shape}
        blocks.update({k[6:]: shape for k, shape in stage})
        for key, shape in blocks.items():
            shape = (shape[0] // n, shape[1])
            scratch.append(("buf_" + key, pltpu.VMEM((4, nz) + shape, BF)))
            outs.append(("sum_" + key, shape, F32, VMEM))
        scratch += [
            ("wide_z", pltpu.VMEM((nz, 8, d), F32)),
            ("wide_xy", pltpu.VMEM((4, 8, d), F32)),
            ("wide_mp", pltpu.VMEM((8, d), F32)),
            ("s_ss", pltpu.SemaphoreType.DMA((len(blocks), 4, nz))),
            ("s_rs", pltpu.SemaphoreType.DMA((len(blocks), 4, nz))),
            ("w_ss", pltpu.SemaphoreType.DMA((2, max(nz, 4)))),
            ("w_rs", pltpu.SemaphoreType.DMA((2, max(nz, 4)))),
        ]
    else:
        outs += [(k, shape, BF, VMEM) for k, shape in stage]
    ins += [(k, v, VMEM) for k, v in fixed]
    kernel = partial(back_kernel, n, passages, heads, direct)
    return run(kernel, ins, outs, scratch, 2, 63, "back")


def shards(
    n,
    tokens,
    cotangent,
    buckets,
    inward_master,
    inward_first,
    inward_second,
    outward_master,
    outward_first,
    outward_second,
    expand_master,
    expand_first,
    expand_second,
    reduce_master,
    reduce_first,
    reduce_second,
    gains_master,
    gains_first,
    gains_second,
    table_master,
    table_first,
    table_second,
):
    d = tokens.shape[1]
    passages = tokens.shape[0] // PLEN
    heads = inward_master.shape[2] // DH
    width = heads * DH
    rows_i, rows_e, rows_r = inward_master.shape[0], expand_master.shape[0], reduce_master.shape[0]
    units = expand_master.shape[1]
    direct = n % 8 == 0 and rows_i % 16 == 0 and rows_r % 32 == 0 and outward_master.shape[0] % 8 == 0

    def unit_halves(a):
        return a.reshape(rows_e, n, 2, units // (2 * n)).transpose(2, 0, 1, 3).reshape(2, rows_e, -1)

    def unit_order(a):
        return a.reshape(2, rows_e, n, units // (2 * n)).transpose(1, 2, 0, 3).reshape(rows_e, units)

    onehot = jnp.asarray(distance_onehot())
    bucket_rows = buckets.transpose(1, 0, 2)
    table_rows = table_master.T
    if direct:
        weights = {
            "own_i": inward_master.transpose(1, 0, 2),
            "own_o": outward_master,
            "own_e": unit_halves(expand_master.astype(BF)),
            "own_r": reduce_master,
        }
    else:
        masters = (inward_master.reshape(-1, 3 * width), outward_master, expand_master, reduce_master)
        wi, wo, we, wr = (
            lax.all_gather(w.astype(BF), "dp", axis=0, tiled=True) for w in masters
        )
        half = units // 2
        weights = {"wi": wi, "wo": wo}
        weights.update({"we_a": we[:, :half], "wr_a": wr[:half], "we_b": we[:, half:], "wr_b": wr[half:]})
    f = forward(
        n, passages, heads, direct, tokens, cotangent, bucket_rows, gains_master, table_rows, onehot, weights
    )
    if direct:
        wi, wo = f["wi_out"], f["wo_out"]
    b = back(n, passages, heads, direct, f, gains_master, wi, wo)

    def scatter(g):
        return lax.psum_scatter(g.astype(F32), "dp", scatter_dimension=0, tiled=True)

    if direct:
        inward_sum = jnp.concatenate([b["sum_qk"], b["sum_v"]], axis=1)
        outward_sum = b["sum_o"][: outward_master.shape[0]]
        expand_sum = unit_order(jnp.stack([f["sum_e"], b["sum_e"]]))
        reduce_sum = jnp.concatenate([f["sum_r"], b["sum_r"]], axis=0)
        wide_sum = b["wide_sum"]
    else:
        inward_sum = scatter(jnp.concatenate([b["stage_qk"], b["stage_v"]], axis=1))
        outward_sum = scatter(b["stage_o"])
        expand_sum = scatter(jnp.concatenate([f["stage_e"], f["grad_e"]], axis=1))
        reduce_sum = scatter(jnp.concatenate([f["stage_r"], f["grad_r"]], axis=0))
        wide_sum = lax.psum(b["wide_sum"], "dp")
        gains = lax.psum(wide_sum[heads : heads + 2], "mp")
        wide_sum = jnp.concatenate([wide_sum[:heads], gains], axis=0)
    inward_sum = inward_sum.reshape(inward_master.shape)
    gains_sum = jnp.concatenate([wide_sum[heads + 1 : heads + 2], wide_sum[heads : heads + 1]], axis=0)
    table_sum = lax.dot_general(
        onehot.T, wide_sum[:heads, : 2 * ROWS], (((1,), (1,)), ((), ())), precision=lax.Precision.HIGHEST
    )

    layer_out = f["layer"][:, :PLEN].reshape(tokens.shape)
    input_grad = b["input_grad"][:, :PLEN].reshape(tokens.shape)
    outputs = [layer_out, input_grad]
    for w, first_moment, second_moment, gradient, rate, copied in (
        (inward_master, inward_first, inward_second, inward_sum, rate_inward, True),
        (outward_master, outward_first, outward_second, outward_sum, rate_outward, True),
        (expand_master, expand_first, expand_second, expand_sum, rate_expand, True),
        (reduce_master, reduce_first, reduce_second, reduce_sum, rate_reduce, True),
        (gains_master, gains_first, gains_second, gains_sum, rate_gains, False),
        (table_master, table_first, table_second, table_sum, rate_table, False),
    ):
        new = adamw(w, first_moment, second_moment, gradient, rate)
        outputs += list(new)
        if copied:
            outputs.append(new[0].astype(BF))
    return tuple(outputs)


def solution(mesh):
    rows = P("dp", None)
    inward = P("dp", None, "mp")
    tall = P(("mp", "dp"), None)
    wide = P("dp", "mp")
    table = P(None, "mp")
    return jax.shard_map(
        partial(shards, mesh.shape["dp"]),
        mesh=mesh,
        in_specs=(rows, rows, P("dp", None, None))
        + (inward,) * 3
        + (tall,) * 3
        + (wide,) * 3
        + (tall,) * 3
        + (P(),) * 3
        + (table,) * 3,
        out_specs=(rows, rows)
        + (inward,) * 4
        + (tall,) * 4
        + (wide,) * 4
        + (tall,) * 4
        + (P(),) * 3
        + (table,) * 3,
        check_vma=False,
    )
```

```python
from functools import partial
import math

import jax
import jax.numpy as jnp
import numpy as np
from jax import lax
from jax.experimental import pallas as pl
from jax.experimental.pallas import tpu as pltpu
from jax.sharding import PartitionSpec as P

DH = 64
PLEN = 250
STEP = 5
ROWS = 256
BUCKETS = 32
SPAN = 128

MESH = pl.DeviceIdType.MESH
BF = jnp.bfloat16
F32 = jnp.float32
MIB = 2**20

norm_eps = 1e-06
masked_score = -1000000000.0
beta_first = 0.5
beta_second = 0.5
adam_eps = 1e-08
decay_rate = 0.01
rate_inward = 0.015
rate_outward = 0.3
rate_expand = 0.04
rate_reduce = 0.02
rate_gains = 0.5
rate_table = 0.5


def adamw(weight, first_moment, second, gradient, step_rate):
    new_first = beta_first * first_moment + (1.0 - beta_first) * gradient
    new_second = beta_second * second + (1.0 - beta_second) * gradient * gradient
    first_hat = new_first / (1.0 - beta_first**STEP)
    second_hat = new_second / (1.0 - beta_second**STEP)
    new_weight = weight - step_rate * (
        first_hat / (jnp.sqrt(second_hat) + adam_eps) + decay_rate * weight
    )
    return (new_weight, new_first, new_second)


def distance_onehot():
    span = 2 * ROWS
    relative = np.arange(span)
    relative = np.where(relative < ROWS, relative, relative - span)
    half = BUCKETS // 2
    exact = half // 2
    distance = np.abs(relative)
    far = np.full_like(distance, exact)
    for level in range(1, half - exact):
        far += distance >= math.ceil(exact * (SPAN / exact) ** (level / (half - exact)))
    bucket = np.where(relative > 0, half, 0) + np.where(distance < exact, distance, far)
    return (bucket[:, None] == np.arange(BUCKETS)[None]).astype(np.float32)


def dot(a, b, ca=1, cb=0):
    return lax.dot_general(a, b, (((ca,), (cb,)), ((), ())), preferred_element_type=F32)


class Refs:
    pass


def run(kernel, ins, outs, scratch, collective, limit, name):
    names = [i[0] for i in ins] + [o[0] for o in outs] + [s[0] for s in scratch]

    def body(*refs):
        space = Refs()
        for key, ref in zip(names, refs, strict=True):
            setattr(space, key, ref)
        kernel(space)

    results = pl.pallas_call(
        body,
        in_specs=[i[2] for i in ins],
        out_specs=[o[3] for o in outs],
        out_shape=[jax.ShapeDtypeStruct(o[1], o[2]) for o in outs],
        scratch_shapes=[s[1] for s in scratch],
        compiler_params=pltpu.CompilerParams(
            collective_id=collective, has_side_effects=collective is not None, vmem_limit_bytes=limit * MIB
        ),
        name=name,
    )(*[i[1] for i in ins])
    space = Refs()
    for out, result in zip(outs, results, strict=True):
        setattr(space, out[0], result)
    return space


ANY = pl.BlockSpec(memory_space=pl.ANY)
VMEM = pl.BlockSpec(memory_space=pltpu.VMEM)


class Load:
    def __init__(self, r, name):
        self.hbm, self.buf, self.sem = (getattr(r, name + part) for part in ("", "_buf", "_sem"))

    def copy(self, p):
        return pltpu.make_async_copy(self.hbm.at[p], self.buf.at[p], self.sem.at[p])

    def start(self):
        for p in range(self.hbm.shape[0]):
            self.copy(p).start()

    def wait(self, p):
        self.copy(p).wait()


class Drain:
    def __init__(self, r, name):
        self.hbm, self.buf, self.sem = (getattr(r, name + part) for part in ("", "_buf", "_sem"))

    def copy(self, p):
        slot = lax.rem(p, 2)
        return pltpu.make_async_copy(self.buf.at[slot], self.hbm.at[p], self.sem.at[slot])

    def slot(self, p):
        pl.when(p >= 2)(lambda: self.copy(p - 2).wait())
        return self.buf.at[lax.rem(p, 2)]

    def start(self, p):
        self.copy(p).start()

    def last(self):
        for p in range(max(self.hbm.shape[0] - 2, 0), self.hbm.shape[0]):
            self.copy(p).wait()


def stream_scratch(name, shape, dtype):
    return [
        (name + "_buf", pltpu.VMEM((2,) + tuple(shape), dtype)),
        (name + "_sem", pltpu.SemaphoreType.DMA((2,))),
    ]


class Links:
    def __init__(self, n):
        me = lax.axis_index("dp")
        self.n, self.nz, self.me = n, n // 4, me
        x, y = lax.rem(me, 2), lax.rem(me // 2, 2)
        self.z, self.column = me // 4, lax.rem(me, 4)
        self.x_peer, self.y_peer = me + 1 - 2 * x, me + 2 - 4 * y
        self.far_peer = self.x_peer + 2 - 4 * y
        self.z_pair = self.z + 1 - 2 * lax.rem(self.z, 2)
        self.pair_peer = self.z_pair * 4 + self.column

    def z_peer(self, k):
        return lax.rem(self.z + k + self.nz, self.nz) * 4 + self.column

    def block(self, k, column_of, z=None):
        return lax.rem((self.z if z is None else z) + k, self.nz) * 4 + lax.rem(column_of, 4)

    def peers(self):
        ids = [self.x_peer, self.y_peer] + [self.z_peer(k) for k in range(1, self.nz)]
        return [{"dp": i} for i in ids]

    def column_peer(self, k):
        return self.z * 4 + lax.rem(self.column + k + 4, 4)


def greet(peers):
    barrier = pltpu.get_barrier_semaphore()
    for peer in peers:
        pl.semaphore_signal(barrier, inc=1, device_id=peer, device_id_type=MESH)
    pl.semaphore_wait(barrier, len(peers))


def partner():
    return {"mp": 1 - lax.axis_index("mp")}


def cut(ref, blk, rows):
    return ref.at[pl.ds(pl.multiple_of(blk * rows, 16), rows)]


def remote(src, dst, send, recv, peer):
    return pltpu.make_async_remote_copy(
        src_ref=src,
        dst_ref=dst,
        send_sem=send,
        recv_sem=recv,
        device_id=peer,
        device_id_type=MESH,
    )


class Gather:
    def __init__(self, links, full, ss, rs):
        self.l, self.full, self.ss, self.rs = links, full, ss, rs

    def at(self, a, blk):
        ref, rows, lanes = self.full[a]
        rows = pl.ds(pl.multiple_of(blk * rows, 16), rows)
        return ref.at[rows] if lanes is None else ref.at[rows, pl.ds(*lanes)]

    def copy(self, a, role, k, blk, peer):
        at = self.at(a, blk)
        return remote(at, at, self.ss.at[a, role, k], self.rs.at[a, role, k], {"dp": peer})

    def put(self, a, value):
        self.at(a, self.l.me)[...] = value

    def own(self, a):
        l = self.l
        for k in range(1, l.nz):
            self.copy(a, 0, k, l.me, l.z_peer(-k)).start()
        self.copy(a, 1, 0, l.me, l.x_peer).start()
        self.copy(a, 2, 0, l.me, l.y_peer).start()

    def along(self, a):
        l = self.l
        for k in range(1, l.nz):
            blk = l.block(k, l.me)
            self.copy(a, 0, k, blk, l.x_peer).wait_recv()
            self.copy(a, 1, k, blk, l.x_peer).start()
            self.copy(a, 2, k, blk, l.y_peer).start()

    def across(self, a):
        l = self.l
        for k in range(0, l.nz, 2):
            role, source, target = (1, l.x_peer, l.y_peer) if k % 4 == 0 else (2, l.y_peer, l.x_peer)
            blk = l.block(k, source)
            self.copy(a, role, k, blk, source).wait_recv()
            self.copy(a, 3, k, blk, target).start()

    def share(self, a):
        l = self.l
        for k in range(0, l.nz, 2):
            blk = l.block(k, l.far_peer)
            self.copy(a, 3, k, blk, l.x_peer).wait_recv()
            self.copy(a, 4, k, blk, l.pair_peer).start()

    def arrived(self, a):
        l = self.l
        for k in range(l.nz):
            if k % 4 != 0:
                self.copy(a, 1, k, l.block(k, l.x_peer), l.x_peer).wait_recv()
            if k % 4 != 2:
                self.copy(a, 2, k, l.block(k, l.y_peer), l.y_peer).wait_recv()
            if k % 2 == 0:
                self.copy(a, 4, k, l.block(k, l.far_peer, l.z_pair), l.pair_peer).wait_recv()

    def sent(self, a):
        l = self.l
        for k in range(l.nz):
            roles = (0,) * (k > 0) + (1, 2) + (3, 4) * (k % 2 == 0)
            for role in roles:
                self.copy(a, role, k, l.me, l.x_peer).wait_send()


class Scatter:
    def __init__(self, links, grads, bufs, ss, rs):
        self.l, self.grads, self.bufs, self.ss, self.rs = links, grads, bufs, ss, rs

    def part(self, a, blk):
        ref, rows = self.grads[a]
        return cut(ref, blk, rows)

    def read(self, a, blk):
        ref, rows = self.grads[a]
        return ref[pl.ds(pl.multiple_of(blk * rows, 16), rows), :].astype(F32)

    def copy(self, a, role, k, src, slot, peer):
        dst = self.bufs[a].at[slot, k]
        return remote(src, dst, self.ss.at[a, role, k], self.rs.at[a, role, k], {"dp": peer})

    def arrive(self, a, role, k, slot):
        self.copy(a, role, k, self.part(a, 0), slot, self.l.x_peer).wait_recv()

    def far(self, a):
        l = self.l
        for k in range(l.nz):
            peer = l.y_peer if k % 2 == 0 else l.x_peer
            self.copy(a, 0, k, self.part(a, l.block(k, l.far_peer)), 0, peer).start()

    def plain(self, a):
        l = self.l
        for k in range(l.nz):
            if k % 2 == 1:
                self.copy(a, 1, k, self.part(a, l.block(k, l.x_peer)), 1, l.x_peer).start()
            else:
                self.copy(a, 2, k, self.part(a, l.block(k, l.y_peer)), 2, l.y_peer).start()

    def near(self, a):
        l = self.l
        for k in range(l.nz):
            self.arrive(a, 0, k, 0)
            role, peer = (1, l.x_peer) if k % 2 == 0 else (2, l.y_peer)
            mine = self.read(a, l.block(k, peer)) + self.bufs[a][0, k].astype(F32)
            self.bufs[a][0, k] = mine.astype(BF)
            self.copy(a, role, k, self.bufs[a].at[0, k], role, peer).start()

    def along(self, a, kept):
        l = self.l
        for k in list(range(1, l.nz)) + [0]:
            self.arrive(a, 1, k, 1)
            self.arrive(a, 2, k, 2)
            mine = (
                self.read(a, l.block(k, l.me))
                + self.bufs[a][1, k].astype(F32)
                + self.bufs[a][2, k].astype(F32)
            )
            if k == 0:
                kept[...] = mine
            else:
                self.bufs[a][1, k] = mine.astype(BF)
                self.copy(a, 3, k, self.bufs[a].at[1, k], 3, l.z_peer(k)).start()

    def total(self, a, kept):
        total = kept[...]
        for k in range(1, self.l.nz):
            self.arrive(a, 3, k, 3)
            total += self.bufs[a][3, k].astype(F32)
        kept[...] = total

    def sent(self, a):
        for k in range(self.l.nz):
            for role in (0, 1, 2) + (3,) * (k > 0):
                self.copy(a, role, k, self.part(a, 0), 0, self.l.x_peer).wait_send()


LAG = 2
SLOTS = 4


class Swap:
    def __init__(self, mine, theirs, ss, rs):
        self.mine, self.theirs, self.ss, self.rs = mine, theirs, ss, rs

    def copy(self, slot):
        return remote(
            self.mine.at[slot], self.theirs.at[slot], self.ss.at[slot], self.rs.at[slot], partner()
        )

    def put(self, p, value):
        self.mine[lax.rem(p, SLOTS)] = value.astype(BF)

    def send(self, p):
        self.copy(lax.rem(p, SLOTS)).start()

    def wait(self, p):
        self.copy(lax.rem(p, SLOTS)).wait()

    def rows(self, p, at):
        slot = lax.rem(p, SLOTS)
        return self.mine[slot, at].astype(F32) + self.theirs[slot, at].astype(F32)


def swap_scratch(name, d):
    return [
        (name + "_mine", pltpu.VMEM((SLOTS, ROWS, d), BF)),
        (name + "_theirs", pltpu.VMEM((SLOTS, ROWS, d), BF)),
        (name + "_ss", pltpu.SemaphoreType.DMA((SLOTS,))),
        (name + "_rs", pltpu.SemaphoreType.DMA((SLOTS,))),
    ]


def swap_of(r, name):
    return Swap(*(getattr(r, name + part) for part in ("_mine", "_theirs", "_ss", "_rs")))


class Spread:
    def __init__(self, links, own, z_slots, xy_slots, mp_slot, ss, rs):
        self.l, self.own, self.z_slots, self.xy_slots = links, own, z_slots, xy_slots
        self.mp_slot = mp_slot
        self.ss, self.rs = ss, rs

    def copy(self, stage, k, src, dst, peer):
        return remote(src, dst, self.ss.at[stage, k], self.rs.at[stage, k], {"dp": peer})

    def along(self):
        l = self.l
        self.z_slots[l.z] = self.own[...]
        for k in range(1, l.nz):
            self.copy(0, k, self.own, self.z_slots.at[l.z], l.z_peer(k)).start()

    def across(self):
        l = self.l
        for k in range(1, l.nz):
            self.copy(0, k, self.own, self.z_slots.at[lax.rem(l.z - k + l.nz, l.nz)], l.z_peer(k)).wait()
        total = self.z_slots[0]
        for k in range(1, l.nz):
            total += self.z_slots[k]
        self.own[...] = total
        self.xy_slots[l.column] = total
        for k in range(1, 4):
            self.copy(1, k, self.own, self.xy_slots.at[l.column], l.column_peer(k)).start()

    def over(self):
        l = self.l
        for k in range(1, 4):
            self.copy(1, k, self.own, self.xy_slots.at[lax.rem(l.column - k + 4, 4)], l.column_peer(k)).wait()
        total = self.xy_slots[0]
        for k in range(1, 4):
            total += self.xy_slots[k]
        self.own[...] = total
        self.pair().start()

    def pair(self):
        return remote(self.own, self.mp_slot, self.ss.at[1, 0], self.rs.at[1, 0], partner())

    def total(self, split):
        self.pair().wait()
        own, other = self.own[...], self.mp_slot[...]
        row = lax.broadcasted_iota(jnp.int32, own.shape, 0)
        return jnp.where(row >= split, own + other, own)


def every(step, actions):
    for at, what, argument in actions:
        pl.when(step == at)(partial(what, argument))


gelu_root = math.sqrt(2.0 / math.pi)
gelu_cube = 0.044715
WINDOW = 272


STRIP = 32


def strips(step=STRIP):
    return [slice(i, i + step) for i in range(0, ROWS, step)]


def inverse_rms(v):
    return lax.rsqrt(jnp.mean(v * v, axis=-1, keepdims=True) + norm_eps)


def window_start(p, total):
    return min(p * PLEN // 16 * 16, total - WINDOW)


def align(source, target, windows, sems, passages):
    total = source.shape[0]

    def fetch(p):
        return pltpu.make_async_copy(
            source.at[pl.ds(window_start(p, total), WINDOW)], windows.at[p % 2], sems.at[p % 2]
        )

    def start():
        fetch(0).start()
        fetch(1).start()

    def move(first, last):
        for p in range(first, last):
            fetch(p).wait()
            off = p * PLEN - window_start(p, total)
            rows = windows[p % 2].astype(F32)[off : off + PLEN]
            pad = jnp.zeros((ROWS - PLEN, rows.shape[1]), F32)
            target[p] = jnp.concatenate([rows, pad], axis=0).astype(BF)
            if p + 2 < passages:
                fetch(p + 2).start()

    return start, move


def loop(first, last, body):
    lax.fori_loop(first, last, lambda p, carry: (body(p), carry)[1], 0)


PAIR = 2 * DH


def low_lanes(shape):
    return lax.broadcasted_iota(jnp.int32, shape, 1) < DH


def of_head(h, pair):
    low = low_lanes(pair.shape)
    zero = jnp.zeros_like(pair)
    return jnp.where(low, pair, zero) if h % 2 == 0 else jnp.where(low, zero, pair)


def either(first, second):
    return jnp.where(low_lanes(first.shape), first, second)


def forward_kernel(n, passages, heads, direct, r):
    width = heads * DH
    count = passages
    pair, back_in = (swap_of(r, name) for name in ("pair", "in"))
    if direct:
        links = Links(n)
        rows_o = r.wo_wide.shape[0] // n
        full = [(r.wi, r.wi.shape[0] // n, None), (r.wo_wide, rows_o, None)]
        full += [(w, w.shape[0] // n, None) for w in (r.we_a, r.wr_a, r.we_b, r.wr_b)]
        gather = Gather(links, full, r.g_ss, r.g_rs)
        grads = [(g, g.shape[0] // n) for g in (r.stage_r, r.stage_e)]
        kept = [r.sum_r, r.sum_e]
        sums = Scatter(links, grads, [r.buf_r, r.buf_e], r.s_ss, r.s_rs)
    tok_start, tok_move = align(r.tokens, r.tok, r.window, r.window_sem, passages)
    cot_start, cot_move = align(r.cotangent, r.cot, r.window, r.window_sem, passages)
    half = passages // 2
    proj, probs, normed_out, ctx = (Drain(r, name) for name in ("proj", "probs", "normed", "ctx"))
    layer, hidden_grad = (Drain(r, name) for name in ("layer", "hidden_grad"))

    def local(src, dst, i):
        return pltpu.make_async_copy(src, dst, r.out_sem.at[i])

    local(r.buckets.at[0], r.bucket_rows, 5).start()
    tok_start()
    if direct:
        gather.put(0, jnp.concatenate([r.own_i[c] for c in range(3)], axis=1).astype(BF))
        pad = jnp.zeros((rows_o - r.own_o.shape[0], r.own_o.shape[1]), F32)
        gather.put(1, jnp.concatenate([r.own_o[...], pad], axis=0).astype(BF))
        greet(links.peers() + [partner()])
        gather.own(0)
        gather.own(1)
        split, rest = full[3][1], full[5][1]
        columns = [r.own_e[:, d * (split + rest) : (d + 1) * (split + rest)].astype(BF) for d in range(n)]
        gather.put(2, jnp.concatenate([c[:, :split] for c in columns], axis=1))
        gather.put(3, r.own_r[:split].astype(BF))
        gather.put(4, jnp.concatenate([c[:, split:] for c in columns], axis=1))
        gather.put(5, r.own_r[split:].astype(BF))
    else:
        greet([partner()])
    tok_move(0, half)
    if direct:
        gather.along(0)
        gather.own(2)
    tok_move(half, passages)
    local(r.tok, r.tok_out, 0).start()
    cot_start()
    if direct:
        gather.across(0)
        gather.along(1)
    cot_move(0, half)
    if direct:
        gather.share(0)
        gather.across(1)
        gather.own(3)
    cot_move(half, passages)
    if direct:
        gather.share(1)
    for h in range(heads):
        line = dot_exact(r.table[h : h + 1, :], r.onehot[...])
        rows = jnp.broadcast_to(line, (ROWS, 2 * ROWS))
        r.bias[h] = pltpu.roll(rows, 0, 1, stride=1, stride_axis=0)[:, :ROWS]
    r.gain_grad[...] = jnp.zeros_like(r.gain_grad)

    def normalise(p):
        for at in strips():
            x = r.tok[p, at].astype(F32)
            r.out_sum[p, at] = x * inverse_rms(x) * r.gains[0:1, :]

    loop(0, count, normalise)
    local(r.buckets.at[0], r.bucket_rows, 5).wait()
    if direct:
        gather.arrived(0)

    def lanes(c, j):
        return slice(c * width + j * PAIR, c * width + (j + 1) * PAIR)

    def settle(p):
        pair.wait(p)
        for at in strips():
            r.hidden[p, at] = r.tok[p, at].astype(F32) + pair.rows(p, at)

    def attend(p):
        normed = r.out_sum[p].astype(BF)
        normed_slot, proj_slot, probs_slot, ctx_slot = (
            stream.slot(p) for stream in (normed_out, proj, probs, ctx)
        )
        normed_slot[...] = normed
        proj_slot[...] = dot(normed, r.wi[...]).astype(BF)
        valid = r.bucket_rows[pl.ds(p, 1), :] < BUCKETS
        masked = jnp.concatenate(
            [jnp.where(valid, 0.0, masked_score), jnp.full((1, ROWS - PLEN), masked_score, F32)], axis=1
        )
        pairs = [[proj_slot[:, lanes(c, j)] for c in range(3)] for j in range(heads // 2)]
        products = [dot(of_head(h, pairs[h // 2][0]), pairs[h // 2][1], 1, 1) for h in range(heads)]
        weighted = []
        for h in range(heads):
            parts = []
            for at in strips(64):
                sc = products[h][at] + r.bias[h, at] + masked
                e_ = jnp.exp(sc - jnp.max(sc, axis=-1, keepdims=True))
                parts.append((e_ * (1.0 / jnp.sum(e_, axis=-1, keepdims=True))).astype(BF))
                probs_slot[h, at] = parts[-1]
            weighted.append(jnp.concatenate(parts, axis=0))
        results = [dot(weighted[h], pairs[h // 2][2]) for h in range(heads)]
        for j in range(heads // 2):
            ctx_slot[:, lanes(0, j)] = either(results[2 * j], results[2 * j + 1]).astype(BF)
        if direct:

            @pl.when(p == 0)
            def _():
                gather.arrived(1)
                rows = r.own_o.shape[0]
                wide = r.acc_r
                for d in range(n):
                    block = r.wo_wide[d * rows_o : (d + 1) * rows_o, :].astype(F32)
                    wide[d * rows : (d + 1) * rows, :] = block[:rows]
                r.wo[...] = wide[: n * rows, :].astype(BF)

            every(p, (
                (0, gather.along, 2),
                (0, gather.along, 3),
                (1, gather.across, 2),
                (2, gather.across, 3),
                (2, gather.share, 2),
                (3, gather.share, 3),
                (3, gather.own, 4),
                (4, gather.own, 5),
                (6, gather.along, 4),
                (7, gather.along, 5),
            ))
        pair.put(p, dot(ctx_slot[...], r.wo[...]))
        pl.when(p >= LAG)(lambda: settle(p - LAG))
        pair.send(p)
        for stream in (normed_out, proj, probs, ctx):
            stream.start(p)

    loop(0, count, attend)

    if direct:
        gather.arrived(2)
        gather.arrived(3)
        local(r.wi, r.wi_out, 1).start()
        local(r.wo, r.wo_out, 2).start()

    def clear():
        r.acc_r[...] = jnp.zeros_like(r.acc_r)
        r.acc_e[...] = jnp.zeros_like(r.acc_e)

    def normed_two(p):
        parts = []
        for at in strips():
            h = r.hidden[p, at]
            parts.append((h * inverse_rms(h) * r.gains[1:2, :]).astype(BF))
        return jnp.concatenate(parts, axis=0)

    def inner_part(normed, c, we, wr):
        u_all, in_all = dot(normed, we[...]), dot(c, wr[...], 1, 1)
        acts, backs = [], []
        for at in strips():
            u = u_all[at]
            square = u * u
            t = jnp.tanh(u * (gelu_root + (gelu_root * gelu_cube) * square))
            half = 0.5 * (1.0 + t)
            acts.append((u * half).astype(BF))
            slope = half + (0.5 * u) * (1.0 - t * t) * (
                gelu_root + (3.0 * gelu_root * gelu_cube) * square
            )
            backs.append((in_all[at] * slope).astype(BF))
        return jnp.concatenate(acts, axis=0), jnp.concatenate(backs, axis=0)

    part_a = r.wr_a.shape[0]

    def outer_part(normed, c, act, back, we, wr):
        units = wr.shape[0]
        r.acc_r[:units] += dot(act, c, 0, 0)
        r.acc_e[:, :units] += dot(normed, back, 0, 0)
        return dot(act, wr[...]), dot(back, we[...], 1, 1)

    def first(p):
        normed, c = normed_two(p), r.cot[p]
        act, back = inner_part(normed, c, r.we_a, r.wr_a)
        r.out_sum[p], r.in_sum[p] = outer_part(normed, c, act, back, r.we_a, r.wr_a)

        @pl.when(p == 0)
        def _():
            for last in range(count - LAG, count):
                settle(last)

        if direct:
            every(p, ((0, gather.across, 4), (1, gather.across, 5), (2, gather.share, 4), (3, gather.share, 5), ))

    clear()
    loop(0, count, first)
    r.stage_r[...] = r.acc_r[:part_a].astype(BF)
    r.stage_e[...] = r.acc_e[:, :part_a].astype(BF)
    if direct:
        sums.far(0)
        sums.far(1)
        gather.arrived(4)
        gather.arrived(5)
    clear()

    def finish(last):
        layer_slot, grad_slot = layer.slot(last), hidden_grad.slot(last)
        pair.wait(count + last)
        back_in.wait(last)
        gain_rows = jnp.zeros((1, r.gains.shape[1]), F32)
        for at in strips():
            h = r.hidden[last, at]
            layer_slot[at] = (h + pair.rows(count + last, at)).astype(BF)
            grad = back_in.rows(last, at)
            inv = inverse_rms(h)
            hr = h * inv
            gain_rows += jnp.sum(grad * hr, axis=0, keepdims=True)
            zed = r.gains[1:2, :] * grad
            inner = jnp.mean(zed * hr, axis=-1, keepdims=True)
            grad_slot[at] = r.cot[last, at].astype(F32) + inv * (zed - hr * inner)
        r.gain_grad[0:1, :] += gain_rows

    def second(p, with_finish=True):
        normed, c = normed_two(p), r.cot[p]
        act, back = inner_part(normed, c, r.we_b, r.wr_b)
        if with_finish:
            finish(p - LAG)
        r_part, n_part = outer_part(normed, c, act, back, r.we_b, r.wr_b)
        pair.put(count + p, r.out_sum[p] + r_part)
        back_in.put(p, r.in_sum[p] + n_part)
        pair.send(count + p)
        back_in.send(p)
        if with_finish:
            for stream in (layer, hidden_grad):
                stream.start(p - LAG)
            if direct:
                every(p, ((3, sums.near, 0), (4, sums.near, 1)))

    loop(0, LAG, lambda p: second(p, False))
    if direct:
        sums.plain(0)
        sums.plain(1)
    loop(LAG, count, second)
    stage_rb, stage_eb = (r.wr_b, r.we_b) if direct else (r.stage_rb, r.stage_eb)
    if direct:
        gather.sent(4)
        gather.sent(5)
    stage_rb[...] = r.acc_r[...].astype(BF)
    stage_eb[...] = r.acc_e[...].astype(BF)
    local(stage_rb, r.grad_r, 3).start()
    local(stage_eb, r.grad_e, 4).start()
    if direct:
        for a in range(2):
            sums.along(a, kept[a])
    for p in range(count - LAG, count):
        finish(p)
        for stream in (layer, hidden_grad):
            stream.start(p)
    if direct:
        for a in range(2):
            sums.total(a, kept[a])
        for a in range(4):
            gather.sent(a)
        for a in range(2):
            sums.sent(a)
        local(r.wi, r.wi_out, 1).wait()
        local(r.wo, r.wo_out, 2).wait()
    local(r.tok, r.tok_out, 0).wait()
    local(stage_rb, r.grad_r, 3).wait()
    local(stage_eb, r.grad_e, 4).wait()
    for stream in (normed_out, proj, probs, ctx, layer, hidden_grad):
        stream.last()


def dot_exact(a, b):
    return lax.dot_general(
        a, b, (((1,), (1,)), ((), ())), precision=lax.Precision.HIGHEST, preferred_element_type=F32
    )


def forward(n, passages, heads, direct, tokens, cotangent, buckets, gains, table, onehot, weights):
    d = tokens.shape[1]
    width = heads * DH
    ins = [("tokens", tokens, ANY), ("cotangent", cotangent, ANY)]
    ins += [("buckets", buckets, ANY)]
    ins += [(k, v, VMEM) for k, v in (("gains", gains), ("table", table), ("onehot", onehot))]
    ins += [(k, v, VMEM) for k, v in weights.items()]
    if direct:
        part = weights["own_r"].shape[0] // 2 * n
        rest = weights["own_r"].shape[0] * n - part
    else:
        part, rest = weights["wr_a"].shape[0], weights["wr_b"].shape[0]
    streams = dict(
        proj=((ROWS, 3 * width), BF),
        probs=((heads, ROWS, ROWS), BF),
        normed=((ROWS, d), BF),
        ctx=((ROWS, width), BF),
        layer=((ROWS, d), BF),
        hidden_grad=((ROWS, d), F32),
    )
    outs = [(k, (passages,) + shape, dtype, ANY) for k, (shape, dtype) in streams.items()]
    outs += [
        ("tok_out", (passages, ROWS, d), BF, ANY),
        ("grad_r", (rest, d), BF, ANY),
        ("grad_e", (d, rest), BF, ANY),
        ("gain_grad", (8, d), F32, VMEM),
    ]
    scratch = [*dict(
        tok=pltpu.VMEM((passages, ROWS, d), BF),
        cot=pltpu.VMEM((passages, ROWS, d), BF),
        window=pltpu.VMEM((2, WINDOW, d), BF),
        window_sem=pltpu.SemaphoreType.DMA((2,)),
        bucket_rows=pltpu.VMEM(buckets.shape[1:], buckets.dtype),
        out_sem=pltpu.SemaphoreType.DMA((6,)),
        bias=pltpu.VMEM((heads, ROWS, ROWS), F32),
        hidden=pltpu.VMEM((passages, ROWS, d), F32),
        out_sum=pltpu.VMEM((passages, ROWS, d), F32),
        in_sum=pltpu.VMEM((passages, ROWS, d), F32),
        acc_r=pltpu.VMEM((rest, d), F32),
        acc_e=pltpu.VMEM((d, rest), F32),
    ).items()]
    for k, (shape, dtype) in streams.items():
        scratch += stream_scratch(k, shape, dtype)
    for name in ("pair", "in"):
        scratch += swap_scratch(name, d)
    stage = [("stage_r", (part, d)), ("stage_e", (d, part))]
    if direct:
        nz = n // 4
        padded = weights["own_o"].shape[0]
        padded += -padded % 16
        outs += [("wi_out", (d, 3 * width), BF, ANY), ("wo_out", (width, d), BF, ANY)]
        for key, shape in (("sum_r", (part // n, d)), ("sum_e", (d // n, part))):
            outs.append((key, shape, F32, VMEM))
        scratch += [(k, pltpu.VMEM(shape, BF)) for k, shape in stage]
        shapes = {"wi": (d, 3 * width), "wo": (width, d), "wo_wide": (n * padded, d)}
        for half, size in (("a", part), ("b", rest)):
            shapes["we_" + half], shapes["wr_" + half] = (d, size), (size, d)
        scratch += [(key, pltpu.VMEM(shape, BF)) for key, shape in shapes.items()]
        scratch += [*dict(
            buf_r=pltpu.VMEM((4, nz, part // n, d), BF),
            buf_e=pltpu.VMEM((4, nz, d // n, part), BF),
            g_ss=pltpu.SemaphoreType.DMA((6, 5, nz)),
            g_rs=pltpu.SemaphoreType.DMA((6, 5, nz)),
            s_ss=pltpu.SemaphoreType.DMA((2, 4, nz)),
            s_rs=pltpu.SemaphoreType.DMA((2, 4, nz)),
        ).items()]
    else:
        outs += [(k, shape, BF, VMEM) for k, shape in stage]
        scratch += [("stage_rb", pltpu.VMEM((rest, d), BF)), ("stage_eb", pltpu.VMEM((d, rest), BF))]
    kernel = partial(forward_kernel, n, passages, heads, direct)
    return run(kernel, ins, outs, scratch, 1, 63, "forward")


def back_kernel(n, passages, heads, direct, r):
    width = heads * DH
    count = passages
    swap = swap_of(r, "in")
    if direct:
        links = Links(n)
        refs = [r.grad_r, r.grad_e, r.stage_o, r.stage_v, r.stage_qk]
        grads = [(g, g.shape[0] // n) for g in refs]
        names = ["r", "e", "o", "v", "qk"]
        bufs = [getattr(r, "buf_" + k) for k in names]
        kept = [getattr(r, "sum_" + k) for k in names]
        sums = Scatter(links, grads, bufs, r.s_ss, r.s_rs)
        wide = Spread(links, r.wide, r.wide_z, r.wide_xy, r.wide_mp, r.w_ss, r.w_rs)
    ctx, normed, probs, proj, tok, hidden_grad = (
        Load(r, name) for name in ("ctx", "normed", "probs", "proj", "tok", "hidden_grad")
    )
    input_grad = Drain(r, "input_grad")

    for p in range(count):
        for stream in (hidden_grad, ctx, probs, normed):
            stream.copy(p).start()
    for stream in (proj, tok):
        stream.start()
    if direct:
        greet(links.peers() + [{"dp": links.far_peer}, partner()])
        sums.far(0)
        sums.far(1)
    else:
        greet([partner()])
    r.acc_o[...] = jnp.zeros_like(r.acc_o)
    r.acc_s[...] = jnp.zeros_like(r.acc_s)
    r.acc_v[...] = jnp.zeros_like(r.acc_v)
    r.acc_qk[...] = jnp.zeros_like(r.acc_qk)

    def lanes(c, j):
        return slice(c * width + j * PAIR, c * width + (j + 1) * PAIR)

    def values(p):
        for stream in (hidden_grad, ctx, probs, normed):
            stream.wait(p)
        top = hidden_grad.buf[p].astype(BF)
        r.acc_o[...] += dot(ctx.buf[p], top, 0, 0)
        dctx = dot(top, r.wo[...], 1, 1).astype(BF)
        r.dctx[p] = dctx
        results = [dot(probs.buf[p, h], dctx[:, lanes(0, h // 2)], 0, 0) for h in range(heads)]
        dv = [either(results[2 * j], results[2 * j + 1]) for j in range(heads // 2)]
        dv = jnp.concatenate(dv, axis=1).astype(BF)
        r.dproj[p, :, 2 * width :] = dv
        r.acc_v[...] += dot(normed.buf[p], dv, 0, 0)
        if direct:
            every(p, (
                (2, sums.plain, 0), (3, sums.plain, 1), (5, sums.near, 0), (7, sums.near, 1),
            ))

    loop(0, count, values)
    blocks = n if direct else 1
    rows = r.acc_o.shape[0] // blocks
    padded = r.stage_o.shape[0] // blocks
    for b in range(blocks):
        part = r.acc_o[b * rows : (b + 1) * rows, :]
        if padded > rows:
            part = jnp.concatenate([part, jnp.zeros((padded - rows, part.shape[1]), F32)], axis=0)
        r.stage_o[b * padded : (b + 1) * padded, :] = part.astype(BF)
    r.stage_v[...] = r.acc_v[...].astype(BF)
    if direct:
        sums.far(2)
        sums.far(3)

    def scores(p):
        proj.wait(p)
        pairs = [[proj.buf[p, :, lanes(c, j)] for c in range(3)] for j in range(heads // 2)]
        products = [
            dot(of_head(h, r.dctx[p, :, lanes(0, h // 2)]), pairs[h // 2][2], 1, 1) for h in range(heads)
        ]
        ds = []
        for h in range(heads):
            parts = []
            for rows in strips(64):
                a = probs.buf[p, h, rows].astype(F32)
                dp = products[h][rows]
                centre = jnp.sum(a * dp, axis=-1, keepdims=True)
                parts.append((a * (dp - centre)).astype(BF))
                r.acc_s[h, rows] += parts[-1].astype(F32)
            ds.append(jnp.concatenate(parts, axis=0))
        dq = [dot(ds[h], pairs[h // 2][1]) for h in range(heads)]
        dk = [dot(ds[h], pairs[h // 2][0], 0, 0) for h in range(heads)]
        for j in range(heads // 2):
            r.dproj[p, :, lanes(0, j)] = either(dq[2 * j], dq[2 * j + 1]).astype(BF)
            r.dproj[p, :, lanes(1, j)] = either(dk[2 * j], dk[2 * j + 1]).astype(BF)
        r.acc_qk[...] += dot(normed.buf[p], r.dproj[p, :, : 2 * width], 0, 0)
        if direct:
            every(p, ((0, sums.plain, 2), (0, sums.plain, 3)))
            for a, at in ((0, 4), (1, 6)):
                pl.when(p == at)(partial(sums.along, a, kept[a]))
            every(p, ((5, sums.near, 2), (7, sums.near, 3)))

    loop(0, count, scores)
    r.stage_qk[...] = r.acc_qk[...].astype(BF)
    if direct:
        sums.far(4)
    terms = jnp.sum(r.acc_v[...] * r.wi[:, 2 * width :].astype(F32), axis=1, keepdims=True)
    terms += jnp.sum(r.acc_qk[...] * r.wi[:, : 2 * width].astype(F32), axis=1, keepdims=True)
    r.wide[...] = jnp.zeros_like(r.wide)
    r.wide[heads : heads + 1, :] = 0.5 * r.gain_two[0:1, :]
    r.wide[heads + 1 : heads + 2, :] = terms.T / r.gains[0:1, :]
    for h in range(heads):
        lines = jnp.concatenate([r.acc_s[h], jnp.zeros((ROWS, ROWS), F32)], axis=1)
        while lines.shape[0] > 1:
            half = lines.shape[0] // 2
            lines = lines[:half] + pltpu.roll(lines[half:], 2 * ROWS - half, 1)
        r.wide[h : h + 1, : 2 * ROWS] = lines
    if direct:
        wide.along()
        sums.plain(4)

    def finish(last):
        tok.wait(last)
        slot = input_grad.slot(last)
        swap.wait(last)
        for at in strips():
            x = tok.buf[last, at].astype(F32)
            inv = inverse_rms(x)
            xr = x * inv
            zed = r.gains[0:1, :] * swap.rows(last, at)
            inner = jnp.mean(zed * xr, axis=-1, keepdims=True)
            slot[at] = hidden_grad.buf[last, at] + inv * (zed - xr * inner)

    def inputs(t, with_finish=True):
        terms = dot(r.dproj[t, :, : 2 * width], r.wi[:, : 2 * width], 1, 1)
        if with_finish:
            finish(t - LAG)
        terms += dot(r.dproj[t, :, 2 * width :], r.wi[:, 2 * width :], 1, 1)
        swap.put(t, terms)
        swap.send(t)
        if with_finish:
            input_grad.start(t - LAG)
            if direct:
                every(t, ((6, sums.near, 4),))
                for a, at in ((2, 3), (3, 5)):
                    pl.when(t == at)(partial(sums.along, a, kept[a]))
                pl.when(t == 2)(wide.across)
                pl.when(t == 5)(wide.over)

    loop(0, LAG, lambda t: inputs(t, False))
    loop(LAG, count, inputs)
    if direct:
        for a in range(4):
            sums.total(a, kept[a])
        sums.along(4, kept[4])
    for p in range(count - LAG, count):
        finish(p)
        input_grad.start(p)
    if direct:
        r.wide_sum[...] = wide.total(heads)
        sums.total(4, kept[4])
        for a in range(5):
            sums.sent(a)
    else:
        r.wide_sum[...] = r.wide[...]
    input_grad.last()


def back(n, passages, heads, direct, f, gains, wi, wo):
    d = gains.shape[1]
    width = heads * DH
    streams = dict(
        ctx=((ROWS, width), BF),
        normed=((ROWS, d), BF),
        probs=((heads, ROWS, ROWS), BF),
        proj=((ROWS, 3 * width), BF),
        tok=((ROWS, d), BF),
        hidden_grad=((ROWS, d), F32),
    )
    ins = [(k, f.tok_out if k == "tok" else getattr(f, k), ANY) for k in streams]
    fixed = [("gains", gains), ("wi", wi), ("wo", wo), ("gain_two", f.gain_grad)]
    outs = [
        ("input_grad", (passages, ROWS, d), F32, ANY),
        ("wide_sum", (8, d), F32, VMEM),
    ]
    scratch = [*dict(
        acc_qk=pltpu.VMEM((d, 2 * width), F32),
        acc_v=pltpu.VMEM((d, width), F32),
        acc_o=pltpu.VMEM((width, d), F32),
        acc_s=pltpu.VMEM((heads, ROWS, ROWS), F32),
        dctx=pltpu.VMEM((passages, ROWS, width), BF),
        dproj=pltpu.VMEM((passages, ROWS, 3 * width), BF),
        wide=pltpu.VMEM((8, d), F32),
    ).items()] + swap_scratch("in", d)
    for k, (shape, dtype) in streams.items():
        scratch.append((k + "_buf", pltpu.VMEM((passages,) + shape, dtype)))
        scratch.append((k + "_sem", pltpu.SemaphoreType.DMA((passages,))))
    scratch += stream_scratch("input_grad", (ROWS, d), F32)
    rows_o = width
    if direct:
        rows_o = width // n
        rows_o = (rows_o + -rows_o % 16) * n
    stage = [("stage_o", (rows_o, d)), ("stage_v", (d, width)), ("stage_qk", (d, 2 * width))]
    if direct:
        nz = n // 4
        fixed += [(k, getattr(f, k)) for k in ("grad_r", "grad_e")]
        scratch += [(k, pltpu.VMEM(shape, BF)) for k, shape in stage]
        blocks = {"r": f.grad_r.shape, "e": f.grad_e.shape}
        blocks.update({k[6:]: shape for k, shape in stage})
        for key, shape in blocks.items():
            shape = (shape[0] // n, shape[1])
            scratch.append(("buf_" + key, pltpu.VMEM((4, nz) + shape, BF)))
            outs.append(("sum_" + key, shape, F32, VMEM))
        scratch += [*dict(
            wide_z=pltpu.VMEM((nz, 8, d), F32),
            wide_xy=pltpu.VMEM((4, 8, d), F32),
            wide_mp=pltpu.VMEM((8, d), F32),
            s_ss=pltpu.SemaphoreType.DMA((len(blocks), 4, nz)),
            s_rs=pltpu.SemaphoreType.DMA((len(blocks), 4, nz)),
            w_ss=pltpu.SemaphoreType.DMA((2, max(nz, 4))),
            w_rs=pltpu.SemaphoreType.DMA((2, max(nz, 4))),
        ).items()]
    else:
        outs += [(k, shape, BF, VMEM) for k, shape in stage]
    ins += [(k, v, VMEM) for k, v in fixed]
    kernel = partial(back_kernel, n, passages, heads, direct)
    return run(kernel, ins, outs, scratch, 2, 63, "back")


rates = {
    "i": rate_inward, "o": rate_outward, "e": rate_expand, "r": rate_reduce, "g": rate_gains, "t": rate_table,
}


def update_kernel(n, passages, heads, keys, r):
    total = r.layer_out.shape[0]
    ins = [(getattr(r, k), getattr(r, k + "_in")) for k in keys]
    fetch = {k: pltpu.make_async_copy(a, b, r.in_sem.at[i]) for i, (k, (a, b)) in enumerate(zip(keys, ins))}
    stores = []

    def store(src, dst):
        copy = pltpu.make_async_copy(src, dst, r.out_sem.at[len(stores)])
        copy.start()
        stores.append(copy)

    def passage(name, p, sem):
        return pltpu.make_async_copy(getattr(r, name).at[p], getattr(r, name + "_in").at[p], sem.at[p])

    for k in keys:
        fetch[k].start()
    for p in range(passages):
        passage("grad", p, r.grad_sem).start()
        passage("layer", p, r.layer_sem).start()

    def get(k):
        fetch[k].wait()
        return getattr(r, k + "_in")

    def step(key, gradient, at=...):
        out = adamw(*(getattr(r, key + part + "_in")[at] for part in "wmv"), gradient, rates[key])
        for part, value in zip(("_nw", "_nm", "_nv"), out):
            getattr(r, key + part + "_out")[at] = value
        if key not in "gt":
            getattr(r, key + "_nc_out")[at] = out[0].astype(BF)

    def ready(key):
        for part in "wmv":
            fetch[key + part].wait()

    def done(key):
        for part in ("_nw", "_nm", "_nv") + ("_nc",) * (key not in "gt"):
            store(getattr(r, key + part + "_out"), getattr(r, key + part))

    first_r, first_e = get("first_r"), get("first_e")
    second_r, second_e = get("second_r"), get("second_e")
    ready("r")
    split = first_r.shape[0]
    step("r", first_r[...], slice(0, split))
    step("r", second_r[...], slice(split, split + second_r.shape[0]))
    done("r")
    ready("e")
    one, two = first_e.shape[1] // n, second_e.shape[1] // n
    columns = []
    for d in range(n):
        columns += [first_e[:, d * one : (d + 1) * one], second_e[:, d * two : (d + 1) * two]]
    step("e", jnp.concatenate(columns, axis=1))
    done("e")
    ready("o")
    step("o", get("sum_o")[: r.ow_in.shape[0]])
    done("o")
    ready("i")
    qk, v = get("sum_qk"), get("sum_v")
    width = v.shape[1]
    step("i", qk[:, :width], 0)
    step("i", qk[:, width:], 1)
    step("i", v[...], 2)
    done("i")
    ready("g")
    small = get("small")
    step("g", small[heads + 1 : heads + 2], slice(0, 1))
    step("g", small[heads : heads + 1], slice(1, 2))
    done("g")
    ready("t")
    onehot = get("onehot")
    step("t", lax.dot_general(
        small[:heads, : 2 * ROWS], onehot[...], (((1,), (0,)), ((), ())),
        precision=lax.Precision.HIGHEST, preferred_element_type=F32,
    ))
    done("t")
    sent = 0
    for p in range(passages):
        at = slice(p * PLEN, (p + 1) * PLEN)
        passage("grad", p, r.grad_sem).wait()
        r.grad_rows[at] = r.grad_in[p, :PLEN]
        passage("layer", p, r.layer_sem).wait()
        r.layer_wide[at] = r.layer_in[p, :PLEN].astype(F32)
        end = total if p == passages - 1 else (p + 1) * PLEN // 16 * 16
        rows = slice(sent, end)
        store(r.grad_rows.at[rows], r.input_grad.at[rows])
        r.layer_rows[rows] = r.layer_wide[rows].astype(BF)
        store(r.layer_rows.at[rows], r.layer_out.at[rows])
        sent = end
    for copy in stores:
        copy.wait()


def update(n, passages, heads, shape, f, b, onehot, states):
    total, d = shape
    small = dict(first_r=f.sum_r, first_e=f.sum_e, second_r=b.sum_r, second_e=b.sum_e)
    ins = [(k, v) for k, v in small.items()]
    ins += [(key + part, a) for key in "reo" for part, a in zip("wmv", states[key])]
    ins += [("sum_o", b.sum_o), ("sum_qk", b.sum_qk), ("sum_v", b.sum_v)]
    ins += [("small", b.wide_sum), ("onehot", onehot)]
    ins += [(key + part, a) for key in "igt" for part, a in zip("wmv", states[key])]
    keys = [k for k, _ in ins]
    scratch = [(k + "_in", pltpu.VMEM(a.shape, a.dtype)) for k, a in ins]
    outs = []
    for key in "ioergt":
        for part in ("_nw", "_nm", "_nv") + ("_nc",) * (key not in "gt"):
            outs.append((key + part, states[key][0].shape, BF if part == "_nc" else F32, ANY))
    scratch += [(k + "_out", pltpu.VMEM(dims, dtype)) for k, dims, dtype, _ in outs]
    padded = (passages, ROWS, d)
    count = len(outs) + 2 * passages
    scratch += [*dict(
        grad_in=pltpu.VMEM(padded, F32),
        layer_in=pltpu.VMEM(padded, BF),
        grad_rows=pltpu.VMEM((total, d), F32),
        layer_wide=pltpu.VMEM((total, d), F32),
        layer_rows=pltpu.VMEM((total, d), BF),
        in_sem=pltpu.SemaphoreType.DMA((len(keys),)),
        out_sem=pltpu.SemaphoreType.DMA((count,)),
        grad_sem=pltpu.SemaphoreType.DMA((passages,)),
        layer_sem=pltpu.SemaphoreType.DMA((passages,)),
    ).items()]
    ins += [("layer", f.layer), ("grad", b.input_grad)]
    outs += [("layer_out", shape, BF, ANY), ("input_grad", shape, F32, ANY)]
    kernel = partial(update_kernel, n, passages, heads, keys)
    o = run(kernel, [(k, a, ANY) for k, a in ins], outs, scratch, None, 60, "update")
    new = [o.layer_out, o.input_grad]
    for key in "ioergt":
        for part in ("_nw", "_nm", "_nv") + ("_nc",) * (key not in "gt"):
            value = getattr(o, key + part)
            if key == "i":
                value = value.transpose(1, 0, 2)
            new.append(value.T if key == "t" else value)
    return tuple(new)


def shards(
    n,
    tokens,
    cotangent,
    buckets,
    inward_master,
    inward_first,
    inward_second,
    outward_master,
    outward_first,
    outward_second,
    expand_master,
    expand_first,
    expand_second,
    reduce_master,
    reduce_first,
    reduce_second,
    gains_master,
    gains_first,
    gains_second,
    table_master,
    table_first,
    table_second,
):
    d = tokens.shape[1]
    passages = tokens.shape[0] // PLEN
    heads = inward_master.shape[2] // DH
    width = heads * DH
    rows_i, rows_r = inward_master.shape[0], reduce_master.shape[0]
    units = expand_master.shape[1]
    direct = n % 8 == 0 and rows_i % 16 == 0 and rows_r % 32 == 0 and outward_master.shape[0] % 8 == 0

    onehot = jnp.asarray(distance_onehot())
    bucket_rows = buckets.transpose(1, 0, 2)
    table_rows = table_master.T
    if direct:
        weights = dict(
            own_i=inward_master.transpose(1, 0, 2),
            own_o=outward_master,
            own_e=expand_master,
            own_r=reduce_master,
        )
    else:
        masters = (inward_master.reshape(-1, 3 * width), outward_master, expand_master, reduce_master)
        wi, wo, we, wr = (
            lax.all_gather(w.astype(BF), "dp", axis=0, tiled=True) for w in masters
        )
        half = units // 2
        weights = {"wi": wi, "wo": wo}
        weights.update({"we_a": we[:, :half], "wr_a": wr[:half], "we_b": we[:, half:], "wr_b": wr[half:]})
    f = forward(
        n, passages, heads, direct, tokens, cotangent, bucket_rows, gains_master, table_rows, onehot, weights
    )
    if direct:
        wi, wo = f.wi_out, f.wo_out
    b = back(n, passages, heads, direct, f, gains_master, wi, wo)

    def scatter(g):
        return lax.psum_scatter(g.astype(F32), "dp", scatter_dimension=0, tiled=True)

    if direct:
        states = dict(
            i=tuple(a.transpose(1, 0, 2) for a in (inward_master, inward_first, inward_second)),
            o=(outward_master, outward_first, outward_second),
            e=(expand_master, expand_first, expand_second),
            r=(reduce_master, reduce_first, reduce_second),
            g=(gains_master, gains_first, gains_second),
            t=(table_master.T, table_first.T, table_second.T),
        )
        return update(n, passages, heads, tokens.shape, f, b, onehot, states)
    else:
        inward_sum = scatter(jnp.concatenate([b.stage_qk, b.stage_v], axis=1))
        outward_sum = scatter(b.stage_o)
        expand_sum = scatter(jnp.concatenate([f.stage_e, f.grad_e], axis=1))
        reduce_sum = scatter(jnp.concatenate([f.stage_r, f.grad_r], axis=0))
        wide_sum = lax.psum(b.wide_sum, "dp")
        gains = lax.psum(wide_sum[heads : heads + 2], "mp")
        wide_sum = jnp.concatenate([wide_sum[:heads], gains], axis=0)
    inward_sum = inward_sum.reshape(inward_master.shape)
    gains_sum = jnp.concatenate([wide_sum[heads + 1 : heads + 2], wide_sum[heads : heads + 1]], axis=0)
    table_sum = lax.dot_general(
        onehot.T, wide_sum[:heads, : 2 * ROWS], (((1,), (1,)), ((), ())), precision=lax.Precision.HIGHEST
    )

    layer_out = f.layer[:, :PLEN].reshape(tokens.shape)
    input_grad = b.input_grad[:, :PLEN].reshape(tokens.shape)
    outputs = [layer_out, input_grad]
    for w, first_moment, second_moment, gradient, rate, copied in (
        (inward_master, inward_first, inward_second, inward_sum, rate_inward, True),
        (outward_master, outward_first, outward_second, outward_sum, rate_outward, True),
        (expand_master, expand_first, expand_second, expand_sum, rate_expand, True),
        (reduce_master, reduce_first, reduce_second, reduce_sum, rate_reduce, True),
        (gains_master, gains_first, gains_second, gains_sum, rate_gains, False),
        (table_master, table_first, table_second, table_sum, rate_table, False),
    ):
        new = adamw(w, first_moment, second_moment, gradient, rate)
        outputs += list(new)
        if copied:
            outputs.append(new[0].astype(BF))
    return tuple(outputs)


def solution(mesh):
    rows = P("dp", None)
    inward = P("dp", None, "mp")
    tall = P(("mp", "dp"), None)
    wide = P("dp", "mp")
    table = P(None, "mp")
    return jax.shard_map(
        partial(shards, mesh.shape["dp"]),
        mesh=mesh,
        in_specs=(rows, rows, P("dp", None, None))
        + (inward,) * 3
        + (tall,) * 3
        + (wide,) * 3
        + (tall,) * 3
        + (P(),) * 3
        + (table,) * 3,
        out_specs=(rows, rows)
        + (inward,) * 4
        + (tall,) * 4
        + (wide,) * 4
        + (tall,) * 4
        + (P(),) * 3
        + (table,) * 3,
        check_vma=False,
    )
```

```python
from functools import partial
import math

import jax
import jax.numpy as jnp
import numpy as np
from jax import lax
from jax.experimental import pallas as pl
from jax.experimental.pallas import tpu as pltpu
from jax.sharding import PartitionSpec as P

DH = 64
PLEN = 250
STEP = 5
ROWS = 256
BUCKETS = 32
SPAN = 128

MESH = pl.DeviceIdType.MESH
BF = jnp.bfloat16
F32 = jnp.float32
MIB = 2**20

norm_eps = 1e-06
masked_score = -1000000000.0
beta_first = 0.5
beta_second = 0.5
adam_eps = 1e-08
decay_rate = 0.01
rate_inward = 0.015
rate_outward = 0.3
rate_expand = 0.04
rate_reduce = 0.02
rate_gains = 0.5
rate_table = 0.5


def adamw(weight, first_moment, second, gradient, step_rate):
    new_first = beta_first * first_moment + (1.0 - beta_first) * gradient
    new_second = beta_second * second + (1.0 - beta_second) * gradient * gradient
    first_hat = new_first / (1.0 - beta_first**STEP)
    second_hat = new_second / (1.0 - beta_second**STEP)
    new_weight = weight - step_rate * (
        first_hat / (jnp.sqrt(second_hat) + adam_eps) + decay_rate * weight
    )
    return (new_weight, new_first, new_second)


def distance_onehot():
    span = 2 * ROWS
    relative = np.arange(span)
    relative = np.where(relative < ROWS, relative, relative - span)
    half = BUCKETS // 2
    exact = half // 2
    distance = np.abs(relative)
    far = np.full_like(distance, exact)
    for level in range(1, half - exact):
        far += distance >= math.ceil(exact * (SPAN / exact) ** (level / (half - exact)))
    bucket = np.where(relative > 0, half, 0) + np.where(distance < exact, distance, far)
    return (bucket[:, None] == np.arange(BUCKETS)[None]).astype(np.float32)


def dot(a, b, ca=1, cb=0):
    return lax.dot_general(a, b, (((ca,), (cb,)), ((), ())), preferred_element_type=F32)


class Refs:
    pass


def run(kernel, ins, outs, scratch, collective, limit, name):
    names = [i[0] for i in ins] + [o[0] for o in outs] + [s[0] for s in scratch]

    def body(*refs):
        space = Refs()
        for key, ref in zip(names, refs, strict=True):
            setattr(space, key, ref)
        kernel(space)

    results = pl.pallas_call(
        body,
        in_specs=[i[2] for i in ins],
        out_specs=[o[3] for o in outs],
        out_shape=[jax.ShapeDtypeStruct(o[1], o[2]) for o in outs],
        scratch_shapes=[s[1] for s in scratch],
        compiler_params=pltpu.CompilerParams(
            collective_id=collective, has_side_effects=collective is not None, vmem_limit_bytes=limit * MIB
        ),
        name=name,
    )(*[i[1] for i in ins])
    space = Refs()
    for out, result in zip(outs, results, strict=True):
        setattr(space, out[0], result)
    return space


ANY = pl.BlockSpec(memory_space=pl.ANY)
VMEM = pl.BlockSpec(memory_space=pltpu.VMEM)


class Load:
    def __init__(self, r, name):
        self.hbm, self.buf, self.sem = (getattr(r, name + part) for part in ("", "_buf", "_sem"))

    def copy(self, p):
        return pltpu.make_async_copy(self.hbm.at[p], self.buf.at[p], self.sem.at[p])

    def start(self):
        for p in range(self.hbm.shape[0]):
            self.copy(p).start()

    def wait(self, p):
        self.copy(p).wait()


class Drain:
    def __init__(self, r, name):
        self.hbm, self.buf, self.sem = (getattr(r, name + part) for part in ("", "_buf", "_sem"))

    def copy(self, p):
        slot = lax.rem(p, 2)
        return pltpu.make_async_copy(self.buf.at[slot], self.hbm.at[p], self.sem.at[slot])

    def slot(self, p):
        pl.when(p >= 2)(lambda: self.copy(p - 2).wait())
        return self.buf.at[lax.rem(p, 2)]

    def start(self, p):
        self.copy(p).start()

    def last(self):
        for p in range(max(self.hbm.shape[0] - 2, 0), self.hbm.shape[0]):
            self.copy(p).wait()


def stream_scratch(name, shape, dtype):
    return [
        (name + "_buf", pltpu.VMEM((2,) + tuple(shape), dtype)),
        (name + "_sem", pltpu.SemaphoreType.DMA((2,))),
    ]


class Links:
    def __init__(self, n):
        me = lax.axis_index("dp")
        self.n, self.nz, self.me = n, n // 4, me
        x, y = lax.rem(me, 2), lax.rem(me // 2, 2)
        self.z, self.column = me // 4, lax.rem(me, 4)
        self.x_peer, self.y_peer = me + 1 - 2 * x, me + 2 - 4 * y
        self.far_peer = self.x_peer + 2 - 4 * y
        self.z_pair = self.z + 1 - 2 * lax.rem(self.z, 2)
        self.pair_peer = self.z_pair * 4 + self.column

    def z_peer(self, k):
        return lax.rem(self.z + k + self.nz, self.nz) * 4 + self.column

    def block(self, k, column_of, z=None):
        return lax.rem((self.z if z is None else z) + k, self.nz) * 4 + lax.rem(column_of, 4)

    def peers(self):
        ids = [self.x_peer, self.y_peer] + [self.z_peer(k) for k in range(1, self.nz)]
        return [{"dp": i} for i in ids]

    def column_peer(self, k):
        return self.z * 4 + lax.rem(self.column + k + 4, 4)


def greet(peers):
    barrier = pltpu.get_barrier_semaphore()
    for peer in peers:
        pl.semaphore_signal(barrier, inc=1, device_id=peer, device_id_type=MESH)
    pl.semaphore_wait(barrier, len(peers))


def partner():
    return {"mp": 1 - lax.axis_index("mp")}


def cut(ref, blk, rows):
    return ref.at[pl.ds(pl.multiple_of(blk * rows, 16), rows)]


def remote(src, dst, send, recv, peer):
    return pltpu.make_async_remote_copy(
        src_ref=src,
        dst_ref=dst,
        send_sem=send,
        recv_sem=recv,
        device_id=peer,
        device_id_type=MESH,
    )


class Gather:
    def __init__(self, links, full, ss, rs):
        self.l, self.full, self.ss, self.rs = links, full, ss, rs

    def at(self, a, blk):
        ref, rows, lanes = self.full[a]
        rows = pl.ds(pl.multiple_of(blk * rows, 16), rows)
        return ref.at[rows] if lanes is None else ref.at[rows, pl.ds(*lanes)]

    def copy(self, a, role, k, blk, peer):
        at = self.at(a, blk)
        return remote(at, at, self.ss.at[a, role, k], self.rs.at[a, role, k], {"dp": peer})

    def put(self, a, value):
        self.at(a, self.l.me)[...] = value

    def own(self, a):
        l = self.l
        for k in range(1, l.nz):
            self.copy(a, 0, k, l.me, l.z_peer(-k)).start()
        self.copy(a, 1, 0, l.me, l.x_peer).start()
        self.copy(a, 2, 0, l.me, l.y_peer).start()

    def along(self, a):
        l = self.l
        for k in range(1, l.nz):
            blk = l.block(k, l.me)
            self.copy(a, 0, k, blk, l.x_peer).wait_recv()
            self.copy(a, 1, k, blk, l.x_peer).start()
            self.copy(a, 2, k, blk, l.y_peer).start()

    def across(self, a):
        l = self.l
        for k in range(0, l.nz, 2):
            role, source, target = (1, l.x_peer, l.y_peer) if k % 4 == 0 else (2, l.y_peer, l.x_peer)
            blk = l.block(k, source)
            self.copy(a, role, k, blk, source).wait_recv()
            self.copy(a, 3, k, blk, target).start()

    def share(self, a):
        l = self.l
        for k in range(0, l.nz, 2):
            blk = l.block(k, l.far_peer)
            self.copy(a, 3, k, blk, l.x_peer).wait_recv()
            self.copy(a, 4, k, blk, l.pair_peer).start()

    def arrived(self, a):
        l = self.l
        for k in range(l.nz):
            if k % 4 != 0:
                self.copy(a, 1, k, l.block(k, l.x_peer), l.x_peer).wait_recv()
            if k % 4 != 2:
                self.copy(a, 2, k, l.block(k, l.y_peer), l.y_peer).wait_recv()
            if k % 2 == 0:
                self.copy(a, 4, k, l.block(k, l.far_peer, l.z_pair), l.pair_peer).wait_recv()

    def sent(self, a):
        l = self.l
        for k in range(l.nz):
            roles = (0,) * (k > 0) + (1, 2) + (3, 4) * (k % 2 == 0)
            for role in roles:
                self.copy(a, role, k, l.me, l.x_peer).wait_send()


class Scatter:
    def __init__(self, links, grads, bufs, ss, rs):
        self.l, self.grads, self.bufs, self.ss, self.rs = links, grads, bufs, ss, rs

    def part(self, a, blk):
        ref, rows = self.grads[a]
        return cut(ref, blk, rows)

    def read(self, a, blk):
        ref, rows = self.grads[a]
        return ref[pl.ds(pl.multiple_of(blk * rows, 16), rows), :].astype(F32)

    def copy(self, a, role, k, src, slot, peer):
        dst = self.bufs[a].at[slot, k]
        return remote(src, dst, self.ss.at[a, role, k], self.rs.at[a, role, k], {"dp": peer})

    def arrive(self, a, role, k, slot):
        self.copy(a, role, k, self.part(a, 0), slot, self.l.x_peer).wait_recv()

    def far(self, a):
        l = self.l
        for k in range(l.nz):
            peer = l.y_peer if k % 2 == 0 else l.x_peer
            self.copy(a, 0, k, self.part(a, l.block(k, l.far_peer)), 0, peer).start()

    def plain(self, a):
        l = self.l
        for k in range(l.nz):
            if k % 2 == 1:
                self.copy(a, 1, k, self.part(a, l.block(k, l.x_peer)), 1, l.x_peer).start()
            else:
                self.copy(a, 2, k, self.part(a, l.block(k, l.y_peer)), 2, l.y_peer).start()

    def near(self, a):
        l = self.l
        for k in range(l.nz):
            self.arrive(a, 0, k, 0)
            role, peer = (1, l.x_peer) if k % 2 == 0 else (2, l.y_peer)
            mine = self.read(a, l.block(k, peer)) + self.bufs[a][0, k].astype(F32)
            self.bufs[a][0, k] = mine.astype(BF)
            self.copy(a, role, k, self.bufs[a].at[0, k], role, peer).start()

    def along(self, a, kept, held=None):
        l = self.l
        for k in list(range(1, l.nz)) + [0]:
            self.arrive(a, 1, k, 1)
            self.arrive(a, 2, k, 2)
            mine = (
                self.read(a, l.block(k, l.me))
                + self.bufs[a][1, k].astype(F32)
                + self.bufs[a][2, k].astype(F32)
            )
            if k == 0:
                kept[...] = mine
            elif held is not None:
                held[k] = mine.astype(BF)
            else:
                self.bufs[a][1, k] = mine.astype(BF)
                self.copy(a, 3, k, self.bufs[a].at[1, k], 3, l.z_peer(k)).start()

    def total(self, a, kept):
        total = kept[...]
        for k in range(1, self.l.nz):
            self.arrive(a, 3, k, 3)
            total += self.bufs[a][3, k].astype(F32)
        kept[...] = total

    def sent(self, a, held=False):
        for k in range(self.l.nz):
            for role in (0, 1, 2) + (3,) * (k > 0 and not held):
                self.copy(a, role, k, self.part(a, 0), 0, self.l.x_peer).wait_send()


LAG = 2
SLOTS = 4


class Swap:
    def __init__(self, mine, theirs, ss, rs):
        self.mine, self.theirs, self.ss, self.rs = mine, theirs, ss, rs

    def copy(self, slot):
        return remote(
            self.mine.at[slot], self.theirs.at[slot], self.ss.at[slot], self.rs.at[slot], partner()
        )

    def put(self, p, value):
        self.mine[lax.rem(p, SLOTS)] = value.astype(BF)

    def send(self, p):
        self.copy(lax.rem(p, SLOTS)).start()

    def wait(self, p):
        self.copy(lax.rem(p, SLOTS)).wait()

    def rows(self, p, at):
        slot = lax.rem(p, SLOTS)
        return self.mine[slot, at].astype(F32) + self.theirs[slot, at].astype(F32)


def swap_scratch(name, d):
    return [
        (name + "_mine", pltpu.VMEM((SLOTS, ROWS, d), BF)),
        (name + "_theirs", pltpu.VMEM((SLOTS, ROWS, d), BF)),
        (name + "_ss", pltpu.SemaphoreType.DMA((SLOTS,))),
        (name + "_rs", pltpu.SemaphoreType.DMA((SLOTS,))),
    ]


def swap_of(r, name):
    return Swap(*(getattr(r, name + part) for part in ("_mine", "_theirs", "_ss", "_rs")))


class Spread:
    def __init__(self, links, own, z_slots, xy_slots, mp_slot, ss, rs):
        self.l, self.own, self.z_slots, self.xy_slots = links, own, z_slots, xy_slots
        self.mp_slot = mp_slot
        self.ss, self.rs = ss, rs

    def copy(self, stage, k, src, dst, peer):
        return remote(src, dst, self.ss.at[stage, k], self.rs.at[stage, k], {"dp": peer})

    def along(self):
        l = self.l
        self.z_slots[l.z] = self.own[...]
        for k in range(1, l.nz):
            self.copy(0, k, self.own, self.z_slots.at[l.z], l.z_peer(k)).start()

    def across(self):
        l = self.l
        for k in range(1, l.nz):
            self.copy(0, k, self.own, self.z_slots.at[lax.rem(l.z - k + l.nz, l.nz)], l.z_peer(k)).wait()
        total = self.z_slots[0]
        for k in range(1, l.nz):
            total += self.z_slots[k]
        self.own[...] = total
        self.xy_slots[l.column] = total
        for k in range(1, 4):
            self.copy(1, k, self.own, self.xy_slots.at[l.column], l.column_peer(k)).start()

    def over(self):
        l = self.l
        for k in range(1, 4):
            self.copy(1, k, self.own, self.xy_slots.at[lax.rem(l.column - k + 4, 4)], l.column_peer(k)).wait()
        total = self.xy_slots[0]
        for k in range(1, 4):
            total += self.xy_slots[k]
        self.own[...] = total
        self.pair().start()

    def pair(self):
        return remote(self.own, self.mp_slot, self.ss.at[1, 0], self.rs.at[1, 0], partner())

    def total(self, split):
        self.pair().wait()
        own, other = self.own[...], self.mp_slot[...]
        row = lax.broadcasted_iota(jnp.int32, own.shape, 0)
        return jnp.where(row >= split, own + other, own)


def every(step, actions):
    for at, what, argument in actions:
        pl.when(step == at)(partial(what, argument))


gelu_root = math.sqrt(2.0 / math.pi)
gelu_cube = 0.044715
WINDOW = 272


STRIP = 32


def strips(step=STRIP):
    return [slice(i, i + step) for i in range(0, ROWS, step)]


def inverse_rms(v):
    return lax.rsqrt(jnp.mean(v * v, axis=-1, keepdims=True) + norm_eps)


def window_start(p, total):
    return min(p * PLEN // 16 * 16, total - WINDOW)


def align(source, target, windows, sems, passages):
    total = source.shape[0]

    def fetch(p):
        return pltpu.make_async_copy(
            source.at[pl.ds(window_start(p, total), WINDOW)], windows.at[p % 2], sems.at[p % 2]
        )

    def start():
        fetch(0).start()
        fetch(1).start()

    def move(first, last):
        for p in range(first, last):
            fetch(p).wait()
            off = p * PLEN - window_start(p, total)
            rows = windows[p % 2].astype(F32)[off : off + PLEN]
            pad = jnp.zeros((ROWS - PLEN, rows.shape[1]), F32)
            target[p] = jnp.concatenate([rows, pad], axis=0).astype(BF)
            if p + 2 < passages:
                fetch(p + 2).start()

    return start, move


def loop(first, last, body):
    lax.fori_loop(first, last, lambda p, carry: (body(p), carry)[1], 0)


PAIR = 2 * DH


def low_lanes(shape):
    return lax.broadcasted_iota(jnp.int32, shape, 1) < DH


def of_head(h, pair):
    low = low_lanes(pair.shape)
    zero = jnp.zeros_like(pair)
    return jnp.where(low, pair, zero) if h % 2 == 0 else jnp.where(low, zero, pair)


def either(first, second):
    return jnp.where(low_lanes(first.shape), first, second)


def forward_kernel(n, passages, heads, direct, r):
    width = heads * DH
    count = passages
    pair, back_in = (swap_of(r, name) for name in ("pair", "in"))
    if direct:
        links = Links(n)
        rows_o = r.wo_wide.shape[0] // n
        full = [(r.wi, r.wi.shape[0] // n, None), (r.wo_wide, rows_o, None)]
        full += [(w, w.shape[0] // n, None) for w in (r.we_a, r.wr_a, r.we_b, r.wr_b, r.we_c, r.wr_c)]
        gather = Gather(links, full, r.g_ss, r.g_rs)
        grads = [(g, g.shape[0] // n) for g in (r.stage_ra, r.stage_ea, r.stage_rb, r.stage_eb)]
        kept = [r.sum_ra, r.sum_ea, r.sum_rb, r.sum_eb]
        sums = Scatter(links, grads, [r.buf_ra, r.buf_ea, r.buf_rb, r.buf_eb], r.s_ss, r.s_rs)
    tok_start, tok_move = align(r.tokens, r.tok, r.window, r.window_sem, passages)
    cot_start, cot_move = align(r.cotangent, r.cot, r.window, r.window_sem, passages)
    half = passages // 2
    proj, probs, normed_out, ctx = (Drain(r, name) for name in ("proj", "probs", "normed", "ctx"))
    layer, hidden_grad = (Drain(r, name) for name in ("layer", "hidden_grad"))

    def local(src, dst, i):
        return pltpu.make_async_copy(src, dst, r.out_sem.at[i])

    local(r.buckets.at[0], r.bucket_rows, 5).start()
    tok_start()
    if direct:
        gather.put(0, jnp.concatenate([r.own_i[c] for c in range(3)], axis=1).astype(BF))
        pad = jnp.zeros((rows_o - r.own_o.shape[0], r.own_o.shape[1]), F32)
        gather.put(1, jnp.concatenate([r.own_o[...], pad], axis=0).astype(BF))
        greet(links.peers() + [partner()])
        gather.own(0)
        gather.own(1)
        third = full[3][1]
        columns = [r.own_e[:, d * 3 * third : (d + 1) * 3 * third].astype(BF) for d in range(n)]
        for i in range(3):
            at = slice(i * third, (i + 1) * third)
            gather.put(2 + 2 * i, jnp.concatenate([c[:, at] for c in columns], axis=1))
            gather.put(3 + 2 * i, r.own_r[at].astype(BF))
    else:
        greet([partner()])
    tok_move(0, half)
    if direct:
        gather.along(0)
        gather.own(2)
    tok_move(half, passages)
    local(r.tok, r.tok_out, 0).start()
    cot_start()
    if direct:
        gather.across(0)
        gather.along(1)
    cot_move(0, half)
    if direct:
        gather.share(0)
        gather.across(1)
        gather.own(3)
    cot_move(half, passages)
    if direct:
        gather.share(1)
    for h in range(heads):
        line = dot_exact(r.table[h : h + 1, :], r.onehot[...])
        rows = jnp.broadcast_to(line, (ROWS, 2 * ROWS))
        r.bias[h] = pltpu.roll(rows, 0, 1, stride=1, stride_axis=0)[:, :ROWS]
    r.gain_grad[...] = jnp.zeros_like(r.gain_grad)

    def normalise(p):
        for at in strips():
            x = r.tok[p, at].astype(F32)
            r.out_sum[p, at] = x * inverse_rms(x) * r.gains[0:1, :]

    loop(0, count, normalise)
    local(r.buckets.at[0], r.bucket_rows, 5).wait()
    if direct:
        gather.arrived(0)

    def lanes(c, j):
        return slice(c * width + j * PAIR, c * width + (j + 1) * PAIR)

    def settle(p):
        pair.wait(p)
        for at in strips():
            r.hidden[p, at] = r.tok[p, at].astype(F32) + pair.rows(p, at)

    def attend(p):
        normed = r.out_sum[p].astype(BF)
        normed_slot, proj_slot, probs_slot, ctx_slot = (
            stream.slot(p) for stream in (normed_out, proj, probs, ctx)
        )
        normed_slot[...] = normed
        proj_slot[...] = dot(normed, r.wi[...]).astype(BF)
        valid = r.bucket_rows[pl.ds(p, 1), :] < BUCKETS
        masked = jnp.concatenate(
            [jnp.where(valid, 0.0, masked_score), jnp.full((1, ROWS - PLEN), masked_score, F32)], axis=1
        )
        pairs = [[proj_slot[:, lanes(c, j)] for c in range(3)] for j in range(heads // 2)]
        products = [dot(of_head(h, pairs[h // 2][0]), pairs[h // 2][1], 1, 1) for h in range(heads)]
        weighted = []
        for h in range(heads):
            parts = []
            for at in strips(64):
                sc = products[h][at] + r.bias[h, at] + masked
                e_ = jnp.exp(sc - jnp.max(sc, axis=-1, keepdims=True))
                parts.append((e_ * (1.0 / jnp.sum(e_, axis=-1, keepdims=True))).astype(BF))
                probs_slot[h, at] = parts[-1]
            weighted.append(jnp.concatenate(parts, axis=0))
        results = [dot(weighted[h], pairs[h // 2][2]) for h in range(heads)]
        for j in range(heads // 2):
            ctx_slot[:, lanes(0, j)] = either(results[2 * j], results[2 * j + 1]).astype(BF)
        if direct:

            @pl.when(p == 0)
            def _():
                gather.arrived(1)
                rows = r.own_o.shape[0]
                wide = r.acc_r
                for d in range(n):
                    block = r.wo_wide[d * rows_o : (d + 1) * rows_o, :].astype(F32)
                    wide[d * rows : (d + 1) * rows, :] = block[:rows]
                r.wo[...] = wide[: n * rows, :].astype(BF)

            every(p, (
                (0, gather.along, 2), (0, gather.along, 3), (0, gather.own, 4), (1, gather.across, 2),
                (1, gather.own, 5), (2, gather.across, 3), (2, gather.share, 2), (3, gather.share, 3),
                (3, gather.along, 4), (4, gather.along, 5), (4, gather.own, 6), (5, gather.across, 4),
                (5, gather.own, 7), (6, gather.across, 5), (6, gather.share, 4), (7, gather.share, 5),
            ))
        pair.put(p, dot(ctx_slot[...], r.wo[...]))
        pl.when(p >= LAG)(lambda: settle(p - LAG))
        pair.send(p)
        for stream in (normed_out, proj, probs, ctx):
            stream.start(p)

    loop(0, count, attend)

    if direct:
        gather.arrived(2)
        gather.arrived(3)
        local(r.wi, r.wi_out, 1).start()
        local(r.wo, r.wo_out, 2).start()

    def clear():
        r.acc_r[...] = jnp.zeros_like(r.acc_r)
        r.acc_e[...] = jnp.zeros_like(r.acc_e)

    def normed_two(p):
        parts = []
        for at in strips():
            h = r.hidden[p, at]
            parts.append((h * inverse_rms(h) * r.gains[1:2, :]).astype(BF))
        return jnp.concatenate(parts, axis=0)

    def inner_part(normed, c, we, wr):
        u_all, in_all = dot(normed, we[...]), dot(c, wr[...], 1, 1)
        acts, backs = [], []
        for at in strips():
            u = u_all[at]
            square = u * u
            t = jnp.tanh(u * (gelu_root + (gelu_root * gelu_cube) * square))
            half = 0.5 * (1.0 + t)
            acts.append((u * half).astype(BF))
            slope = half + (0.5 * u) * (1.0 - t * t) * (
                gelu_root + (3.0 * gelu_root * gelu_cube) * square
            )
            backs.append((in_all[at] * slope).astype(BF))
        return jnp.concatenate(acts, axis=0), jnp.concatenate(backs, axis=0)

    def outer_part(normed, c, act, back, we, wr):
        r.acc_r[...] += dot(act, c, 0, 0)
        r.acc_e[...] += dot(normed, back, 0, 0)
        return dot(act, wr[...]), dot(back, we[...], 1, 1)

    def staged(stage_r, stage_e):
        stage_r[...] = r.acc_r[...].astype(BF)
        stage_e[...] = r.acc_e[...].astype(BF)

    def first(p):
        normed, c = normed_two(p), r.cot[p]
        act, back = inner_part(normed, c, r.we_a, r.wr_a)
        r.out_sum[p], r.in_sum[p] = outer_part(normed, c, act, back, r.we_a, r.wr_a)

        @pl.when(p == 0)
        def _():
            for last in range(count - LAG, count):
                settle(last)

        if direct:
            every(p, (
                (0, gather.along, 6), (1, gather.along, 7), (2, gather.across, 6), (3, gather.across, 7),
                (4, gather.share, 6), (5, gather.share, 7),
            ))

    clear()
    loop(0, count, first)
    staged(r.stage_ra, r.stage_ea)
    if direct:
        sums.far(0)
        sums.far(1)
        gather.arrived(4)
        gather.arrived(5)
    clear()

    def middle(p):
        normed, c = normed_two(p), r.cot[p]
        act, back = inner_part(normed, c, r.we_b, r.wr_b)
        r_part, n_part = outer_part(normed, c, act, back, r.we_b, r.wr_b)
        r.out_sum[p] += r_part
        r.in_sum[p] += n_part
        if direct:
            every(p, ((1, sums.plain, 0), (1, sums.plain, 1), (4, sums.near, 0), (6, sums.near, 1)))

    loop(0, count, middle)
    staged(r.stage_rb, r.stage_eb)
    if direct:
        sums.far(2)
        sums.far(3)
        sums.plain(2)
        sums.plain(3)
        gather.arrived(6)
        gather.arrived(7)
    clear()

    def finish(last):
        layer_slot, grad_slot = layer.slot(last), hidden_grad.slot(last)
        pair.wait(count + last)
        back_in.wait(last)
        gain_rows = jnp.zeros((1, r.gains.shape[1]), F32)
        for at in strips():
            h = r.hidden[last, at]
            layer_slot[at] = (h + pair.rows(count + last, at)).astype(BF)
            grad = back_in.rows(last, at)
            inv = inverse_rms(h)
            hr = h * inv
            gain_rows += jnp.sum(grad * hr, axis=0, keepdims=True)
            zed = r.gains[1:2, :] * grad
            inner = jnp.mean(zed * hr, axis=-1, keepdims=True)
            grad_slot[at] = r.cot[last, at].astype(F32) + inv * (zed - hr * inner)
        r.gain_grad[0:1, :] += gain_rows

    def last_part(p, with_finish=True):
        normed, c = normed_two(p), r.cot[p]
        act, back = inner_part(normed, c, r.we_c, r.wr_c)
        if with_finish:
            finish(p - LAG)
        r_part, n_part = outer_part(normed, c, act, back, r.we_c, r.wr_c)
        pair.put(count + p, r.out_sum[p] + r_part)
        back_in.put(p, r.in_sum[p] + n_part)
        pair.send(count + p)
        back_in.send(p)
        if with_finish:
            for stream in (layer, hidden_grad):
                stream.start(p - LAG)
            if direct:
                for a, at in ((0, 2), (1, 3)):
                    pl.when(p == at)(partial(sums.along, a, kept[a]))
                every(p, ((4, sums.near, 2), (5, sums.near, 3)))

    loop(0, LAG, lambda p: last_part(p, False))
    loop(LAG, count, last_part)
    stage_rc, stage_ec = (r.wr_c, r.we_c) if direct else (r.stage_rc, r.stage_ec)
    if direct:
        gather.sent(6)
        gather.sent(7)
    staged(stage_rc, stage_ec)
    local(stage_rc, r.grad_r, 3).start()
    local(stage_ec, r.grad_e, 4).start()
    if direct:
        for a, held in ((2, r.held_rb), (3, r.held_eb)):
            held[0] = jnp.zeros(held.shape[1:], BF)
            sums.along(a, kept[a], held)
    for p in range(count - LAG, count):
        finish(p)
        for stream in (layer, hidden_grad):
            stream.start(p)
    if direct:
        for a in range(2):
            sums.total(a, kept[a])
        for a in range(6):
            gather.sent(a)
        for a in range(4):
            sums.sent(a, a >= 2)
        local(r.wi, r.wi_out, 1).wait()
        local(r.wo, r.wo_out, 2).wait()
    local(r.tok, r.tok_out, 0).wait()
    local(stage_rc, r.grad_r, 3).wait()
    local(stage_ec, r.grad_e, 4).wait()
    for stream in (normed_out, proj, probs, ctx, layer, hidden_grad):
        stream.last()


def dot_exact(a, b):
    return lax.dot_general(
        a, b, (((1,), (1,)), ((), ())), precision=lax.Precision.HIGHEST, preferred_element_type=F32
    )


def forward(n, passages, heads, direct, tokens, cotangent, buckets, gains, table, onehot, weights):
    d = tokens.shape[1]
    width = heads * DH
    ins = [("tokens", tokens, ANY), ("cotangent", cotangent, ANY)]
    ins += [("buckets", buckets, ANY)]
    ins += [(k, v, VMEM) for k, v in (("gains", gains), ("table", table), ("onehot", onehot))]
    ins += [(k, v, VMEM) for k, v in weights.items()]
    if direct:
        part = weights["own_r"].shape[0] // 3 * n
    else:
        part = weights["wr_a"].shape[0]
    streams = dict(
        proj=((ROWS, 3 * width), BF),
        probs=((heads, ROWS, ROWS), BF),
        normed=((ROWS, d), BF),
        ctx=((ROWS, width), BF),
        layer=((ROWS, d), BF),
        hidden_grad=((ROWS, d), F32),
    )
    outs = [(k, (passages,) + shape, dtype, ANY) for k, (shape, dtype) in streams.items()]
    outs += [
        ("tok_out", (passages, ROWS, d), BF, ANY),
        ("grad_r", (part, d), BF, ANY),
        ("grad_e", (d, part), BF, ANY),
        ("gain_grad", (8, d), F32, VMEM),
    ]
    scratch = [*dict(
        tok=pltpu.VMEM((passages, ROWS, d), BF),
        cot=pltpu.VMEM((passages, ROWS, d), BF),
        window=pltpu.VMEM((2, WINDOW, d), BF),
        window_sem=pltpu.SemaphoreType.DMA((2,)),
        bucket_rows=pltpu.VMEM(buckets.shape[1:], buckets.dtype),
        out_sem=pltpu.SemaphoreType.DMA((6,)),
        bias=pltpu.VMEM((heads, ROWS, ROWS), F32),
        hidden=pltpu.VMEM((passages, ROWS, d), F32),
        out_sum=pltpu.VMEM((passages, ROWS, d), F32),
        in_sum=pltpu.VMEM((passages, ROWS, d), F32),
        acc_r=pltpu.VMEM((part, d), F32),
        acc_e=pltpu.VMEM((d, part), F32),
    ).items()]
    for k, (shape, dtype) in streams.items():
        scratch += stream_scratch(k, shape, dtype)
    for name in ("pair", "in"):
        scratch += swap_scratch(name, d)
    stage = [("r" + half, (part, d)) for half in "ab"] + [("e" + half, (d, part)) for half in "ab"]
    if direct:
        nz = n // 4
        padded = weights["own_o"].shape[0]
        padded += -padded % 16
        outs += [("wi_out", (d, 3 * width), BF, ANY), ("wo_out", (width, d), BF, ANY)]
        for key, shape in stage:
            block = (shape[0] // n, shape[1])
            outs.append(("sum_" + key, block, F32, VMEM))
            if key[1] == "b":
                outs.append(("held_" + key, (nz,) + block, BF, VMEM))
            scratch.append(("stage_" + key, pltpu.VMEM(shape, BF)))
            scratch.append(("buf_" + key, pltpu.VMEM((4, nz) + block, BF)))
        shapes = {"wi": (d, 3 * width), "wo": (width, d), "wo_wide": (n * padded, d)}
        for third in "abc":
            shapes["we_" + third], shapes["wr_" + third] = (d, part), (part, d)
        scratch += [(key, pltpu.VMEM(shape, BF)) for key, shape in shapes.items()]
        scratch += [*dict(
            g_ss=pltpu.SemaphoreType.DMA((8, 5, nz)),
            g_rs=pltpu.SemaphoreType.DMA((8, 5, nz)),
            s_ss=pltpu.SemaphoreType.DMA((4, 4, nz)),
            s_rs=pltpu.SemaphoreType.DMA((4, 4, nz)),
        ).items()]
    else:
        outs += [("stage_" + k, shape, BF, VMEM) for k, shape in stage]
        scratch += [("stage_rc", pltpu.VMEM((part, d), BF)), ("stage_ec", pltpu.VMEM((d, part), BF))]
    kernel = partial(forward_kernel, n, passages, heads, direct)
    return run(kernel, ins, outs, scratch, 1, 63, "forward")


def back_kernel(n, passages, heads, direct, r):
    width = heads * DH
    count = passages
    swap = swap_of(r, "in")
    if direct:
        links = Links(n)
        refs = [r.grad_r, r.grad_e, r.stage_o, r.stage_v, r.stage_qk]
        grads = [(g, g.shape[0] // n) for g in refs]
        names = ["r", "e", "o", "v", "qk"]
        bufs = [getattr(r, "buf_" + k) for k in names]
        kept = [getattr(r, "sum_" + k) for k in names]
        sums = Scatter(links, grads, bufs, r.s_ss, r.s_rs)
        late = [
            remote(held.at[k], land.at[k], r.c_ss.at[i, k], r.c_rs.at[i, k], {"dp": links.z_peer(k)})
            for i, (held, land) in enumerate(((r.held_rb, r.land_rb), (r.held_eb, r.land_eb)))
            for k in range(1, links.nz)
        ]
        wide = Spread(links, r.wide, r.wide_z, r.wide_xy, r.wide_mp, r.w_ss, r.w_rs)
    ctx, normed, probs, proj, tok, hidden_grad = (
        Load(r, name) for name in ("ctx", "normed", "probs", "proj", "tok", "hidden_grad")
    )
    input_grad = Drain(r, "input_grad")

    for p in range(count):
        for stream in (hidden_grad, ctx, probs, normed):
            stream.copy(p).start()
    for stream in (proj, tok):
        stream.start()
    if direct:
        greet(links.peers() + [{"dp": links.far_peer}, partner()])
        for copy in late:
            copy.start()
        sums.far(0)
        sums.far(1)
    else:
        greet([partner()])
    r.acc_o[...] = jnp.zeros_like(r.acc_o)
    r.acc_s[...] = jnp.zeros_like(r.acc_s)
    r.acc_v[...] = jnp.zeros_like(r.acc_v)
    r.acc_qk[...] = jnp.zeros_like(r.acc_qk)

    def lanes(c, j):
        return slice(c * width + j * PAIR, c * width + (j + 1) * PAIR)

    def values(p):
        for stream in (hidden_grad, ctx, probs, normed):
            stream.wait(p)
        top = hidden_grad.buf[p].astype(BF)
        r.acc_o[...] += dot(ctx.buf[p], top, 0, 0)
        dctx = dot(top, r.wo[...], 1, 1).astype(BF)
        r.dctx[p] = dctx
        results = [dot(probs.buf[p, h], dctx[:, lanes(0, h // 2)], 0, 0) for h in range(heads)]
        dv = [either(results[2 * j], results[2 * j + 1]) for j in range(heads // 2)]
        dv = jnp.concatenate(dv, axis=1).astype(BF)
        r.dproj[p, :, 2 * width :] = dv
        r.acc_v[...] += dot(normed.buf[p], dv, 0, 0)
        if direct:
            every(p, (
                (1, sums.plain, 0), (1, sums.plain, 1), (4, sums.near, 0), (6, sums.near, 1),
            ))

    loop(0, count, values)
    blocks = n if direct else 1
    rows = r.acc_o.shape[0] // blocks
    padded = r.stage_o.shape[0] // blocks
    for b in range(blocks):
        part = r.acc_o[b * rows : (b + 1) * rows, :]
        if padded > rows:
            part = jnp.concatenate([part, jnp.zeros((padded - rows, part.shape[1]), F32)], axis=0)
        r.stage_o[b * padded : (b + 1) * padded, :] = part.astype(BF)
    r.stage_v[...] = r.acc_v[...].astype(BF)
    if direct:
        sums.far(2)
        sums.far(3)

    def scores(p):
        proj.wait(p)
        pairs = [[proj.buf[p, :, lanes(c, j)] for c in range(3)] for j in range(heads // 2)]
        products = [
            dot(of_head(h, r.dctx[p, :, lanes(0, h // 2)]), pairs[h // 2][2], 1, 1) for h in range(heads)
        ]
        ds = []
        for h in range(heads):
            parts = []
            for rows in strips(64):
                a = probs.buf[p, h, rows].astype(F32)
                dp = products[h][rows]
                centre = jnp.sum(a * dp, axis=-1, keepdims=True)
                parts.append((a * (dp - centre)).astype(BF))
                r.acc_s[h, rows] += parts[-1].astype(F32)
            ds.append(jnp.concatenate(parts, axis=0))
        dq = [dot(ds[h], pairs[h // 2][1]) for h in range(heads)]
        dk = [dot(ds[h], pairs[h // 2][0], 0, 0) for h in range(heads)]
        for j in range(heads // 2):
            r.dproj[p, :, lanes(0, j)] = either(dq[2 * j], dq[2 * j + 1]).astype(BF)
            r.dproj[p, :, lanes(1, j)] = either(dk[2 * j], dk[2 * j + 1]).astype(BF)
        r.acc_qk[...] += dot(normed.buf[p], r.dproj[p, :, : 2 * width], 0, 0)
        if direct:
            every(p, ((0, sums.plain, 2), (0, sums.plain, 3)))
            for a, at in ((0, 2), (1, 4)):
                pl.when(p == at)(partial(sums.along, a, kept[a]))
            every(p, ((3, sums.near, 2), (5, sums.near, 3)))

    loop(0, count, scores)
    r.stage_qk[...] = r.acc_qk[...].astype(BF)
    if direct:
        sums.far(4)
    terms = jnp.sum(r.acc_v[...] * r.wi[:, 2 * width :].astype(F32), axis=1, keepdims=True)
    terms += jnp.sum(r.acc_qk[...] * r.wi[:, : 2 * width].astype(F32), axis=1, keepdims=True)
    r.wide[...] = jnp.zeros_like(r.wide)
    r.wide[heads : heads + 1, :] = 0.5 * r.gain_two[0:1, :]
    r.wide[heads + 1 : heads + 2, :] = terms.T / r.gains[0:1, :]
    for h in range(heads):
        lines = jnp.concatenate([r.acc_s[h], jnp.zeros((ROWS, ROWS), F32)], axis=1)
        while lines.shape[0] > 1:
            half = lines.shape[0] // 2
            lines = lines[:half] + pltpu.roll(lines[half:], 2 * ROWS - half, 1)
        r.wide[h : h + 1, : 2 * ROWS] = lines
    if direct:
        wide.along()
        sums.plain(4)

    def finish(last):
        tok.wait(last)
        slot = input_grad.slot(last)
        swap.wait(last)
        for at in strips():
            x = tok.buf[last, at].astype(F32)
            inv = inverse_rms(x)
            xr = x * inv
            zed = r.gains[0:1, :] * swap.rows(last, at)
            inner = jnp.mean(zed * xr, axis=-1, keepdims=True)
            slot[at] = hidden_grad.buf[last, at] + inv * (zed - xr * inner)

    def inputs(t, with_finish=True):
        terms = dot(r.dproj[t, :, : 2 * width], r.wi[:, : 2 * width], 1, 1)
        if with_finish:
            finish(t - LAG)
        terms += dot(r.dproj[t, :, 2 * width :], r.wi[:, 2 * width :], 1, 1)
        swap.put(t, terms)
        swap.send(t)
        if with_finish:
            input_grad.start(t - LAG)
            if direct:
                every(t, ((4, sums.near, 4),))
                pl.when(t == 7)(partial(sums.along, 4, kept[4]))
                for a, at in ((2, 2), (3, 3)):
                    pl.when(t == at)(partial(sums.along, a, kept[a]))
                pl.when(t == 2)(wide.across)
                pl.when(t == 5)(wide.over)

    loop(0, LAG, lambda t: inputs(t, False))
    loop(LAG, count, inputs)
    if direct:
        for copy in late:
            copy.wait()
        for part, land, target in (
            (r.part_rb, r.land_rb, r.sum_rb), (r.part_eb, r.land_eb, r.sum_eb),
        ):
            total = part[...]
            for k in range(1, links.nz):
                total += land[k].astype(F32)
            target[...] = total
        for a in range(4):
            sums.total(a, kept[a])
    for p in range(count - LAG, count):
        finish(p)
        input_grad.start(p)
    if direct:
        r.wide_sum[...] = wide.total(heads)
        sums.total(4, kept[4])
        for a in range(5):
            sums.sent(a)
    else:
        r.wide_sum[...] = r.wide[...]
    input_grad.last()


def back(n, passages, heads, direct, f, gains, wi, wo):
    d = gains.shape[1]
    width = heads * DH
    streams = dict(
        ctx=((ROWS, width), BF),
        normed=((ROWS, d), BF),
        probs=((heads, ROWS, ROWS), BF),
        proj=((ROWS, 3 * width), BF),
        tok=((ROWS, d), BF),
        hidden_grad=((ROWS, d), F32),
    )
    ins = [(k, f.tok_out if k == "tok" else getattr(f, k), ANY) for k in streams]
    fixed = [("gains", gains), ("wi", wi), ("wo", wo), ("gain_two", f.gain_grad)]
    outs = [
        ("input_grad", (passages, ROWS, d), F32, ANY),
        ("wide_sum", (8, d), F32, VMEM),
    ]
    scratch = [*dict(
        acc_qk=pltpu.VMEM((d, 2 * width), F32),
        acc_v=pltpu.VMEM((d, width), F32),
        acc_o=pltpu.VMEM((width, d), F32),
        acc_s=pltpu.VMEM((heads, ROWS, ROWS), F32),
        dctx=pltpu.VMEM((passages, ROWS, width), BF),
        dproj=pltpu.VMEM((passages, ROWS, 3 * width), BF),
        wide=pltpu.VMEM((8, d), F32),
    ).items()] + swap_scratch("in", d)
    for k, (shape, dtype) in streams.items():
        scratch.append((k + "_buf", pltpu.VMEM((passages,) + shape, dtype)))
        scratch.append((k + "_sem", pltpu.SemaphoreType.DMA((passages,))))
    scratch += stream_scratch("input_grad", (ROWS, d), F32)
    rows_o = width
    if direct:
        rows_o = width // n
        rows_o = (rows_o + -rows_o % 16) * n
    stage = [("stage_o", (rows_o, d)), ("stage_v", (d, width)), ("stage_qk", (d, 2 * width))]
    if direct:
        nz = n // 4
        fixed += [(k, getattr(f, k)) for k in ("grad_r", "grad_e", "held_rb", "held_eb")]
        fixed += [("part_rb", f.sum_rb), ("part_eb", f.sum_eb)]
        for key, shape in (("rb", f.sum_rb.shape), ("eb", f.sum_eb.shape)):
            outs.append(("sum_" + key, shape, F32, VMEM))
            scratch.append(("land_" + key, pltpu.VMEM((nz,) + shape, BF)))
        scratch += [(k, pltpu.VMEM(shape, BF)) for k, shape in stage]
        blocks = {"r": f.grad_r.shape, "e": f.grad_e.shape}
        blocks.update({k[6:]: shape for k, shape in stage})
        for key, shape in blocks.items():
            shape = (shape[0] // n, shape[1])
            scratch.append(("buf_" + key, pltpu.VMEM((4, nz) + shape, BF)))
            outs.append(("sum_" + key, shape, F32, VMEM))
        scratch += [*dict(
            wide_z=pltpu.VMEM((nz, 8, d), F32),
            wide_xy=pltpu.VMEM((4, 8, d), F32),
            wide_mp=pltpu.VMEM((8, d), F32),
            c_ss=pltpu.SemaphoreType.DMA((2, nz)),
            c_rs=pltpu.SemaphoreType.DMA((2, nz)),
            s_ss=pltpu.SemaphoreType.DMA((len(blocks), 4, nz)),
            s_rs=pltpu.SemaphoreType.DMA((len(blocks), 4, nz)),
            w_ss=pltpu.SemaphoreType.DMA((2, max(nz, 4))),
            w_rs=pltpu.SemaphoreType.DMA((2, max(nz, 4))),
        ).items()]
    else:
        outs += [(k, shape, BF, VMEM) for k, shape in stage]
    ins += [(k, v, VMEM) for k, v in fixed]
    kernel = partial(back_kernel, n, passages, heads, direct)
    return run(kernel, ins, outs, scratch, 2, 63, "back")


rates = {
    "i": rate_inward, "o": rate_outward, "e": rate_expand, "r": rate_reduce, "g": rate_gains, "t": rate_table,
}


def update_kernel(n, passages, heads, keys, r):
    total = r.layer_out.shape[0]
    ins = [(getattr(r, k), getattr(r, k + "_in")) for k in keys]
    fetch = {k: pltpu.make_async_copy(a, b, r.in_sem.at[i]) for i, (k, (a, b)) in enumerate(zip(keys, ins))}
    stores = []

    def store(src, dst):
        copy = pltpu.make_async_copy(src, dst, r.out_sem.at[len(stores)])
        copy.start()
        stores.append(copy)

    def passage(name, p, sem):
        return pltpu.make_async_copy(getattr(r, name).at[p], getattr(r, name + "_in").at[p], sem.at[p])

    for k in keys:
        fetch[k].start()
    for p in range(passages):
        passage("grad", p, r.grad_sem).start()
        passage("layer", p, r.layer_sem).start()

    def get(k):
        fetch[k].wait()
        return getattr(r, k + "_in")

    def step(key, gradient, at=...):
        out = adamw(*(getattr(r, key + part + "_in")[at] for part in "wmv"), gradient, rates[key])
        for part, value in zip(("_nw", "_nm", "_nv"), out):
            getattr(r, key + part + "_out")[at] = value
        if key not in "gt":
            getattr(r, key + "_nc_out")[at] = out[0].astype(BF)

    def ready(key):
        for part in "wmv":
            fetch[key + part].wait()

    def done(key):
        for part in ("_nw", "_nm", "_nv") + ("_nc",) * (key not in "gt"):
            store(getattr(r, key + part + "_out"), getattr(r, key + part))

    pieces_r, pieces_e = ([get(key + third) for third in "abc"] for key in "re")
    ready("r")
    third = pieces_r[0].shape[0]
    for i, piece in enumerate(pieces_r):
        step("r", piece[...], slice(i * third, (i + 1) * third))
    done("r")
    ready("e")
    columns = [piece[:, d * third : (d + 1) * third] for d in range(n) for piece in pieces_e]
    step("e", jnp.concatenate(columns, axis=1))
    done("e")
    ready("o")
    step("o", get("sum_o")[: r.ow_in.shape[0]])
    done("o")
    ready("i")
    qk, v = get("sum_qk"), get("sum_v")
    width = v.shape[1]
    step("i", qk[:, :width], 0)
    step("i", qk[:, width:], 1)
    step("i", v[...], 2)
    done("i")
    ready("g")
    small = get("small")
    step("g", small[heads + 1 : heads + 2], slice(0, 1))
    step("g", small[heads : heads + 1], slice(1, 2))
    done("g")
    ready("t")
    onehot = get("onehot")
    step("t", lax.dot_general(
        small[:heads, : 2 * ROWS], onehot[...], (((1,), (0,)), ((), ())),
        precision=lax.Precision.HIGHEST, preferred_element_type=F32,
    ))
    done("t")
    sent = 0
    for p in range(passages):
        at = slice(p * PLEN, (p + 1) * PLEN)
        passage("grad", p, r.grad_sem).wait()
        r.grad_rows[at] = r.grad_in[p, :PLEN]
        passage("layer", p, r.layer_sem).wait()
        r.layer_wide[at] = r.layer_in[p, :PLEN].astype(F32)
        end = total if p == passages - 1 else (p + 1) * PLEN // 16 * 16
        rows = slice(sent, end)
        store(r.grad_rows.at[rows], r.input_grad.at[rows])
        r.layer_rows[rows] = r.layer_wide[rows].astype(BF)
        store(r.layer_rows.at[rows], r.layer_out.at[rows])
        sent = end
    for copy in stores:
        copy.wait()


def update(n, passages, heads, shape, f, b, onehot, states):
    total, d = shape
    small = dict(ra=f.sum_ra, rb=b.sum_rb, rc=b.sum_r, ea=f.sum_ea, eb=b.sum_eb, ec=b.sum_e)
    ins = [(k, v) for k, v in small.items()]
    ins += [(key + part, a) for key in "reo" for part, a in zip("wmv", states[key])]
    ins += [("sum_o", b.sum_o), ("sum_qk", b.sum_qk), ("sum_v", b.sum_v)]
    ins += [("small", b.wide_sum), ("onehot", onehot)]
    ins += [(key + part, a) for key in "igt" for part, a in zip("wmv", states[key])]
    keys = [k for k, _ in ins]
    scratch = [(k + "_in", pltpu.VMEM(a.shape, a.dtype)) for k, a in ins]
    outs = []
    for key in "ioergt":
        for part in ("_nw", "_nm", "_nv") + ("_nc",) * (key not in "gt"):
            outs.append((key + part, states[key][0].shape, BF if part == "_nc" else F32, ANY))
    scratch += [(k + "_out", pltpu.VMEM(dims, dtype)) for k, dims, dtype, _ in outs]
    padded = (passages, ROWS, d)
    count = len(outs) + 2 * passages
    scratch += [*dict(
        grad_in=pltpu.VMEM(padded, F32),
        layer_in=pltpu.VMEM(padded, BF),
        grad_rows=pltpu.VMEM((total, d), F32),
        layer_wide=pltpu.VMEM((total, d), F32),
        layer_rows=pltpu.VMEM((total, d), BF),
        in_sem=pltpu.SemaphoreType.DMA((len(keys),)),
        out_sem=pltpu.SemaphoreType.DMA((count,)),
        grad_sem=pltpu.SemaphoreType.DMA((passages,)),
        layer_sem=pltpu.SemaphoreType.DMA((passages,)),
    ).items()]
    ins += [("layer", f.layer), ("grad", b.input_grad)]
    outs += [("layer_out", shape, BF, ANY), ("input_grad", shape, F32, ANY)]
    kernel = partial(update_kernel, n, passages, heads, keys)
    o = run(kernel, [(k, a, ANY) for k, a in ins], outs, scratch, None, 60, "update")
    new = [o.layer_out, o.input_grad]
    for key in "ioergt":
        for part in ("_nw", "_nm", "_nv") + ("_nc",) * (key not in "gt"):
            value = getattr(o, key + part)
            if key == "i":
                value = value.transpose(1, 0, 2)
            new.append(value.T if key == "t" else value)
    return tuple(new)


def shards(
    n,
    tokens,
    cotangent,
    buckets,
    inward_master,
    inward_first,
    inward_second,
    outward_master,
    outward_first,
    outward_second,
    expand_master,
    expand_first,
    expand_second,
    reduce_master,
    reduce_first,
    reduce_second,
    gains_master,
    gains_first,
    gains_second,
    table_master,
    table_first,
    table_second,
):
    d = tokens.shape[1]
    passages = tokens.shape[0] // PLEN
    heads = inward_master.shape[2] // DH
    width = heads * DH
    rows_i, rows_r = inward_master.shape[0], reduce_master.shape[0]
    units = expand_master.shape[1]
    direct = n % 8 == 0 and rows_i % 16 == 0 and rows_r % 48 == 0 and outward_master.shape[0] % 8 == 0

    onehot = jnp.asarray(distance_onehot())
    bucket_rows = buckets.transpose(1, 0, 2)
    table_rows = table_master.T
    if direct:
        weights = dict(
            own_i=inward_master.transpose(1, 0, 2),
            own_o=outward_master,
            own_e=expand_master,
            own_r=reduce_master,
        )
    else:
        masters = (inward_master.reshape(-1, 3 * width), outward_master, expand_master, reduce_master)
        wi, wo, we, wr = (
            lax.all_gather(w.astype(BF), "dp", axis=0, tiled=True) for w in masters
        )
        cuts = [slice(i * units // 3, (i + 1) * units // 3) for i in range(3)]
        weights = {"wi": wi, "wo": wo}
        for third, at in zip("abc", cuts):
            weights["we_" + third], weights["wr_" + third] = we[:, at], wr[at]
    f = forward(
        n, passages, heads, direct, tokens, cotangent, bucket_rows, gains_master, table_rows, onehot, weights
    )
    if direct:
        wi, wo = f.wi_out, f.wo_out
    b = back(n, passages, heads, direct, f, gains_master, wi, wo)

    def scatter(g):
        return lax.psum_scatter(g.astype(F32), "dp", scatter_dimension=0, tiled=True)

    if direct:
        states = dict(
            i=tuple(a.transpose(1, 0, 2) for a in (inward_master, inward_first, inward_second)),
            o=(outward_master, outward_first, outward_second),
            e=(expand_master, expand_first, expand_second),
            r=(reduce_master, reduce_first, reduce_second),
            g=(gains_master, gains_first, gains_second),
            t=(table_master.T, table_first.T, table_second.T),
        )
        return update(n, passages, heads, tokens.shape, f, b, onehot, states)
    else:
        inward_sum = scatter(jnp.concatenate([b.stage_qk, b.stage_v], axis=1))
        outward_sum = scatter(b.stage_o)
        expand_sum = scatter(jnp.concatenate([f.stage_ea, f.stage_eb, f.grad_e], axis=1))
        reduce_sum = scatter(jnp.concatenate([f.stage_ra, f.stage_rb, f.grad_r], axis=0))
        wide_sum = lax.psum(b.wide_sum, "dp")
        gains = lax.psum(wide_sum[heads : heads + 2], "mp")
        wide_sum = jnp.concatenate([wide_sum[:heads], gains], axis=0)
    inward_sum = inward_sum.reshape(inward_master.shape)
    gains_sum = jnp.concatenate([wide_sum[heads + 1 : heads + 2], wide_sum[heads : heads + 1]], axis=0)
    table_sum = lax.dot_general(
        onehot.T, wide_sum[:heads, : 2 * ROWS], (((1,), (1,)), ((), ())), precision=lax.Precision.HIGHEST
    )

    layer_out = f.layer[:, :PLEN].reshape(tokens.shape)
    input_grad = b.input_grad[:, :PLEN].reshape(tokens.shape)
    outputs = [layer_out, input_grad]
    for w, first_moment, second_moment, gradient, rate, copied in (
        (inward_master, inward_first, inward_second, inward_sum, rate_inward, True),
        (outward_master, outward_first, outward_second, outward_sum, rate_outward, True),
        (expand_master, expand_first, expand_second, expand_sum, rate_expand, True),
        (reduce_master, reduce_first, reduce_second, reduce_sum, rate_reduce, True),
        (gains_master, gains_first, gains_second, gains_sum, rate_gains, False),
        (table_master, table_first, table_second, table_sum, rate_table, False),
    ):
        new = adamw(w, first_moment, second_moment, gradient, rate)
        outputs += list(new)
        if copied:
            outputs.append(new[0].astype(BF))
    return tuple(outputs)


def solution(mesh):
    rows = P("dp", None)
    inward = P("dp", None, "mp")
    tall = P(("mp", "dp"), None)
    wide = P("dp", "mp")
    table = P(None, "mp")
    return jax.shard_map(
        partial(shards, mesh.shape["dp"]),
        mesh=mesh,
        in_specs=(rows, rows, P("dp", None, None))
        + (inward,) * 3
        + (tall,) * 3
        + (wide,) * 3
        + (tall,) * 3
        + (P(),) * 3
        + (table,) * 3,
        out_specs=(rows, rows)
        + (inward,) * 4
        + (tall,) * 4
        + (wide,) * 4
        + (tall,) * 4
        + (P(),) * 3
        + (table,) * 3,
        check_vma=False,
    )
```

```python
from functools import partial
import math

import jax
import jax.numpy as jnp
import numpy as np
from jax import lax
from jax.experimental import pallas as pl
from jax.experimental.pallas import tpu as pltpu
from jax.sharding import PartitionSpec as P

DH = 64
PLEN = 250
STEP = 5
ROWS = 256
BUCKETS = 32
SPAN = 128

MESH = pl.DeviceIdType.MESH
BF = jnp.bfloat16
F32 = jnp.float32
MIB = 2**20

norm_eps = 1e-06
masked_score = -1000000000.0
beta_first = 0.5
beta_second = 0.5
adam_eps = 1e-08
decay_rate = 0.01
rate_inward = 0.015
rate_outward = 0.3
rate_expand = 0.04
rate_reduce = 0.02
rate_gains = 0.5
rate_table = 0.5


def adamw(weight, first_moment, second, gradient, step_rate):
    new_first = beta_first * first_moment + (1.0 - beta_first) * gradient
    new_second = beta_second * second + (1.0 - beta_second) * gradient * gradient
    first_hat = new_first / (1.0 - beta_first**STEP)
    second_hat = new_second / (1.0 - beta_second**STEP)
    new_weight = weight - step_rate * (
        first_hat / (jnp.sqrt(second_hat) + adam_eps) + decay_rate * weight
    )
    return (new_weight, new_first, new_second)


def distance_onehot():
    span = 2 * ROWS
    relative = np.arange(span)
    relative = np.where(relative < ROWS, relative, relative - span)
    half = BUCKETS // 2
    exact = half // 2
    distance = np.abs(relative)
    far = np.full_like(distance, exact)
    for level in range(1, half - exact):
        far += distance >= math.ceil(exact * (SPAN / exact) ** (level / (half - exact)))
    bucket = np.where(relative > 0, half, 0) + np.where(distance < exact, distance, far)
    return (bucket[:, None] == np.arange(BUCKETS)[None]).astype(np.float32)


def dot(a, b, ca=1, cb=0):
    return lax.dot_general(a, b, (((ca,), (cb,)), ((), ())), preferred_element_type=F32)


class Refs:
    pass


def run(kernel, ins, outs, scratch, collective, limit, name):
    names = [i[0] for i in ins] + [o[0] for o in outs] + [s[0] for s in scratch]

    def body(*refs):
        space = Refs()
        for key, ref in zip(names, refs, strict=True):
            setattr(space, key, ref)
        kernel(space)

    results = pl.pallas_call(
        body,
        in_specs=[i[2] for i in ins],
        out_specs=[o[3] for o in outs],
        out_shape=[jax.ShapeDtypeStruct(o[1], o[2]) for o in outs],
        scratch_shapes=[s[1] for s in scratch],
        compiler_params=pltpu.CompilerParams(
            collective_id=collective, has_side_effects=collective is not None, vmem_limit_bytes=limit * MIB
        ),
        name=name,
    )(*[i[1] for i in ins])
    space = Refs()
    for out, result in zip(outs, results, strict=True):
        setattr(space, out[0], result)
    return space


ANY = pl.BlockSpec(memory_space=pl.ANY)
VMEM = pl.BlockSpec(memory_space=pltpu.VMEM)


class Load:
    def __init__(self, r, name):
        self.hbm, self.buf, self.sem = (getattr(r, name + part) for part in ("", "_buf", "_sem"))

    def copy(self, p):
        return pltpu.make_async_copy(self.hbm.at[p], self.buf.at[p], self.sem.at[p])

    def start(self):
        for p in range(self.hbm.shape[0]):
            self.copy(p).start()

    def wait(self, p):
        self.copy(p).wait()


class Drain:
    def __init__(self, r, name):
        self.hbm, self.buf, self.sem = (getattr(r, name + part) for part in ("", "_buf", "_sem"))

    def copy(self, p):
        slot = lax.rem(p, 2)
        return pltpu.make_async_copy(self.buf.at[slot], self.hbm.at[p], self.sem.at[slot])

    def slot(self, p):
        pl.when(p >= 2)(lambda: self.copy(p - 2).wait())
        return self.buf.at[lax.rem(p, 2)]

    def start(self, p):
        self.copy(p).start()

    def last(self):
        for p in range(max(self.hbm.shape[0] - 2, 0), self.hbm.shape[0]):
            self.copy(p).wait()


def stream_scratch(name, shape, dtype):
    return [
        (name + "_buf", pltpu.VMEM((2,) + tuple(shape), dtype)),
        (name + "_sem", pltpu.SemaphoreType.DMA((2,))),
    ]


class Links:
    def __init__(self, n):
        me = lax.axis_index("dp")
        self.n, self.nz, self.me = n, n // 4, me
        x, y = lax.rem(me, 2), lax.rem(me // 2, 2)
        self.z, self.column = me // 4, lax.rem(me, 4)
        self.x_peer, self.y_peer = me + 1 - 2 * x, me + 2 - 4 * y
        self.far_peer = self.x_peer + 2 - 4 * y
        self.z_pair = self.z + 1 - 2 * lax.rem(self.z, 2)
        self.pair_peer = self.z_pair * 4 + self.column

    def z_peer(self, k):
        return lax.rem(self.z + k + self.nz, self.nz) * 4 + self.column

    def block(self, k, column_of, z=None):
        return lax.rem((self.z if z is None else z) + k, self.nz) * 4 + lax.rem(column_of, 4)

    def peers(self):
        ids = [self.x_peer, self.y_peer] + [self.z_peer(k) for k in range(1, self.nz)]
        return [{"dp": i} for i in ids]

    def column_peer(self, k):
        return self.z * 4 + lax.rem(self.column + k + 4, 4)


def greet(peers):
    barrier = pltpu.get_barrier_semaphore()
    for peer in peers:
        pl.semaphore_signal(barrier, inc=1, device_id=peer, device_id_type=MESH)
    pl.semaphore_wait(barrier, len(peers))


def partner():
    return {"mp": 1 - lax.axis_index("mp")}


def cut(ref, blk, rows):
    return ref.at[pl.ds(pl.multiple_of(blk * rows, 16), rows)]


def remote(src, dst, send, recv, peer):
    return pltpu.make_async_remote_copy(
        src_ref=src,
        dst_ref=dst,
        send_sem=send,
        recv_sem=recv,
        device_id=peer,
        device_id_type=MESH,
    )


class Gather:
    def __init__(self, links, full, ss, rs, short=()):
        self.l, self.full, self.ss, self.rs, self.short = links, full, ss, rs, short

    def at(self, a, blk):
        ref, rows, lanes = self.full[a]
        rows = pl.ds(pl.multiple_of(blk * rows, 16), rows)
        return ref.at[rows] if lanes is None else ref.at[rows, pl.ds(*lanes)]

    def copy(self, a, role, k, blk, peer):
        at = self.at(a, blk)
        return remote(at, at, self.ss.at[a, role, k], self.rs.at[a, role, k], {"dp": peer})

    def put(self, a, value):
        self.at(a, self.l.me)[...] = value

    def own(self, a):
        l = self.l
        for k in range(1, l.nz):
            self.copy(a, 0, k, l.me, l.z_peer(-k)).start()
        self.copy(a, 1, 0, l.me, l.x_peer).start()
        self.copy(a, 2, 0, l.me, l.y_peer).start()

    def along(self, a):
        l = self.l
        for k in range(1, l.nz):
            blk = l.block(k, l.me)
            self.copy(a, 0, k, blk, l.x_peer).wait_recv()
            self.copy(a, 1, k, blk, l.x_peer).start()
            self.copy(a, 2, k, blk, l.y_peer).start()

    def across(self, a):
        l = self.l
        for k in range(0, l.nz, 1 if a in self.short else 2):
            over_x = k % 2 == 0 if a in self.short else k % 4 == 0
            role, source, target = (1, l.x_peer, l.y_peer) if over_x else (2, l.y_peer, l.x_peer)
            blk = l.block(k, source)
            self.copy(a, role, k, blk, source).wait_recv()
            self.copy(a, 3, k, blk, target).start()

    def share(self, a):
        l = self.l
        if a in self.short:
            return
        for k in range(0, l.nz, 2):
            blk = l.block(k, l.far_peer)
            self.copy(a, 3, k, blk, l.x_peer).wait_recv()
            self.copy(a, 4, k, blk, l.pair_peer).start()

    def arrived(self, a):
        l = self.l
        for k in range(l.nz):
            if a in self.short:
                role, source = (2, l.y_peer) if k % 2 == 0 else (1, l.x_peer)
                self.copy(a, role, k, l.block(k, source), source).wait_recv()
                self.copy(a, 3, k, l.block(k, l.far_peer), l.x_peer).wait_recv()
                continue
            if k % 4 != 0:
                self.copy(a, 1, k, l.block(k, l.x_peer), l.x_peer).wait_recv()
            if k % 4 != 2:
                self.copy(a, 2, k, l.block(k, l.y_peer), l.y_peer).wait_recv()
            if k % 2 == 0:
                self.copy(a, 4, k, l.block(k, l.far_peer, l.z_pair), l.pair_peer).wait_recv()

    def sent(self, a):
        l = self.l
        for k in range(l.nz):
            roles = (0,) * (k > 0) + (1, 2) + ((3,) if a in self.short else (3, 4) * (k % 2 == 0))
            for role in roles:
                self.copy(a, role, k, l.me, l.x_peer).wait_send()


class Scatter:
    def __init__(self, links, grads, bufs, ss, rs):
        self.l, self.grads, self.bufs, self.ss, self.rs = links, grads, bufs, ss, rs

    def part(self, a, blk):
        ref, rows = self.grads[a]
        return cut(ref, blk, rows)

    def read(self, a, blk):
        ref, rows = self.grads[a]
        return ref[pl.ds(pl.multiple_of(blk * rows, 16), rows), :].astype(F32)

    def copy(self, a, role, k, src, slot, peer):
        dst = self.bufs[a].at[slot, k]
        return remote(src, dst, self.ss.at[a, role, k], self.rs.at[a, role, k], {"dp": peer})

    def arrive(self, a, role, k, slot):
        self.copy(a, role, k, self.part(a, 0), slot, self.l.x_peer).wait_recv()

    def far(self, a):
        l = self.l
        for k in range(l.nz):
            peer = l.y_peer if k % 2 == 0 else l.x_peer
            self.copy(a, 0, k, self.part(a, l.block(k, l.far_peer)), 0, peer).start()

    def plain(self, a):
        l = self.l
        for k in range(l.nz):
            if k % 2 == 1:
                self.copy(a, 1, k, self.part(a, l.block(k, l.x_peer)), 1, l.x_peer).start()
            else:
                self.copy(a, 2, k, self.part(a, l.block(k, l.y_peer)), 2, l.y_peer).start()

    def near(self, a):
        l = self.l
        for k in range(l.nz):
            self.arrive(a, 0, k, 0)
            role, peer = (1, l.x_peer) if k % 2 == 0 else (2, l.y_peer)
            mine = self.read(a, l.block(k, peer)) + self.bufs[a][0, k].astype(F32)
            self.bufs[a][0, k] = mine.astype(BF)
            self.copy(a, role, k, self.bufs[a].at[0, k], role, peer).start()

    def along(self, a, kept, held=None):
        l = self.l
        for k in list(range(1, l.nz)) + [0]:
            self.arrive(a, 1, k, 1)
            self.arrive(a, 2, k, 2)
            mine = (
                self.read(a, l.block(k, l.me))
                + self.bufs[a][1, k].astype(F32)
                + self.bufs[a][2, k].astype(F32)
            )
            if k == 0:
                kept[...] = mine
            elif held is not None:
                held[k] = mine.astype(BF)
            else:
                self.bufs[a][1, k] = mine.astype(BF)
                self.copy(a, 3, k, self.bufs[a].at[1, k], 3, l.z_peer(k)).start()

    def total(self, a, kept):
        total = kept[...]
        for k in range(1, self.l.nz):
            self.arrive(a, 3, k, 3)
            total += self.bufs[a][3, k].astype(F32)
        kept[...] = total

    def sent(self, a, held=False):
        for k in range(self.l.nz):
            for role in (0, 1, 2) + (3,) * (k > 0 and not held):
                self.copy(a, role, k, self.part(a, 0), 0, self.l.x_peer).wait_send()


LAG = 2
SLOTS = 4


class Swap:
    def __init__(self, mine, theirs, ss, rs):
        self.mine, self.theirs, self.ss, self.rs = mine, theirs, ss, rs

    def copy(self, slot):
        return remote(
            self.mine.at[slot], self.theirs.at[slot], self.ss.at[slot], self.rs.at[slot], partner()
        )

    def put(self, p, value):
        self.mine[lax.rem(p, SLOTS)] = value.astype(BF)

    def send(self, p):
        self.copy(lax.rem(p, SLOTS)).start()

    def wait(self, p):
        self.copy(lax.rem(p, SLOTS)).wait()

    def rows(self, p, at):
        slot = lax.rem(p, SLOTS)
        return self.mine[slot, at].astype(F32) + self.theirs[slot, at].astype(F32)


def swap_scratch(name, d):
    return [
        (name + "_mine", pltpu.VMEM((SLOTS, ROWS, d), BF)),
        (name + "_theirs", pltpu.VMEM((SLOTS, ROWS, d), BF)),
        (name + "_ss", pltpu.SemaphoreType.DMA((SLOTS,))),
        (name + "_rs", pltpu.SemaphoreType.DMA((SLOTS,))),
    ]


def swap_of(r, name):
    return Swap(*(getattr(r, name + part) for part in ("_mine", "_theirs", "_ss", "_rs")))


class Spread:
    def __init__(self, links, own, z_slots, xy_slots, mp_slot, ss, rs):
        self.l, self.own, self.z_slots, self.xy_slots = links, own, z_slots, xy_slots
        self.mp_slot = mp_slot
        self.ss, self.rs = ss, rs

    def copy(self, stage, k, src, dst, peer):
        return remote(src, dst, self.ss.at[stage, k], self.rs.at[stage, k], {"dp": peer})

    def along(self):
        l = self.l
        self.z_slots[l.z] = self.own[...]
        for k in range(1, l.nz):
            self.copy(0, k, self.own, self.z_slots.at[l.z], l.z_peer(k)).start()

    def across(self):
        l = self.l
        for k in range(1, l.nz):
            self.copy(0, k, self.own, self.z_slots.at[lax.rem(l.z - k + l.nz, l.nz)], l.z_peer(k)).wait()
        total = self.z_slots[0]
        for k in range(1, l.nz):
            total += self.z_slots[k]
        self.own[...] = total
        self.xy_slots[l.column] = total
        for k in range(1, 4):
            self.copy(1, k, self.own, self.xy_slots.at[l.column], l.column_peer(k)).start()

    def over(self):
        l = self.l
        for k in range(1, 4):
            self.copy(1, k, self.own, self.xy_slots.at[lax.rem(l.column - k + 4, 4)], l.column_peer(k)).wait()
        total = self.xy_slots[0]
        for k in range(1, 4):
            total += self.xy_slots[k]
        self.own[...] = total
        self.pair().start()

    def pair(self):
        return remote(self.own, self.mp_slot, self.ss.at[1, 0], self.rs.at[1, 0], partner())

    def total(self, split):
        self.pair().wait()
        own, other = self.own[...], self.mp_slot[...]
        row = lax.broadcasted_iota(jnp.int32, own.shape, 0)
        return jnp.where(row >= split, own + other, own)


def every(step, actions):
    for at, what, argument in actions:
        pl.when(step == at)(partial(what, argument))


gelu_root = math.sqrt(2.0 / math.pi)
gelu_cube = 0.044715
WINDOW = 272


STRIP = 32


def strips(step=STRIP):
    return [slice(i, i + step) for i in range(0, ROWS, step)]


def inverse_rms(v):
    return lax.rsqrt(jnp.mean(v * v, axis=-1, keepdims=True) + norm_eps)


def window_start(p, total):
    return min(p * PLEN // 16 * 16, total - WINDOW)


def align(source, target, windows, sems, passages):
    total = source.shape[0]

    def fetch(p):
        return pltpu.make_async_copy(
            source.at[pl.ds(window_start(p, total), WINDOW)], windows.at[p % 2], sems.at[p % 2]
        )

    def start():
        fetch(0).start()
        fetch(1).start()

    def move(first, last):
        for p in range(first, last):
            fetch(p).wait()
            off = p * PLEN - window_start(p, total)
            rows = windows[p % 2].astype(F32)[off : off + PLEN]
            pad = jnp.zeros((ROWS - PLEN, rows.shape[1]), F32)
            target[p] = jnp.concatenate([rows, pad], axis=0).astype(BF)
            if p + 2 < passages:
                fetch(p + 2).start()

    return start, move


def loop(first, last, body):
    lax.fori_loop(first, last, lambda p, carry: (body(p), carry)[1], 0)


PAIR = 2 * DH


def low_lanes(shape):
    return lax.broadcasted_iota(jnp.int32, shape, 1) < DH


def of_head(h, pair):
    low = low_lanes(pair.shape)
    zero = jnp.zeros_like(pair)
    return jnp.where(low, pair, zero) if h % 2 == 0 else jnp.where(low, zero, pair)


def either(first, second):
    return jnp.where(low_lanes(first.shape), first, second)


def forward_kernel(n, passages, heads, direct, r):
    width = heads * DH
    count = passages
    pair, back_in = (swap_of(r, name) for name in ("pair", "in"))
    if direct:
        links = Links(n)
        rows_o = r.wo_wide.shape[0] // n
        full = [(r.wi, r.wi.shape[0] // n, None), (r.wo_wide, rows_o, None)]
        full += [(w, w.shape[0] // n, None) for w in (r.we_a, r.wr_a, r.we_b, r.wr_b, r.we_c, r.wr_c)]
        gather = Gather(links, full, r.g_ss, r.g_rs, (0, 1))
        grads = [(g, g.shape[0] // n) for g in (r.stage_ra, r.stage_ea, r.stage_rb, r.stage_eb)]
        kept = [r.sum_ra, r.sum_ea, r.sum_rb, r.sum_eb]
        sums = Scatter(links, grads, [r.buf_ra, r.buf_ea, r.buf_rb, r.buf_eb], r.s_ss, r.s_rs)
    tok_start, tok_move = align(r.tokens, r.tok, r.window, r.window_sem, passages)
    cot_start, cot_move = align(r.cotangent, r.cot, r.window, r.window_sem, passages)
    half = passages // 2
    proj, probs, normed_out, ctx = (Drain(r, name) for name in ("proj", "probs", "normed", "ctx"))
    layer, hidden_grad = (Drain(r, name) for name in ("layer", "hidden_grad"))

    def local(src, dst, i):
        return pltpu.make_async_copy(src, dst, r.out_sem.at[i])

    local(r.buckets.at[0], r.bucket_rows, 5).start()
    tok_start()
    if direct:
        gather.put(0, jnp.concatenate([r.own_i[c] for c in range(3)], axis=1).astype(BF))
        pad = jnp.zeros((rows_o - r.own_o.shape[0], r.own_o.shape[1]), F32)
        gather.put(1, jnp.concatenate([r.own_o[...], pad], axis=0).astype(BF))
        greet(links.peers() + [partner()])
        gather.own(0)
        third = full[3][1]
        columns = [r.own_e[:, d * 3 * third : (d + 1) * 3 * third].astype(BF) for d in range(n)]
        for i in range(3):
            at = slice(i * third, (i + 1) * third)
            gather.put(2 + 2 * i, jnp.concatenate([c[:, at] for c in columns], axis=1))
            gather.put(3 + 2 * i, r.own_r[at].astype(BF))
    else:
        greet([partner()])
    tok_move(0, half)
    if direct:
        gather.along(0)
        gather.own(1)
    tok_move(half, passages)
    local(r.tok, r.tok_out, 0).start()
    cot_start()
    if direct:
        gather.across(0)
        gather.share(0)
    cot_move(0, half)
    if direct:
        gather.along(1)
        gather.across(1)
        gather.own(2)
    cot_move(half, passages)
    if direct:
        gather.share(1)
        gather.own(3)
    for h in range(heads):
        line = dot_exact(r.table[h : h + 1, :], r.onehot[...])
        rows = jnp.broadcast_to(line, (ROWS, 2 * ROWS))
        r.bias[h] = pltpu.roll(rows, 0, 1, stride=1, stride_axis=0)[:, :ROWS]
    r.gain_grad[...] = jnp.zeros_like(r.gain_grad)

    def normalise(p):
        for at in strips():
            x = r.tok[p, at].astype(F32)
            r.out_sum[p, at] = x * inverse_rms(x) * r.gains[0:1, :]

    loop(0, count, normalise)
    local(r.buckets.at[0], r.bucket_rows, 5).wait()
    if direct:
        gather.arrived(0)

    def lanes(c, j):
        return slice(c * width + j * PAIR, c * width + (j + 1) * PAIR)

    def settle(p):
        pair.wait(p)
        for at in strips():
            r.hidden[p, at] = r.tok[p, at].astype(F32) + pair.rows(p, at)

    def attend(p):
        normed = r.out_sum[p].astype(BF)
        normed_slot, proj_slot, probs_slot, ctx_slot = (
            stream.slot(p) for stream in (normed_out, proj, probs, ctx)
        )
        normed_slot[...] = normed
        proj_slot[...] = dot(normed, r.wi[...]).astype(BF)
        valid = r.bucket_rows[pl.ds(p, 1), :] < BUCKETS
        masked = jnp.concatenate(
            [jnp.where(valid, 0.0, masked_score), jnp.full((1, ROWS - PLEN), masked_score, F32)], axis=1
        )
        pairs = [[proj_slot[:, lanes(c, j)] for c in range(3)] for j in range(heads // 2)]
        products = [dot(of_head(h, pairs[h // 2][0]), pairs[h // 2][1], 1, 1) for h in range(heads)]
        weighted = []
        for h in range(heads):
            parts = []
            for at in strips(64):
                sc = products[h][at] + r.bias[h, at] + masked
                e_ = jnp.exp(sc - jnp.max(sc, axis=-1, keepdims=True))
                parts.append((e_ * (1.0 / jnp.sum(e_, axis=-1, keepdims=True))).astype(BF))
                probs_slot[h, at] = parts[-1]
            weighted.append(jnp.concatenate(parts, axis=0))
        results = [dot(weighted[h], pairs[h // 2][2]) for h in range(heads)]
        for j in range(heads // 2):
            ctx_slot[:, lanes(0, j)] = either(results[2 * j], results[2 * j + 1]).astype(BF)
        if direct:

            @pl.when(p == 0)
            def _():
                gather.arrived(1)
                rows = r.own_o.shape[0]
                wide = r.acc_r
                for d in range(n):
                    block = r.wo_wide[d * rows_o : (d + 1) * rows_o, :].astype(F32)
                    wide[d * rows : (d + 1) * rows, :] = block[:rows]
                r.wo[...] = wide[: n * rows, :].astype(BF)

            every(p, (
                (0, gather.along, 2), (0, gather.along, 3), (0, gather.own, 4), (1, gather.across, 2),
                (1, gather.own, 5), (2, gather.across, 3), (2, gather.share, 2), (3, gather.share, 3),
                (3, gather.along, 4), (4, gather.along, 5), (4, gather.own, 6), (5, gather.across, 4),
                (5, gather.own, 7), (6, gather.across, 5), (6, gather.share, 4), (7, gather.share, 5),
            ))
        pair.put(p, dot(ctx_slot[...], r.wo[...]))
        pl.when(p >= LAG)(lambda: settle(p - LAG))
        pair.send(p)
        for stream in (normed_out, proj, probs, ctx):
            stream.start(p)

    loop(0, count, attend)

    if direct:
        gather.arrived(2)
        gather.arrived(3)
        local(r.wi, r.wi_out, 1).start()
        local(r.wo, r.wo_out, 2).start()

    def clear():
        r.acc_r[...] = jnp.zeros_like(r.acc_r)
        r.acc_e[...] = jnp.zeros_like(r.acc_e)

    def normed_two(p):
        parts = []
        for at in strips():
            h = r.hidden[p, at]
            parts.append((h * inverse_rms(h) * r.gains[1:2, :]).astype(BF))
        return jnp.concatenate(parts, axis=0)

    def inner_part(normed, c, we, wr):
        u_all, in_all = dot(normed, we[...]), dot(c, wr[...], 1, 1)
        acts, backs = [], []
        for at in strips():
            u = u_all[at]
            square = u * u
            t = jnp.tanh(u * (gelu_root + (gelu_root * gelu_cube) * square))
            half = 0.5 * (1.0 + t)
            acts.append((u * half).astype(BF))
            slope = half + (0.5 * u) * (1.0 - t * t) * (
                gelu_root + (3.0 * gelu_root * gelu_cube) * square
            )
            backs.append((in_all[at] * slope).astype(BF))
        return jnp.concatenate(acts, axis=0), jnp.concatenate(backs, axis=0)

    def outer_part(normed, c, act, back, we, wr):
        r.acc_r[...] += dot(act, c, 0, 0)
        r.acc_e[...] += dot(normed, back, 0, 0)
        return dot(act, wr[...]), dot(back, we[...], 1, 1)

    def staged(stage_r, stage_e):
        stage_r[...] = r.acc_r[...].astype(BF)
        stage_e[...] = r.acc_e[...].astype(BF)

    def first(p):
        normed, c = normed_two(p), r.cot[p]
        act, back = inner_part(normed, c, r.we_a, r.wr_a)
        r.out_sum[p], r.in_sum[p] = outer_part(normed, c, act, back, r.we_a, r.wr_a)

        @pl.when(p == 0)
        def _():
            for last in range(count - LAG, count):
                settle(last)

        if direct:
            every(p, (
                (0, gather.along, 6), (1, gather.along, 7), (2, gather.across, 6), (3, gather.across, 7),
                (4, gather.share, 6), (5, gather.share, 7),
            ))

    clear()
    loop(0, count, first)
    staged(r.stage_ra, r.stage_ea)
    if direct:
        sums.far(0)
        sums.far(1)
        gather.arrived(4)
        gather.arrived(5)
    clear()

    def middle(p):
        normed, c = normed_two(p), r.cot[p]
        act, back = inner_part(normed, c, r.we_b, r.wr_b)
        r_part, n_part = outer_part(normed, c, act, back, r.we_b, r.wr_b)
        r.out_sum[p] += r_part
        r.in_sum[p] += n_part
        if direct:
            every(p, ((1, sums.plain, 0), (1, sums.plain, 1), (4, sums.near, 0), (6, sums.near, 1)))

    loop(0, count, middle)
    staged(r.stage_rb, r.stage_eb)
    if direct:
        sums.far(2)
        sums.far(3)
        sums.plain(2)
        sums.plain(3)
        gather.arrived(6)
        gather.arrived(7)
    clear()

    def finish(last):
        layer_slot, grad_slot = layer.slot(last), hidden_grad.slot(last)
        pair.wait(count + last)
        back_in.wait(last)
        gain_rows = jnp.zeros((1, r.gains.shape[1]), F32)
        for at in strips():
            h = r.hidden[last, at]
            layer_slot[at] = (h + pair.rows(count + last, at)).astype(BF)
            grad = back_in.rows(last, at)
            inv = inverse_rms(h)
            hr = h * inv
            gain_rows += jnp.sum(grad * hr, axis=0, keepdims=True)
            zed = r.gains[1:2, :] * grad
            inner = jnp.mean(zed * hr, axis=-1, keepdims=True)
            grad_slot[at] = r.cot[last, at].astype(F32) + inv * (zed - hr * inner)
        r.gain_grad[0:1, :] += gain_rows

    def last_part(p, with_finish=True):
        normed, c = normed_two(p), r.cot[p]
        act, back = inner_part(normed, c, r.we_c, r.wr_c)
        if with_finish:
            finish(p - LAG)
        r_part, n_part = outer_part(normed, c, act, back, r.we_c, r.wr_c)
        pair.put(count + p, r.out_sum[p] + r_part)
        back_in.put(p, r.in_sum[p] + n_part)
        pair.send(count + p)
        back_in.send(p)
        if with_finish:
            for stream in (layer, hidden_grad):
                stream.start(p - LAG)
            if direct:
                for a, at in ((0, 2), (1, 3)):
                    pl.when(p == at)(partial(sums.along, a, kept[a]))
                every(p, ((4, sums.near, 2), (5, sums.near, 3)))

    loop(0, LAG, lambda p: last_part(p, False))
    loop(LAG, count, last_part)
    stage_rc, stage_ec = (r.wr_c, r.we_c) if direct else (r.stage_rc, r.stage_ec)
    if direct:
        gather.sent(6)
        gather.sent(7)
    staged(stage_rc, stage_ec)
    local(stage_rc, r.grad_r, 3).start()
    local(stage_ec, r.grad_e, 4).start()
    for p in range(count - LAG, count):
        finish(p)
        for stream in (layer, hidden_grad):
            stream.start(p)
    if direct:
        for a, held in ((2, r.held_rb), (3, r.held_eb)):
            held[0] = jnp.zeros(held.shape[1:], BF)
            sums.along(a, kept[a], held)
        for a in range(2):
            sums.total(a, kept[a])
        for a in range(6):
            gather.sent(a)
        for a in range(4):
            sums.sent(a, a >= 2)
        local(r.wi, r.wi_out, 1).wait()
        local(r.wo, r.wo_out, 2).wait()
    local(r.tok, r.tok_out, 0).wait()
    local(stage_rc, r.grad_r, 3).wait()
    local(stage_ec, r.grad_e, 4).wait()
    for stream in (normed_out, proj, probs, ctx, layer, hidden_grad):
        stream.last()


def dot_exact(a, b):
    return lax.dot_general(
        a, b, (((1,), (1,)), ((), ())), precision=lax.Precision.HIGHEST, preferred_element_type=F32
    )


def forward(n, passages, heads, direct, tokens, cotangent, buckets, gains, table, onehot, weights):
    d = tokens.shape[1]
    width = heads * DH
    ins = [("tokens", tokens, ANY), ("cotangent", cotangent, ANY)]
    ins += [("buckets", buckets, ANY)]
    ins += [(k, v, VMEM) for k, v in (("gains", gains), ("table", table), ("onehot", onehot))]
    ins += [(k, v, VMEM) for k, v in weights.items()]
    if direct:
        part = weights["own_r"].shape[0] // 3 * n
    else:
        part = weights["wr_a"].shape[0]
    streams = dict(
        proj=((ROWS, 3 * width), BF),
        probs=((heads, ROWS, ROWS), BF),
        normed=((ROWS, d), BF),
        ctx=((ROWS, width), BF),
        layer=((ROWS, d), BF),
        hidden_grad=((ROWS, d), F32),
    )
    outs = [(k, (passages,) + shape, dtype, ANY) for k, (shape, dtype) in streams.items()]
    outs += [
        ("tok_out", (passages, ROWS, d), BF, ANY),
        ("grad_r", (part, d), BF, ANY),
        ("grad_e", (d, part), BF, ANY),
        ("gain_grad", (8, d), F32, VMEM),
    ]
    scratch = [*dict(
        tok=pltpu.VMEM((passages, ROWS, d), BF),
        cot=pltpu.VMEM((passages, ROWS, d), BF),
        window=pltpu.VMEM((2, WINDOW, d), BF),
        window_sem=pltpu.SemaphoreType.DMA((2,)),
        bucket_rows=pltpu.VMEM(buckets.shape[1:], buckets.dtype),
        out_sem=pltpu.SemaphoreType.DMA((6,)),
        bias=pltpu.VMEM((heads, ROWS, ROWS), F32),
        hidden=pltpu.VMEM((passages, ROWS, d), F32),
        out_sum=pltpu.VMEM((passages, ROWS, d), F32),
        in_sum=pltpu.VMEM((passages, ROWS, d), F32),
        acc_r=pltpu.VMEM((part, d), F32),
        acc_e=pltpu.VMEM((d, part), F32),
    ).items()]
    for k, (shape, dtype) in streams.items():
        scratch += stream_scratch(k, shape, dtype)
    for name in ("pair", "in"):
        scratch += swap_scratch(name, d)
    stage = [("r" + half, (part, d)) for half in "ab"] + [("e" + half, (d, part)) for half in "ab"]
    if direct:
        nz = n // 4
        padded = weights["own_o"].shape[0]
        padded += -padded % 16
        outs += [("wi_out", (d, 3 * width), BF, ANY), ("wo_out", (width, d), BF, ANY)]
        for key, shape in stage:
            block = (shape[0] // n, shape[1])
            outs.append(("sum_" + key, block, F32, VMEM))
            if key[1] == "b":
                outs.append(("held_" + key, (nz,) + block, BF, VMEM))
            scratch.append(("stage_" + key, pltpu.VMEM(shape, BF)))
            scratch.append(("buf_" + key, pltpu.VMEM((4, nz) + block, BF)))
        shapes = {"wi": (d, 3 * width), "wo": (width, d), "wo_wide": (n * padded, d)}
        for third in "abc":
            shapes["we_" + third], shapes["wr_" + third] = (d, part), (part, d)
        scratch += [(key, pltpu.VMEM(shape, BF)) for key, shape in shapes.items()]
        scratch += [*dict(
            g_ss=pltpu.SemaphoreType.DMA((8, 5, nz)),
            g_rs=pltpu.SemaphoreType.DMA((8, 5, nz)),
            s_ss=pltpu.SemaphoreType.DMA((4, 4, nz)),
            s_rs=pltpu.SemaphoreType.DMA((4, 4, nz)),
        ).items()]
    else:
        outs += [("stage_" + k, shape, BF, VMEM) for k, shape in stage]
        scratch += [("stage_rc", pltpu.VMEM((part, d), BF)), ("stage_ec", pltpu.VMEM((d, part), BF))]
    kernel = partial(forward_kernel, n, passages, heads, direct)
    return run(kernel, ins, outs, scratch, 1, 63, "forward")


def back_kernel(n, passages, heads, direct, r):
    width = heads * DH
    count = passages
    swap = swap_of(r, "in")
    if direct:
        links = Links(n)
        refs = [r.grad_r, r.grad_e, r.stage_o, r.stage_v, r.stage_qk]
        grads = [(g, g.shape[0] // n) for g in refs]
        names = ["r", "e", "o", "v", "qk"]
        bufs = [getattr(r, "buf_" + k) for k in names]
        kept = [getattr(r, "sum_" + k) for k in names]
        sums = Scatter(links, grads, bufs, r.s_ss, r.s_rs)
        late = [
            remote(held.at[k], land.at[k], r.c_ss.at[i, k], r.c_rs.at[i, k], {"dp": links.z_peer(k)})
            for i, (held, land) in enumerate(((r.held_rb, r.land_rb), (r.held_eb, r.land_eb)))
            for k in range(1, links.nz)
        ]
        wide = Spread(links, r.wide, r.wide_z, r.wide_xy, r.wide_mp, r.w_ss, r.w_rs)
    ctx, normed, probs, proj, tok, hidden_grad = (
        Load(r, name) for name in ("ctx", "normed", "probs", "proj", "tok", "hidden_grad")
    )
    input_grad = Drain(r, "input_grad")

    for p in range(count):
        for stream in (hidden_grad, ctx, probs, normed):
            stream.copy(p).start()
    for stream in (proj, tok):
        stream.start()
    if direct:
        greet(links.peers() + [{"dp": links.far_peer}, partner()])
        for copy in late:
            copy.start()
        sums.far(0)
        sums.far(1)
    else:
        greet([partner()])
    r.acc_o[...] = jnp.zeros_like(r.acc_o)
    r.acc_s[...] = jnp.zeros_like(r.acc_s)
    r.acc_v[...] = jnp.zeros_like(r.acc_v)
    r.acc_qk[...] = jnp.zeros_like(r.acc_qk)

    def lanes(c, j):
        return slice(c * width + j * PAIR, c * width + (j + 1) * PAIR)

    def values(p):
        for stream in (hidden_grad, ctx, probs, normed):
            stream.wait(p)
        top = hidden_grad.buf[p].astype(BF)
        r.acc_o[...] += dot(ctx.buf[p], top, 0, 0)
        dctx = dot(top, r.wo[...], 1, 1).astype(BF)
        r.dctx[p] = dctx
        results = [dot(probs.buf[p, h], dctx[:, lanes(0, h // 2)], 0, 0) for h in range(heads)]
        dv = [either(results[2 * j], results[2 * j + 1]) for j in range(heads // 2)]
        dv = jnp.concatenate(dv, axis=1).astype(BF)
        r.dproj[p, :, 2 * width :] = dv
        r.acc_v[...] += dot(normed.buf[p], dv, 0, 0)
        if direct:
            every(p, (
                (1, sums.plain, 0), (1, sums.plain, 1), (4, sums.near, 0), (6, sums.near, 1),
            ))

    loop(0, count, values)
    blocks = n if direct else 1
    rows = r.acc_o.shape[0] // blocks
    padded = r.stage_o.shape[0] // blocks
    for b in range(blocks):
        part = r.acc_o[b * rows : (b + 1) * rows, :]
        if padded > rows:
            part = jnp.concatenate([part, jnp.zeros((padded - rows, part.shape[1]), F32)], axis=0)
        r.stage_o[b * padded : (b + 1) * padded, :] = part.astype(BF)
    r.stage_v[...] = r.acc_v[...].astype(BF)
    if direct:
        sums.far(2)
        sums.far(3)

    def scores(p):
        proj.wait(p)
        pairs = [[proj.buf[p, :, lanes(c, j)] for c in range(3)] for j in range(heads // 2)]
        products = [
            dot(of_head(h, r.dctx[p, :, lanes(0, h // 2)]), pairs[h // 2][2], 1, 1) for h in range(heads)
        ]
        ds = []
        for h in range(heads):
            parts = []
            for rows in strips(64):
                a = probs.buf[p, h, rows].astype(F32)
                dp = products[h][rows]
                centre = jnp.sum(a * dp, axis=-1, keepdims=True)
                parts.append((a * (dp - centre)).astype(BF))
                r.acc_s[h, rows] += parts[-1].astype(F32)
            ds.append(jnp.concatenate(parts, axis=0))
        dq = [dot(ds[h], pairs[h // 2][1]) for h in range(heads)]
        dk = [dot(ds[h], pairs[h // 2][0], 0, 0) for h in range(heads)]
        for j in range(heads // 2):
            r.dproj[p, :, lanes(0, j)] = either(dq[2 * j], dq[2 * j + 1]).astype(BF)
            r.dproj[p, :, lanes(1, j)] = either(dk[2 * j], dk[2 * j + 1]).astype(BF)
        r.acc_qk[...] += dot(normed.buf[p], r.dproj[p, :, : 2 * width], 0, 0)
        if direct:
            every(p, ((0, sums.plain, 2), (0, sums.plain, 3)))
            for a, at in ((0, 2), (1, 4)):
                pl.when(p == at)(partial(sums.along, a, kept[a]))
            every(p, ((3, sums.near, 2), (5, sums.near, 3)))

    loop(0, count, scores)
    r.stage_qk[...] = r.acc_qk[...].astype(BF)
    if direct:
        sums.far(4)
    terms = jnp.sum(r.acc_v[...] * r.wi[:, 2 * width :].astype(F32), axis=1, keepdims=True)
    terms += jnp.sum(r.acc_qk[...] * r.wi[:, : 2 * width].astype(F32), axis=1, keepdims=True)
    r.wide[...] = jnp.zeros_like(r.wide)
    r.wide[heads : heads + 1, :] = 0.5 * r.gain_two[0:1, :]
    r.wide[heads + 1 : heads + 2, :] = terms.T / r.gains[0:1, :]
    for h in range(heads):
        lines = jnp.concatenate([r.acc_s[h], jnp.zeros((ROWS, ROWS), F32)], axis=1)
        while lines.shape[0] > 1:
            half = lines.shape[0] // 2
            lines = lines[:half] + pltpu.roll(lines[half:], 2 * ROWS - half, 1)
        r.wide[h : h + 1, : 2 * ROWS] = lines
    if direct:
        wide.along()
        sums.plain(4)

    def finish(last):
        tok.wait(last)
        slot = input_grad.slot(last)
        swap.wait(last)
        for at in strips():
            x = tok.buf[last, at].astype(F32)
            inv = inverse_rms(x)
            xr = x * inv
            zed = r.gains[0:1, :] * swap.rows(last, at)
            inner = jnp.mean(zed * xr, axis=-1, keepdims=True)
            slot[at] = hidden_grad.buf[last, at] + inv * (zed - xr * inner)

    def inputs(t, with_finish=True):
        terms = dot(r.dproj[t, :, : 2 * width], r.wi[:, : 2 * width], 1, 1)
        if with_finish:
            finish(t - LAG)
        terms += dot(r.dproj[t, :, 2 * width :], r.wi[:, 2 * width :], 1, 1)
        swap.put(t, terms)
        swap.send(t)
        if with_finish:
            input_grad.start(t - LAG)
            if direct:
                every(t, ((4, sums.near, 4),))
                pl.when(t == 7)(partial(sums.along, 4, kept[4]))
                for a, at in ((2, 2), (3, 3)):
                    pl.when(t == at)(partial(sums.along, a, kept[a]))
                pl.when(t == 2)(wide.across)
                pl.when(t == 5)(wide.over)

    loop(0, LAG, lambda t: inputs(t, False))
    loop(LAG, count, inputs)
    if direct:
        for copy in late:
            copy.wait()
        for part, land, target in (
            (r.part_rb, r.land_rb, r.sum_rb), (r.part_eb, r.land_eb, r.sum_eb),
        ):
            total = part[...]
            for k in range(1, links.nz):
                total += land[k].astype(F32)
            target[...] = total
        for a in range(4):
            sums.total(a, kept[a])
    for p in range(count - LAG, count):
        finish(p)
        input_grad.start(p)
    if direct:
        r.wide_sum[...] = wide.total(heads)
        sums.total(4, kept[4])
        for a in range(5):
            sums.sent(a)
    else:
        r.wide_sum[...] = r.wide[...]
    input_grad.last()


def back(n, passages, heads, direct, f, gains, wi, wo):
    d = gains.shape[1]
    width = heads * DH
    streams = dict(
        ctx=((ROWS, width), BF),
        normed=((ROWS, d), BF),
        probs=((heads, ROWS, ROWS), BF),
        proj=((ROWS, 3 * width), BF),
        tok=((ROWS, d), BF),
        hidden_grad=((ROWS, d), F32),
    )
    ins = [(k, f.tok_out if k == "tok" else getattr(f, k), ANY) for k in streams]
    fixed = [("gains", gains), ("wi", wi), ("wo", wo), ("gain_two", f.gain_grad)]
    outs = [
        ("input_grad", (passages, ROWS, d), F32, ANY),
        ("wide_sum", (8, d), F32, VMEM),
    ]
    scratch = [*dict(
        acc_qk=pltpu.VMEM((d, 2 * width), F32),
        acc_v=pltpu.VMEM((d, width), F32),
        acc_o=pltpu.VMEM((width, d), F32),
        acc_s=pltpu.VMEM((heads, ROWS, ROWS), F32),
        dctx=pltpu.VMEM((passages, ROWS, width), BF),
        dproj=pltpu.VMEM((passages, ROWS, 3 * width), BF),
        wide=pltpu.VMEM((8, d), F32),
    ).items()] + swap_scratch("in", d)
    for k, (shape, dtype) in streams.items():
        scratch.append((k + "_buf", pltpu.VMEM((passages,) + shape, dtype)))
        scratch.append((k + "_sem", pltpu.SemaphoreType.DMA((passages,))))
    scratch += stream_scratch("input_grad", (ROWS, d), F32)
    rows_o = width
    if direct:
        rows_o = width // n
        rows_o = (rows_o + -rows_o % 16) * n
    stage = [("stage_o", (rows_o, d)), ("stage_v", (d, width)), ("stage_qk", (d, 2 * width))]
    if direct:
        nz = n // 4
        fixed += [(k, getattr(f, k)) for k in ("grad_r", "grad_e", "held_rb", "held_eb")]
        fixed += [("part_rb", f.sum_rb), ("part_eb", f.sum_eb)]
        for key, shape in (("rb", f.sum_rb.shape), ("eb", f.sum_eb.shape)):
            outs.append(("sum_" + key, shape, F32, VMEM))
            scratch.append(("land_" + key, pltpu.VMEM((nz,) + shape, BF)))
        scratch += [(k, pltpu.VMEM(shape, BF)) for k, shape in stage]
        blocks = {"r": f.grad_r.shape, "e": f.grad_e.shape}
        blocks.update({k[6:]: shape for k, shape in stage})
        for key, shape in blocks.items():
            shape = (shape[0] // n, shape[1])
            scratch.append(("buf_" + key, pltpu.VMEM((4, nz) + shape, BF)))
            outs.append(("sum_" + key, shape, F32, VMEM))
        scratch += [*dict(
            wide_z=pltpu.VMEM((nz, 8, d), F32),
            wide_xy=pltpu.VMEM((4, 8, d), F32),
            wide_mp=pltpu.VMEM((8, d), F32),
            c_ss=pltpu.SemaphoreType.DMA((2, nz)),
            c_rs=pltpu.SemaphoreType.DMA((2, nz)),
            s_ss=pltpu.SemaphoreType.DMA((len(blocks), 4, nz)),
            s_rs=pltpu.SemaphoreType.DMA((len(blocks), 4, nz)),
            w_ss=pltpu.SemaphoreType.DMA((2, max(nz, 4))),
            w_rs=pltpu.SemaphoreType.DMA((2, max(nz, 4))),
        ).items()]
    else:
        outs += [(k, shape, BF, VMEM) for k, shape in stage]
    ins += [(k, v, VMEM) for k, v in fixed]
    kernel = partial(back_kernel, n, passages, heads, direct)
    return run(kernel, ins, outs, scratch, 2, 63, "back")


rates = {
    "i": rate_inward, "o": rate_outward, "e": rate_expand, "r": rate_reduce, "g": rate_gains, "t": rate_table,
}


def update_kernel(n, passages, heads, keys, r):
    total = r.layer_out.shape[0]
    ins = [(getattr(r, k), getattr(r, k + "_in")) for k in keys]
    fetch = {k: pltpu.make_async_copy(a, b, r.in_sem.at[i]) for i, (k, (a, b)) in enumerate(zip(keys, ins))}
    stores = []

    def store(src, dst):
        copy = pltpu.make_async_copy(src, dst, r.out_sem.at[len(stores)])
        copy.start()
        stores.append(copy)

    def passage(name, p, sem):
        return pltpu.make_async_copy(getattr(r, name).at[p], getattr(r, name + "_in").at[p], sem.at[p])

    for p in range(passages):
        passage("grad", p, r.grad_sem).start()
        passage("layer", p, r.layer_sem).start()
    for k in keys:
        fetch[k].start()

    def get(k):
        fetch[k].wait()
        return getattr(r, k + "_in")

    def step(key, gradient, at=...):
        out = adamw(*(getattr(r, key + part + "_in")[at] for part in "wmv"), gradient, rates[key])
        for part, value in zip(("_nw", "_nm", "_nv"), out):
            getattr(r, key + part + "_out")[at] = value
        if key not in "gt":
            getattr(r, key + "_nc_out")[at] = out[0].astype(BF)

    def ready(key):
        for part in "wmv":
            fetch[key + part].wait()

    def done(key):
        for part in ("_nw", "_nm", "_nv") + ("_nc",) * (key not in "gt"):
            store(getattr(r, key + part + "_out"), getattr(r, key + part))

    sent = 0
    for p in range(passages):
        at = slice(p * PLEN, (p + 1) * PLEN)
        passage("grad", p, r.grad_sem).wait()
        r.grad_rows[at] = r.grad_in[p, :PLEN]
        passage("layer", p, r.layer_sem).wait()
        r.layer_wide[at] = r.layer_in[p, :PLEN].astype(F32)
        end = total if p == passages - 1 else (p + 1) * PLEN // 16 * 16
        rows = slice(sent, end)
        store(r.grad_rows.at[rows], r.input_grad.at[rows])
        r.layer_rows[rows] = r.layer_wide[rows].astype(BF)
        store(r.layer_rows.at[rows], r.layer_out.at[rows])
        sent = end
    pieces_r, pieces_e = ([get(key + third) for third in "abc"] for key in "re")
    ready("r")
    third = pieces_r[0].shape[0]
    for i, piece in enumerate(pieces_r):
        step("r", piece[...], slice(i * third, (i + 1) * third))
    done("r")
    ready("e")
    columns = [piece[:, d * third : (d + 1) * third] for d in range(n) for piece in pieces_e]
    step("e", jnp.concatenate(columns, axis=1))
    done("e")
    ready("o")
    step("o", get("sum_o")[: r.ow_in.shape[0]])
    done("o")
    ready("i")
    qk, v = get("sum_qk"), get("sum_v")
    width = v.shape[1]
    step("i", qk[:, :width], 0)
    step("i", qk[:, width:], 1)
    step("i", v[...], 2)
    done("i")
    ready("g")
    small = get("small")
    step("g", small[heads + 1 : heads + 2], slice(0, 1))
    step("g", small[heads : heads + 1], slice(1, 2))
    done("g")
    ready("t")
    onehot = get("onehot")
    step("t", lax.dot_general(
        small[:heads, : 2 * ROWS], onehot[...], (((1,), (0,)), ((), ())),
        precision=lax.Precision.HIGHEST, preferred_element_type=F32,
    ))
    done("t")
    for copy in stores:
        copy.wait()


def update(n, passages, heads, shape, f, b, onehot, states):
    total, d = shape
    small = dict(ra=f.sum_ra, rb=b.sum_rb, rc=b.sum_r, ea=f.sum_ea, eb=b.sum_eb, ec=b.sum_e)
    ins = [(k, v) for k, v in small.items()]
    ins += [(key + part, a) for key in "reo" for part, a in zip("wmv", states[key])]
    ins += [("sum_o", b.sum_o), ("sum_qk", b.sum_qk), ("sum_v", b.sum_v)]
    ins += [("small", b.wide_sum), ("onehot", onehot)]
    ins += [(key + part, a) for key in "igt" for part, a in zip("wmv", states[key])]
    keys = [k for k, _ in ins]
    scratch = [(k + "_in", pltpu.VMEM(a.shape, a.dtype)) for k, a in ins]
    outs = []
    for key in "ioergt":
        for part in ("_nw", "_nm", "_nv") + ("_nc",) * (key not in "gt"):
            outs.append((key + part, states[key][0].shape, BF if part == "_nc" else F32, ANY))
    scratch += [(k + "_out", pltpu.VMEM(dims, dtype)) for k, dims, dtype, _ in outs]
    padded = (passages, ROWS, d)
    count = len(outs) + 2 * passages
    scratch += [*dict(
        grad_in=pltpu.VMEM(padded, F32),
        layer_in=pltpu.VMEM(padded, BF),
        grad_rows=pltpu.VMEM((total, d), F32),
        layer_wide=pltpu.VMEM((total, d), F32),
        layer_rows=pltpu.VMEM((total, d), BF),
        in_sem=pltpu.SemaphoreType.DMA((len(keys),)),
        out_sem=pltpu.SemaphoreType.DMA((count,)),
        grad_sem=pltpu.SemaphoreType.DMA((passages,)),
        layer_sem=pltpu.SemaphoreType.DMA((passages,)),
    ).items()]
    ins += [("layer", f.layer), ("grad", b.input_grad)]
    outs += [("layer_out", shape, BF, ANY), ("input_grad", shape, F32, ANY)]
    kernel = partial(update_kernel, n, passages, heads, keys)
    o = run(kernel, [(k, a, ANY) for k, a in ins], outs, scratch, None, 60, "update")
    new = [o.layer_out, o.input_grad]
    for key in "ioergt":
        for part in ("_nw", "_nm", "_nv") + ("_nc",) * (key not in "gt"):
            value = getattr(o, key + part)
            if key == "i":
                value = value.transpose(1, 0, 2)
            new.append(value.T if key == "t" else value)
    return tuple(new)


def shards(
    n,
    tokens,
    cotangent,
    buckets,
    inward_master,
    inward_first,
    inward_second,
    outward_master,
    outward_first,
    outward_second,
    expand_master,
    expand_first,
    expand_second,
    reduce_master,
    reduce_first,
    reduce_second,
    gains_master,
    gains_first,
    gains_second,
    table_master,
    table_first,
    table_second,
):
    d = tokens.shape[1]
    passages = tokens.shape[0] // PLEN
    heads = inward_master.shape[2] // DH
    width = heads * DH
    rows_i, rows_r = inward_master.shape[0], reduce_master.shape[0]
    units = expand_master.shape[1]
    direct = n % 8 == 0 and rows_i % 16 == 0 and rows_r % 48 == 0 and outward_master.shape[0] % 8 == 0

    onehot = jnp.asarray(distance_onehot())
    bucket_rows = buckets.transpose(1, 0, 2)
    table_rows = table_master.T
    if direct:
        weights = dict(
            own_i=inward_master.transpose(1, 0, 2),
            own_o=outward_master,
            own_e=expand_master,
            own_r=reduce_master,
        )
    else:
        masters = (inward_master.reshape(-1, 3 * width), outward_master, expand_master, reduce_master)
        wi, wo, we, wr = (
            lax.all_gather(w.astype(BF), "dp", axis=0, tiled=True) for w in masters
        )
        cuts = [slice(i * units // 3, (i + 1) * units // 3) for i in range(3)]
        weights = {"wi": wi, "wo": wo}
        for third, at in zip("abc", cuts):
            weights["we_" + third], weights["wr_" + third] = we[:, at], wr[at]
    f = forward(
        n, passages, heads, direct, tokens, cotangent, bucket_rows, gains_master, table_rows, onehot, weights
    )
    if direct:
        wi, wo = f.wi_out, f.wo_out
    b = back(n, passages, heads, direct, f, gains_master, wi, wo)

    def scatter(g):
        return lax.psum_scatter(g.astype(F32), "dp", scatter_dimension=0, tiled=True)

    if direct:
        states = dict(
            i=tuple(a.transpose(1, 0, 2) for a in (inward_master, inward_first, inward_second)),
            o=(outward_master, outward_first, outward_second),
            e=(expand_master, expand_first, expand_second),
            r=(reduce_master, reduce_first, reduce_second),
            g=(gains_master, gains_first, gains_second),
            t=(table_master.T, table_first.T, table_second.T),
        )
        return update(n, passages, heads, tokens.shape, f, b, onehot, states)
    else:
        inward_sum = scatter(jnp.concatenate([b.stage_qk, b.stage_v], axis=1))
        outward_sum = scatter(b.stage_o)
        expand_sum = scatter(jnp.concatenate([f.stage_ea, f.stage_eb, f.grad_e], axis=1))
        reduce_sum = scatter(jnp.concatenate([f.stage_ra, f.stage_rb, f.grad_r], axis=0))
        wide_sum = lax.psum(b.wide_sum, "dp")
        gains = lax.psum(wide_sum[heads : heads + 2], "mp")
        wide_sum = jnp.concatenate([wide_sum[:heads], gains], axis=0)
    inward_sum = inward_sum.reshape(inward_master.shape)
    gains_sum = jnp.concatenate([wide_sum[heads + 1 : heads + 2], wide_sum[heads : heads + 1]], axis=0)
    table_sum = lax.dot_general(
        onehot.T, wide_sum[:heads, : 2 * ROWS], (((1,), (1,)), ((), ())), precision=lax.Precision.HIGHEST
    )

    layer_out = f.layer[:, :PLEN].reshape(tokens.shape)
    input_grad = b.input_grad[:, :PLEN].reshape(tokens.shape)
    outputs = [layer_out, input_grad]
    for w, first_moment, second_moment, gradient, rate, copied in (
        (inward_master, inward_first, inward_second, inward_sum, rate_inward, True),
        (outward_master, outward_first, outward_second, outward_sum, rate_outward, True),
        (expand_master, expand_first, expand_second, expand_sum, rate_expand, True),
        (reduce_master, reduce_first, reduce_second, reduce_sum, rate_reduce, True),
        (gains_master, gains_first, gains_second, gains_sum, rate_gains, False),
        (table_master, table_first, table_second, table_sum, rate_table, False),
    ):
        new = adamw(w, first_moment, second_moment, gradient, rate)
        outputs += list(new)
        if copied:
            outputs.append(new[0].astype(BF))
    return tuple(outputs)


def solution(mesh):
    rows = P("dp", None)
    inward = P("dp", None, "mp")
    tall = P(("mp", "dp"), None)
    wide = P("dp", "mp")
    table = P(None, "mp")
    return jax.shard_map(
        partial(shards, mesh.shape["dp"]),
        mesh=mesh,
        in_specs=(rows, rows, P("dp", None, None))
        + (inward,) * 3
        + (tall,) * 3
        + (wide,) * 3
        + (tall,) * 3
        + (P(),) * 3
        + (table,) * 3,
        out_specs=(rows, rows)
        + (inward,) * 4
        + (tall,) * 4
        + (wide,) * 4
        + (tall,) * 4
        + (P(),) * 3
        + (table,) * 3,
        check_vma=False,
    )
```
